32 devices in a mesh: date: 8 (over y, x, core), strip: 4 (over z).
Axes of the slice: x: 2, y: 2, z: 4, core: 2. Of those that a mesh axis runs over, the one named last changes fastest.
Arguments:
- slc: bfloat16 [2, 16, 128, 1024], P(None, 'date', 'strip')
- block_order: int32 [8], replicated, may hold values from 0 to 7, each once
- az_offset: int32 [32], P('strip'), may hold values from 0 to 3
- rg_offset: int32 [256], replicated, may hold values from 0 to 3
Outputs:
- coherence: float32 [2, 16, 16, 32, 256], P(None, 'date', None, 'strip')
The draws below stay inside these ranges and needn't reach their ends.
Inputs may be any that keep to these rules, and one draw needn't show every extreme that they name: block_order is a permutation of the 8 chronological block numbers.
All inputs are finite; a program needn't handle non-finite values.
Results may differ from the reference program's by a relative error of at most 0.0003.
Values may be sent and summed in bfloat16 or wider, within the bound.
No kernel may reach another device: no remote copies, remote signals or barrier semaphores. Data moves between devices by JAX's collectives and lax.ppermute only.
A program may use at most 64 MiB of HBM per device.

```python
import jax
import jax.numpy as jnp
from jax import lax

DATE_DEV = 2
RANGE = 1024
RG_WIN = 5
STEP = 4
HALO = 5
DATES = 16
BLOCKS = 8
LINES = 128
OUT_AZ = 32
OUT_RG = 256


def draw_slc(key, part):
    subkeys = jax.random.split(key, 6)
    scene_field = jax.random.normal(subkeys[0], (2, 1, LINES, RANGE), jnp.float32)
    phase_angle = jax.random.uniform(subkeys[1], (1, DATES, 1, 1), jnp.float32, -3.14159, 3.14159)
    roughness = jax.random.uniform(subkeys[5], (1, DATES, LINES, RANGE), jnp.float32, 0.5, 1.5)
    weight = jax.random.uniform(subkeys[2], (1, DATES, 1, 1), jnp.float32, 0.4, 1.2)
    noise_part = 0.7 * jax.random.normal(subkeys[4], (2, DATES, LINES, RANGE), jnp.float32)
    phase_cos = jnp.cos(phase_angle)
    phase_sin = jnp.sin(phase_angle)
    real_part = scene_field[0:1] * phase_cos - scene_field[1:2] * phase_sin
    imag_part = scene_field[0:1] * phase_sin + scene_field[1:2] * phase_cos
    signal = jnp.concatenate([real_part, imag_part], 0) * (weight * roughness)
    return (signal + noise_part).astype(jnp.bfloat16)


def plant(values, own_key, least, largest):
    extent = values.shape
    index_at = [jax.random.randint(jax.random.fold_in(own_key, axis), (), 0, extent[axis]) for axis in range(len(extent))]
    values = values.at[tuple(index_at)].set(least)
    longest = extent.index(max(extent))
    index_at[longest] = (index_at[longest] + 1) % extent[longest]
    return values.at[tuple(index_at)].set(largest)


def setup_inputs(seed: int = 0) -> dict:
    arg_keys = jax.random.split(jax.random.key(seed), 5)
    slc = draw_slc(jax.random.fold_in(arg_keys[4], 71), 0)
    block_order = jax.random.permutation(arg_keys[1], BLOCKS).astype(jnp.int32)
    az_offset = plant(jax.random.randint(arg_keys[2], (OUT_AZ,), 0, STEP), jax.random.fold_in(arg_keys[2], 1), 0, STEP - 1).astype(jnp.int32)
    rg_offset = plant(jax.random.randint(arg_keys[3], (OUT_RG,), 0, STEP), jax.random.fold_in(arg_keys[3], 1), 0, STEP - 1).astype(jnp.int32)
    return {"slc": slc, "block_order": block_order, "az_offset": az_offset, "rg_offset": rg_offset}


epsilon = 1e-06

def window_sums(field, az_box, rg_box):
    along = jnp.einsum('ol,...lr->...or', az_box, field, precision=lax.Precision.HIGHEST)
    return jnp.einsum('...or,rc->...oc', along, rg_box, precision=lax.Precision.HIGHEST)

def reference(slc, block_order, az_offset, rg_offset):
    data = slc.astype(jnp.float32)
    row_index = jnp.arange(OUT_AZ, dtype=jnp.int32)[:, None]
    lower = STEP * row_index + az_offset[:, None] - HALO
    line_index = jnp.arange(LINES, dtype=jnp.int32)[None]
    az_box = ((line_index >= lower) & (line_index <= lower + 2 * HALO)).astype(jnp.float32)
    centre = STEP * jnp.arange(OUT_RG, dtype=jnp.int32)[None] + rg_offset[None]
    sample = jnp.arange(RANGE, dtype=jnp.int32)[:, None]
    rg_box = (jnp.abs(sample - centre) <= RG_WIN // 2).astype(jnp.float32)
    scales = lax.rsqrt(window_sums(data[0] * data[0] + data[1] * data[1], az_box, rg_box) + epsilon)
    date_rank = (block_order[:, None] * DATE_DEV + jnp.arange(DATE_DEV, dtype=jnp.int32)[None]).reshape(-1)

    def one_row(inputs):
        single, own_scale, own_rank = inputs
        real_part = single[0] * data[0] + single[1] * data[1]
        imag_part = single[1] * data[0] - single[0] * data[1]
        sums = window_sums(jnp.stack([real_part, imag_part]), az_box, rg_box)
        coherent = sums * own_scale * scales[None]
        return jnp.where((date_rank > own_rank)[None, :, None, None], coherent, 0.0)
    all_rows = lax.map(one_row, (jnp.moveaxis(data, 1, 0), scales, date_rank))
    return jnp.moveaxis(all_rows, 0, 1)
```

```python
import functools

import jax
import jax.numpy as jnp
from jax import lax
from jax.experimental import pallas as pl
from jax.experimental.pallas import tpu as pltpu
from jax.sharding import PartitionSpec as P

STEP = 4
HALO = 5
REACH = 2
EDGE = 4
LANES = 128
VMEM = pl.BlockSpec(memory_space=pltpu.VMEM)
SMEM = pl.BlockSpec(memory_space=pltpu.SMEM)
PARAMS = pltpu.CompilerParams(vmem_limit_bytes=48 * 1024 * 1024)

epsilon = 1e-06


def iota(shape, dim):
    return lax.broadcasted_iota(jnp.int32, shape, dim)


def row_of(part, line, lines):
    if line < HALO:
        return 2 * lines + part * 2 * HALO + line
    if line < HALO + lines:
        return part * lines + line - HALO
    return 2 * lines + part * 2 * HALO + line - lines


def pack_kernel(blocks, per, lines, chunk, slc, low, high, send, stage, piece):
    rows = 2 * (lines + 2 * HALO)
    date_rows = rows + EDGE
    span = blocks * chunk
    for date in range(per):
        base = date * date_rows
        for part in range(2):
            edge = base + 2 * lines + part * 2 * HALO
            stage[base + part * lines : base + (part + 1) * lines, :] = slc[part, date].astype(jnp.float32)
            stage[edge : edge + HALO, :] = low[part, date].astype(jnp.float32)
            stage[edge + HALO : edge + 2 * HALO, :] = high[part, date].astype(jnp.float32)
        stage[base + rows : base + date_rows, :] = jnp.zeros((EDGE, span), jnp.float32)
    samples = stage[...].astype(jnp.bfloat16)
    shape = (EDGE * blocks, span)
    place = iota(shape, 0) % EDGE
    wanted = iota(shape, 0) // EDGE * chunk + jnp.where(place < REACH, place - REACH, place - REACH + chunk)
    picks = (iota(shape, 1) == wanted).astype(jnp.bfloat16)
    edges = lax.dot_general(picks, samples, (((1,), (1,)), ((), ())), preferred_element_type=jnp.float32)
    lane = iota((EDGE, LANES), 1)
    for block in range(blocks):
        if chunk == LANES:
            piece[...] = stage[:, block * chunk : (block + 1) * chunk]
        else:
            piece[...] = jnp.zeros(piece.shape, jnp.float32)
            piece[:, :chunk] = stage[:, block * chunk : (block + 1) * chunk]
        for date in range(per):
            base = date * date_rows
            mine = edges[block * EDGE : (block + 1) * EDGE, base : base + date_rows]
            piece[base + rows : base + date_rows, :] = jnp.zeros((EDGE, LANES), jnp.float32)
            piece[base + rows : base + date_rows, :date_rows] = mine
        send[block] = piece[...].astype(jnp.bfloat16)


def split(value):
    high = value.astype(jnp.bfloat16)
    return high, (value - high.astype(jnp.float32)).astype(jnp.bfloat16)


def pair_kernel(blocks, per, lines, chunk, group, recv, order, az, rg, tiled, send, x, left, weights, power):
    dates = blocks * per
    out_rows = lines // STEP
    cols = chunk // STEP
    wide = out_rows * cols
    rows = 2 * (lines + 2 * HALO)
    date_rows = rows + EDGE
    me = lax.axis_index("date")
    depth = out_rows * 2 * LANES

    for block in range(blocks):
        value = recv[block].astype(jnp.float32)
        for date in range(per):
            for tile in range(date_rows // 8):
                part = value[date * date_rows + 8 * tile : date * date_rows + 8 * tile + 8]
                x[pl.ds(8 * tile * dates + block * per + date, 8, stride=dates), :] = part

    shape = (LANES, wide)
    col = iota(shape, 1) % cols
    out_row = iota(shape, 1) // cols
    box = jnp.abs(iota(shape, 0) - STEP * col - tiled[...]) <= REACH
    for o in range(out_rows):
        mine = (box & (out_row == o)).astype(jnp.bfloat16)
        weights[2 * o * LANES : (2 * o + 1) * LANES, :] = mine
        weights[(2 * o + 1) * LANES : (2 * o + 2) * LANES, :] = mine
    at = iota(shape, 0)
    turn = jnp.where(at < 2 * lines, 0, (at - 2 * lines) % (2 * HALO))
    line = jnp.where(at < 2 * lines, at % lines + HALO, jnp.where(turn < HALO, turn, turn + lines))
    line = jnp.where(at < rows, line, -100)
    lower = jnp.zeros(shape, jnp.int32)
    for o in range(out_rows):
        lower = jnp.where(out_row == o, STEP * o + az[o], lower)
    window = (line >= lower) & (line <= lower + 2 * HALO)
    for side, edge_col in ((0, 0), (1, cols - 1)):
        mine = (window & (col == edge_col)).astype(jnp.bfloat16)
        for term in range(2):
            start = depth + (2 * side + term) * LANES
            weights[start : start + LANES, :] = mine
    first = rg[me * cols]
    last = rg[me * cols + cols - 1]
    edge_on = (first <= 0, first <= 1, last >= 2, last >= 3)

    lane = iota((16, LANES), 1)

    def swapped(value):
        up = jnp.where(lane < lines, pltpu.roll(value, LANES - lines, 1), pltpu.roll(value, LANES - 2 * HALO, 1))
        down = jnp.where(lane < 2 * lines, pltpu.roll(value, lines, 1), pltpu.roll(value, 2 * HALO, 1))
        real = (lane < lines) | ((lane >= 2 * lines) & (lane < 2 * lines + 2 * HALO))
        return jnp.where(real, up, -down)

    def one_date(first_date, step, carry):
        date = first_date + step
        target = (step // per * 2) * per + step % per
        for tile in range(dates // 16):

            def own(row):
                return x[pl.ds(row * dates + date, 1), :]

            def others(row):
                return x[row * dates + tile * 16 : row * dates + tile * 16 + 16, :]

            real, imag = [], []
            for line in range(lines + 2 * HALO):
                re_i, im_i = own(row_of(0, line, lines)), own(row_of(1, line, lines))
                re_j, im_j = others(row_of(0, line, lines)), others(row_of(1, line, lines))
                real.append(re_i * re_j + im_i * im_j)
                imag.append(im_i * re_j - re_i * im_j)
            for part, product in enumerate((real, imag)):
                start = pl.multiple_of((target + part * per) * dates + tile * 16, 16)
                at_rows = pl.ds(start, 16)
                quads = []
                for k in range(out_rows + 1):
                    q = product[STEP * k + 3 : STEP * k + 7]
                    quads.append((q[0] + q[1]) + (q[2] + q[3]))
                for o in range(out_rows):
                    total = quads[o] + quads[o + 1]
                    for k in range(3):
                        total += jnp.where(az[o] <= k, product[STEP * o + k], product[STEP * o + 11 + k])
                    high, low = split(total)
                    left[at_rows, 2 * o * LANES : (2 * o + 1) * LANES] = high
                    left[at_rows, (2 * o + 1) * LANES : (2 * o + 2) * LANES] = low
                for side in range(2):
                    total = jnp.zeros((16, LANES), jnp.float32)
                    for edge in (2 * side, 2 * side + 1):
                        mine = jnp.broadcast_to(own(rows + edge), (16, LANES))
                        if part:
                            mine = swapped(mine)
                        total += jnp.where(edge_on[edge], mine * others(rows + edge), 0.0)
                    high, low = split(total)
                    start_col = depth + 2 * side * LANES
                    left[at_rows, start_col : start_col + LANES] = high
                    left[at_rows, start_col + LANES : start_col + 2 * LANES] = low
        return carry

    for first_date in range(0, dates, group):
        lax.fori_loop(0, group, functools.partial(one_date, first_date), 0)
        sums = jnp.dot(left[...], weights[...], preferred_element_type=jnp.float32)
        send[first_date * 2 * dates : (first_date + group) * 2 * dates, :] = sums
    for date in range(dates):
        at_row = (date // per * 2 * per + date % per) * dates + date
        power[date : date + 1, :] = send[at_row : at_row + 1, :]
    scale = lax.rsqrt(power[...] + epsilon)
    power[...] = scale
    position = iota((dates, wide), 0)
    rank = jnp.zeros((dates, wide), jnp.int32)
    for block in range(blocks):
        rank = jnp.where(position // per == block, order[block] * per + position % per, rank)
    for date in range(dates):
        later = rank > order[date // per] * per + date % per
        factor = jnp.where(later, scale * power[date : date + 1, :], 0.0)
        for part in range(2):
            start = ((date // per * 2 + part) * per + date % per) * dates
            send[start : start + dates, :] = send[start : start + dates, :] * factor


def join_kernel(blocks, count, out_rows, cols, recv, out, halves):
    per_tile = LANES // cols
    lane = iota((8, LANES), 1) // cols
    for start in range(0, count, 8):
        for o_tile in range(out_rows // per_tile):
            for d_tile in range(blocks // per_tile):
                tiles = [
                    recv[d_tile * per_tile + d, start : start + 8, o_tile * LANES : (o_tile + 1) * LANES]
                    for d in range(per_tile)
                ]
                width = 1
                while width < per_tile:
                    swap = [None] * per_tile
                    upper = (lane // width) % 2 == 1
                    for a in range(per_tile):
                        if (a // width) % 2 == 0:
                            b = a + width
                            shift = width * cols
                            swap[a] = jnp.where(upper, pltpu.roll(tiles[b], shift, 1), tiles[a])
                            swap[b] = jnp.where(upper, tiles[b], pltpu.roll(tiles[a], LANES - shift, 1))
                    tiles = swap
                    width *= 2
                for o in range(per_tile):
                    at = start * out_rows + o_tile * per_tile + o
                    halves[d_tile, pl.ds(at, 8, stride=out_rows), :] = tiles[o]
    for d_tile in range(blocks // per_tile):
        out[:, d_tile * LANES : (d_tile + 1) * LANES] = halves[d_tile]


def on_device(slc, block_order, az_offset, rg_offset):
    blocks = lax.axis_size("date")
    strips = lax.axis_size("strip")
    per, lines, span = slc.shape[1:]
    dates = blocks * per
    chunk = span // blocks
    out_rows = lines // STEP
    cols = chunk // STEP
    wide = out_rows * cols
    date_rows = 2 * (lines + 2 * HALO) + EDGE
    group = max(per, 256 // dates)
    me = lax.axis_index("date")

    forward = [(i, i + 1) for i in range(strips - 1)]
    backward = [(target, source) for source, target in forward]
    low = lax.ppermute(slc[:, :, lines - HALO :], "strip", forward)
    high = lax.ppermute(slc[:, :, :HALO], "strip", backward)
    tiled = jnp.tile(lax.dynamic_slice_in_dim(rg_offset, me * cols, cols), out_rows)[None]

    send = pl.pallas_call(
        functools.partial(pack_kernel, blocks, per, lines, chunk),
        out_shape=jax.ShapeDtypeStruct((blocks, per * date_rows, LANES), jnp.bfloat16),
        in_specs=[VMEM] * 3,
        out_specs=VMEM,
        scratch_shapes=[
            pltpu.VMEM((per * date_rows, span), jnp.float32),
            pltpu.VMEM((per * date_rows, LANES), jnp.float32),
        ],
        compiler_params=PARAMS,
        name="pack",
    )(slc, low, high)
    recv = lax.all_to_all(send, "date", 0, 0, tiled=True)
    depth = (out_rows + 2) * 2 * LANES
    pairs = pl.pallas_call(
        functools.partial(pair_kernel, blocks, per, lines, chunk, group),
        out_shape=jax.ShapeDtypeStruct((dates * 2 * dates, wide), jnp.float32),
        in_specs=[VMEM, SMEM, SMEM, SMEM, VMEM],
        out_specs=VMEM,
        scratch_shapes=[
            pltpu.VMEM((date_rows * dates, LANES), jnp.float32),
            pltpu.VMEM((group * 2 * dates, depth), jnp.bfloat16),
            pltpu.VMEM((depth, wide), jnp.bfloat16),
            pltpu.VMEM((dates, wide), jnp.float32),
        ],
        compiler_params=PARAMS,
        name="pairs",
    )(recv, block_order, az_offset, rg_offset, tiled)
    count = 2 * per * dates
    back = lax.all_to_all(pairs.reshape(blocks, count, wide), "date", 0, 0, tiled=True)
    if LANES % cols == 0 and out_rows * cols % LANES == 0 and blocks * cols % LANES == 0:
        out = pl.pallas_call(
            functools.partial(join_kernel, blocks, count, out_rows, cols),
            out_shape=jax.ShapeDtypeStruct((count * out_rows, blocks * cols), jnp.float32),
            in_specs=[VMEM],
            out_specs=VMEM,
            scratch_shapes=[pltpu.VMEM((blocks * cols // LANES, count * out_rows, LANES), jnp.float32)],
            compiler_params=PARAMS,
            name="join",
        )(back)
    else:
        out = back.reshape(blocks, count, out_rows, cols).transpose(1, 2, 0, 3)
    return out.reshape(2, per, dates, out_rows, blocks * cols)


def solution(mesh):
    placed = (P(None, "date", "strip", None), P(), P("strip"), P())
    return jax.shard_map(
        on_device,
        mesh=mesh,
        in_specs=placed,
        out_specs=P(None, "date", None, "strip", None),
        check_vma=False,
    )
```

```python
import functools

import jax
import jax.numpy as jnp
from jax import lax
from jax.experimental import pallas as pl
from jax.experimental.pallas import tpu as pltpu
from jax.sharding import PartitionSpec as P

STEP = 4
HALO = 5
REACH = 2
EDGE = 4
LANES = 128
GROUP = 16
VMEM = pl.BlockSpec(memory_space=pltpu.VMEM)
SMEM = pl.BlockSpec(memory_space=pltpu.SMEM)
PARAMS = pltpu.CompilerParams(vmem_limit_bytes=48 * 1024 * 1024)

epsilon = 1e-06


def iota(shape, dim):
    return lax.broadcasted_iota(jnp.int32, shape, dim)


def row_of(part, line, lines):
    if line < HALO:
        return part * HALO + line
    if line >= lines - HALO:
        return GROUP + part * HALO + line - (lines - HALO)
    middle = part * (lines - 2 * HALO) + line - HALO
    spare = GROUP - 2 * HALO - EDGE
    if middle < spare:
        return 2 * HALO + EDGE + middle
    if middle < 2 * spare:
        return GROUP + 2 * HALO + EDGE + middle - spare
    return 2 * GROUP + middle - 2 * spare


def place_of(date, row, per, date_rows):
    if row < GROUP:
        return date * GROUP + row
    if row < 2 * GROUP:
        return (per + date - 1) * GROUP + row
    return 2 * per * GROUP + date * (date_rows - 2 * GROUP) + row - 2 * GROUP


def rows_of_date(lines):
    return 2 * GROUP + 2 * (lines - 2 * HALO) - 2 * (GROUP - 2 * HALO - EDGE)


def runs(part, lines):
    found = []
    for line in range(lines):
        row = row_of(part, line, lines)
        if line and row == row_of(part, line - 1, lines) + 1 and row % GROUP:
            found[-1][1] += 1
        else:
            found.append([line, 1])
    return found


def pack_kernel(blocks, per, lines, chunk, slc, send, stage):
    date_rows = rows_of_date(lines)
    span = blocks * chunk
    shape = (EDGE * blocks, span)
    place = iota(shape, 0) % EDGE
    wanted = iota(shape, 0) // EDGE * chunk + jnp.where(place < REACH, place - REACH, place - REACH + chunk)
    picks = (iota(shape, 1) == wanted).astype(jnp.bfloat16)
    lane = iota((EDGE * blocks, LANES), 1)
    edges = []
    for date in range(per):
        mine = jnp.zeros((EDGE * blocks, LANES), jnp.float32)
        for part in range(2):
            samples = slc[part, date]
            for first, count in runs(part, lines):
                at = place_of(date, row_of(part, first, lines), per, date_rows)
                stage[at : at + count, :] = samples[first : first + count].astype(jnp.float32)
            found = lax.dot_general(picks, samples, (((1,), (1,)), ((), ())), preferred_element_type=jnp.float32)
            found = jnp.concatenate([found, jnp.zeros((EDGE * blocks, LANES - lines), jnp.float32)], axis=1)
            mine += pltpu.roll(found, part * (LANES // 2), 1) if part else found
        edges.append(mine)
    for block in range(blocks):
        for date in range(per):
            for group in range(2):
                at = place_of(date, group * GROUP + 2 * HALO, per, date_rows)
                value = edges[date][block * EDGE : (block + 1) * EDGE]
                if chunk == LANES:
                    stage[at : at + EDGE, block * LANES : (block + 1) * LANES] = value
        if chunk == LANES:
            piece = stage[:, block * chunk : (block + 1) * chunk]
        else:
            piece = stage[:, block * chunk : (block + 1) * chunk]
            piece = jnp.concatenate([piece, jnp.zeros((per * date_rows, LANES - chunk), jnp.float32)], axis=1)
            row = iota((per * date_rows, LANES), 0)
            for date in range(per):
                for group in range(2):
                    at = place_of(date, group * GROUP + 2 * HALO, per, date_rows)
                    for k in range(EDGE):
                        value = edges[date][block * EDGE + k : block * EDGE + k + 1]
                        piece = jnp.where(row == at + k, value, piece)
        send[block] = piece.astype(jnp.bfloat16)


def weight_kernel(lines, chunk, az, tiled, weights):
    out_rows = lines // STEP
    cols = chunk // STEP
    wide = out_rows * cols
    depth = out_rows * 2 * LANES
    shape = (LANES, wide)
    col = iota(shape, 1) % cols
    out_row = iota(shape, 1) // cols
    box = jnp.abs(iota(shape, 0) - STEP * col - tiled[...]) <= REACH
    for o in range(out_rows):
        mine = (box & (out_row == o)).astype(jnp.bfloat16)
        weights[2 * o * LANES : (2 * o + 1) * LANES, :] = mine
        weights[(2 * o + 1) * LANES : (2 * o + 2) * LANES, :] = mine
    turn = iota(shape, 0) % (LANES // 2)
    line = jnp.where(turn < lines + HALO, turn + HALO, turn + HALO - LANES // 2)
    lower = jnp.zeros(shape, jnp.int32)
    for o in range(out_rows):
        lower = jnp.where(out_row == o, STEP * o + az[o], lower)
    window = (line >= lower) & (line <= lower + 2 * HALO)
    for side, edge_col in ((0, 0), (1, cols - 1)):
        mine = (window & (col == edge_col)).astype(jnp.bfloat16)
        for term in range(2):
            start = depth + (2 * side + term) * LANES
            weights[start : start + LANES, :] = mine


def to_sublanes(blocks, per, rows, place, source, target):
    dates = blocks * per
    for block in range(blocks):
        value = source[block].astype(jnp.float32)
        for date in range(per):
            for row in range(0, rows, 8):
                at = place(date, row)
                target[pl.ds(row * dates + block * per + date, 8, stride=dates), :] = value[at : at + 8]


def spread_kernel(blocks, per, lines, recv, x):
    date_rows = rows_of_date(lines)
    to_sublanes(blocks, per, date_rows, lambda date, row: place_of(date, row, per, date_rows), recv, x)


def split(value):
    high = value.astype(jnp.bfloat16)
    return high, (value - high.astype(jnp.float32)).astype(jnp.bfloat16)


def pair_kernel(
    blocks, per, lines, chunk, group, x, low, high, order, az, rg, weights, send, below, above, edges, turned, left, power
):
    dates = blocks * per
    out_rows = lines // STEP
    cols = chunk // STEP
    wide = out_rows * cols
    me = lax.axis_index("date")
    depth = out_rows * 2 * LANES

    to_sublanes(blocks, per, GROUP, lambda date, row: date * GROUP + row, low, below)
    to_sublanes(blocks, per, GROUP, lambda date, row: date * GROUP + row, high, above)
    lane = iota((dates, LANES), 1)
    turn = lane % (LANES // 2)
    for k in range(EDGE):
        at = (2 * HALO + k) * dates
        lower_part = pltpu.roll(below[at : at + dates, :], lines, 1)
        upper_part = pltpu.roll(above[at : at + dates, :], lines, 1)
        value = jnp.where(turn < lines, x[at : at + dates, :], jnp.where(turn < lines + HALO, upper_part, lower_part))
        edges[k * dates : (k + 1) * dates, :] = value
        value = pltpu.roll(value, LANES // 2, 1)
        turned[k * dates : (k + 1) * dates, :] = jnp.where(lane < LANES // 2, value, -value)
    first = rg[me * cols]
    last = rg[me * cols + cols - 1]
    edge_on = (first <= 0, first <= 1, last >= 2, last >= 3)

    def where_line(part, line):
        if line < HALO:
            return below, part * HALO + line
        if line >= lines + HALO:
            return above, part * HALO + line - (lines + HALO)
        return x, row_of(part, line - HALO, lines)

    def one_date(first_date, step, carry):
        date = first_date + step
        target = (step // per * 2) * per + step % per
        for tile in range(dates // 16):

            def own(ref, row):
                return ref[pl.ds(row * dates + date, 1), :]

            def others(ref, row):
                return ref[row * dates + tile * 16 : row * dates + tile * 16 + 16, :]

            real, imag = [], []
            for line in range(lines + 2 * HALO):
                at_re, at_im = where_line(0, line), where_line(1, line)
                re_i, im_i = own(*at_re), own(*at_im)
                re_j, im_j = others(*at_re), others(*at_im)
                real.append(re_i * re_j + im_i * im_j)
                imag.append(im_i * re_j - re_i * im_j)
            for part, product in enumerate((real, imag)):
                start = pl.multiple_of((target + part * per) * dates + tile * 16, 16)
                at_rows = pl.ds(start, 16)
                quads = []
                for k in range(out_rows + 1):
                    q = product[STEP * k + 3 : STEP * k + 7]
                    quads.append((q[0] + q[1]) + (q[2] + q[3]))
                for o in range(out_rows):
                    total = quads[o] + quads[o + 1]
                    for k in range(3):
                        total += jnp.where(az[o] <= k, product[STEP * o + k], product[STEP * o + 11 + k])
                    upper, rest = split(total)
                    left[at_rows, 2 * o * LANES : (2 * o + 1) * LANES] = upper
                    left[at_rows, (2 * o + 1) * LANES : (2 * o + 2) * LANES] = rest
                for side in range(2):
                    total = jnp.zeros((16, LANES), jnp.float32)
                    for edge in (2 * side, 2 * side + 1):
                        mine = own(turned if part else edges, edge)
                        total += jnp.where(edge_on[edge], mine * others(edges, edge), 0.0)
                    upper, rest = split(total)
                    start_col = depth + 2 * side * LANES
                    left[at_rows, start_col : start_col + LANES] = upper
                    left[at_rows, start_col + LANES : start_col + 2 * LANES] = rest
        return carry

    for first_date in range(0, dates, group):
        lax.fori_loop(0, group, functools.partial(one_date, first_date), 0)
        sums = jnp.dot(left[...], weights[...], preferred_element_type=jnp.float32)
        send[first_date * 2 * dates : (first_date + group) * 2 * dates, :] = sums
    for date in range(dates):
        at_row = (date // per * 2 * per + date % per) * dates + date
        power[date : date + 1, :] = send[at_row : at_row + 1, :]
    scale = lax.rsqrt(power[...] + epsilon)
    power[...] = scale
    position = iota((dates, wide), 0)
    rank = jnp.zeros((dates, wide), jnp.int32)
    for block in range(blocks):
        rank = jnp.where(position // per == block, order[block] * per + position % per, rank)
    for date in range(dates):
        later = rank > order[date // per] * per + date % per
        factor = jnp.where(later, scale * power[date : date + 1, :], 0.0)
        for part in range(2):
            start = ((date // per * 2 + part) * per + date % per) * dates
            send[start : start + dates, :] = send[start : start + dates, :] * factor


def join_kernel(blocks, count, out_rows, cols, recv, out, halves):
    per_tile = LANES // cols
    lane = iota((8, LANES), 1) // cols
    for start in range(0, count, 8):
        for o_tile in range(out_rows // per_tile):
            for d_tile in range(blocks // per_tile):
                tiles = [
                    recv[d_tile * per_tile + d, start : start + 8, o_tile * LANES : (o_tile + 1) * LANES]
                    for d in range(per_tile)
                ]
                width = 1
                while width < per_tile:
                    swap = [None] * per_tile
                    upper = (lane // width) % 2 == 1
                    for a in range(per_tile):
                        if (a // width) % 2 == 0:
                            b = a + width
                            shift = width * cols
                            swap[a] = jnp.where(upper, pltpu.roll(tiles[b], shift, 1), tiles[a])
                            swap[b] = jnp.where(upper, tiles[b], pltpu.roll(tiles[a], LANES - shift, 1))
                    tiles = swap
                    width *= 2
                for o in range(per_tile):
                    at = start * out_rows + o_tile * per_tile + o
                    halves[d_tile, pl.ds(at, 8, stride=out_rows), :] = tiles[o]
    for d_tile in range(blocks // per_tile):
        out[:, d_tile * LANES : (d_tile + 1) * LANES] = halves[d_tile]


def on_device(slc, block_order, az_offset, rg_offset):
    blocks = lax.axis_size("date")
    strips = lax.axis_size("strip")
    per, lines, span = slc.shape[1:]
    dates = blocks * per
    chunk = span // blocks
    out_rows = lines // STEP
    cols = chunk // STEP
    wide = out_rows * cols
    date_rows = rows_of_date(lines)
    depth = (out_rows + 2) * 2 * LANES
    group = max(per, 256 // dates)
    me = lax.axis_index("date")

    send = pl.pallas_call(
        functools.partial(pack_kernel, blocks, per, lines, chunk),
        out_shape=jax.ShapeDtypeStruct((blocks, per * date_rows, LANES), jnp.bfloat16),
        in_specs=[VMEM],
        out_specs=VMEM,
        scratch_shapes=[pltpu.VMEM((per * date_rows, span), jnp.float32)],
        compiler_params=PARAMS,
        name="pack",
    )(slc)
    recv = lax.all_to_all(send, "date", 0, 0, tiled=True)
    tiled = jnp.tile(lax.dynamic_slice_in_dim(rg_offset, me * cols, cols), out_rows)[None]
    weights = pl.pallas_call(
        functools.partial(weight_kernel, lines, chunk),
        out_shape=jax.ShapeDtypeStruct((depth, wide), jnp.bfloat16),
        in_specs=[SMEM, VMEM],
        out_specs=VMEM,
        compiler_params=PARAMS,
        cost_estimate=pl.CostEstimate(flops=0, bytes_accessed=4 * 1024 * 1024, transcendentals=0),
        name="weights",
    )(az_offset, tiled)

    forward = [(i, i + 1) for i in range(strips - 1)]
    backward = [(target, source) for source, target in forward]
    edge_rows = per * GROUP
    low = lax.ppermute(recv[:, edge_rows : 2 * edge_rows], "strip", forward)
    high = lax.ppermute(recv[:, :edge_rows], "strip", backward)
    x = pl.pallas_call(
        functools.partial(spread_kernel, blocks, per, lines),
        out_shape=jax.ShapeDtypeStruct((date_rows * dates, LANES), jnp.float32),
        in_specs=[VMEM],
        out_specs=VMEM,
        compiler_params=PARAMS,
        cost_estimate=pl.CostEstimate(flops=0, bytes_accessed=4 * 1024 * 1024, transcendentals=0),
        name="spread",
    )(recv)
    pairs = pl.pallas_call(
        functools.partial(pair_kernel, blocks, per, lines, chunk, group),
        out_shape=jax.ShapeDtypeStruct((dates * 2 * dates, wide), jnp.float32),
        in_specs=[VMEM, VMEM, VMEM, SMEM, SMEM, SMEM, VMEM],
        out_specs=VMEM,
        scratch_shapes=[
            pltpu.VMEM((GROUP * dates, LANES), jnp.float32),
            pltpu.VMEM((GROUP * dates, LANES), jnp.float32),
            pltpu.VMEM((EDGE * dates, LANES), jnp.float32),
            pltpu.VMEM((EDGE * dates, LANES), jnp.float32),
            pltpu.VMEM((group * 2 * dates, depth), jnp.bfloat16),
            pltpu.VMEM((dates, wide), jnp.float32),
        ],
        compiler_params=PARAMS,
        name="pairs",
    )(x, low, high, block_order, az_offset, rg_offset, weights)
    count = 2 * per * dates
    back = lax.all_to_all(pairs.reshape(blocks, count, wide), "date", 0, 0, tiled=True)
    if LANES % cols == 0 and out_rows * cols % LANES == 0 and blocks * cols % LANES == 0:
        out = pl.pallas_call(
            functools.partial(join_kernel, blocks, count, out_rows, cols),
            out_shape=jax.ShapeDtypeStruct((count * out_rows, blocks * cols), jnp.float32),
            in_specs=[VMEM],
            out_specs=VMEM,
            scratch_shapes=[pltpu.VMEM((blocks * cols // LANES, count * out_rows, LANES), jnp.float32)],
            compiler_params=PARAMS,
            name="join",
        )(back)
    else:
        out = back.reshape(blocks, count, out_rows, cols).transpose(1, 2, 0, 3)
    return out.reshape(2, per, dates, out_rows, blocks * cols)


def solution(mesh):
    placed = (P(None, "date", "strip", None), P(), P("strip"), P())
    return jax.shard_map(
        on_device,
        mesh=mesh,
        in_specs=placed,
        out_specs=P(None, "date", None, "strip", None),
        check_vma=False,
    )
```

```python
import functools

import jax
import jax.numpy as jnp
from jax import lax
from jax.experimental import pallas as pl
from jax.experimental.pallas import tpu as pltpu
from jax.sharding import PartitionSpec as P

STEP = 4
HALO = 5
REACH = 2
EDGE = 4
LANES = 128
GROUP = 16
VMEM = pl.BlockSpec(memory_space=pltpu.VMEM)
SMEM = pl.BlockSpec(memory_space=pltpu.SMEM)
PARAMS = pltpu.CompilerParams(vmem_limit_bytes=48 * 1024 * 1024)

epsilon = 1e-06
LEVELS = 8.0
LOWEST, HIGHEST = -880.0, 64.0
TOP = 32760.0
LOG_2 = 0.6931471805599453


def iota(shape, dim):
    return lax.broadcasted_iota(jnp.int32, shape, dim)


def row_of(part, line, lines):
    if line < HALO:
        return part * HALO + line
    if line >= lines - HALO:
        return GROUP + part * HALO + line - (lines - HALO)
    middle = part * (lines - 2 * HALO) + line - HALO
    spare = GROUP - 2 * HALO - EDGE
    if middle < spare:
        return 2 * HALO + EDGE + middle
    if middle < 2 * spare:
        return GROUP + 2 * HALO + EDGE + middle - spare
    return 2 * GROUP + middle - 2 * spare


def place_of(date, row, per, date_rows):
    if row < GROUP:
        return date * GROUP + row
    if row < 2 * GROUP:
        return (per + date - 1) * GROUP + row
    return 2 * per * GROUP + date * (date_rows - 2 * GROUP) + row - 2 * GROUP


def rows_of_date(lines):
    return 2 * GROUP + 2 * (lines - 2 * HALO) - 2 * (GROUP - 2 * HALO - EDGE)


def runs(part, lines):
    found = []
    for line in range(lines):
        row = row_of(part, line, lines)
        if line and row == row_of(part, line - 1, lines) + 1 and row % GROUP:
            found[-1][1] += 1
        else:
            found.append([line, 1])
    return found


def pack_kernel(blocks, per, lines, chunk, slc, send, stage):
    date_rows = rows_of_date(lines)
    span = blocks * chunk
    shape = (EDGE * blocks, span)
    place = iota(shape, 0) % EDGE
    wanted = iota(shape, 0) // EDGE * chunk + jnp.where(place < REACH, place - REACH, place - REACH + chunk)
    picks = (iota(shape, 1) == wanted).astype(jnp.bfloat16)
    lane = iota((EDGE * blocks, LANES), 1)
    edges = []
    for date in range(per):
        mine = jnp.zeros((EDGE * blocks, LANES), jnp.float32)
        for part in range(2):
            samples = slc[part, date]
            for first, count in runs(part, lines):
                at = place_of(date, row_of(part, first, lines), per, date_rows)
                stage[at : at + count, :] = samples[first : first + count].astype(jnp.float32)
            found = lax.dot_general(picks, samples, (((1,), (1,)), ((), ())), preferred_element_type=jnp.float32)
            found = jnp.concatenate([found, jnp.zeros((EDGE * blocks, LANES - lines), jnp.float32)], axis=1)
            mine += pltpu.roll(found, part * (LANES // 2), 1) if part else found
        edges.append(mine)
    for block in range(blocks):
        for date in range(per):
            for group in range(2):
                at = place_of(date, group * GROUP + 2 * HALO, per, date_rows)
                value = edges[date][block * EDGE : (block + 1) * EDGE]
                if chunk == LANES:
                    stage[at : at + EDGE, block * LANES : (block + 1) * LANES] = value
        if chunk == LANES:
            piece = stage[:, block * chunk : (block + 1) * chunk]
        else:
            piece = stage[:, block * chunk : (block + 1) * chunk]
            piece = jnp.concatenate([piece, jnp.zeros((per * date_rows, LANES - chunk), jnp.float32)], axis=1)
            row = iota((per * date_rows, LANES), 0)
            for date in range(per):
                for group in range(2):
                    at = place_of(date, group * GROUP + 2 * HALO, per, date_rows)
                    for k in range(EDGE):
                        value = edges[date][block * EDGE + k : block * EDGE + k + 1]
                        piece = jnp.where(row == at + k, value, piece)
        send[block] = piece.astype(jnp.bfloat16)


def weight_kernel(lines, chunk, az, tiled, weights):
    out_rows = lines // STEP
    cols = chunk // STEP
    wide = out_rows * cols
    depth = out_rows * 2 * LANES
    shape = (LANES, wide)
    col = iota(shape, 1) % cols
    out_row = iota(shape, 1) // cols
    box = jnp.abs(iota(shape, 0) - STEP * col - tiled[...]) <= REACH
    for o in range(out_rows):
        mine = (box & (out_row == o)).astype(jnp.bfloat16)
        weights[2 * o * LANES : (2 * o + 1) * LANES, :] = mine
        weights[(2 * o + 1) * LANES : (2 * o + 2) * LANES, :] = mine
    turn = iota(shape, 0) % (LANES // 2)
    line = jnp.where(turn < lines + HALO, turn + HALO, turn + HALO - LANES // 2)
    lower = jnp.zeros(shape, jnp.int32)
    for o in range(out_rows):
        lower = jnp.where(out_row == o, STEP * o + az[o], lower)
    window = (line >= lower) & (line <= lower + 2 * HALO)
    for side, edge_col in ((0, 0), (1, cols - 1)):
        mine = (window & (col == edge_col)).astype(jnp.bfloat16)
        for term in range(2):
            start = depth + (2 * side + term) * LANES
            weights[start : start + LANES, :] = mine


def to_sublanes(blocks, per, rows, place, source, target):
    dates = blocks * per
    for block in range(blocks):
        value = source[block].astype(jnp.float32)
        for date in range(per):
            for row in range(0, rows, 8):
                at = place(date, row)
                target[pl.ds(row * dates + block * per + date, 8, stride=dates), :] = value[at : at + 8]


def spread_kernel(blocks, per, lines, recv, x):
    date_rows = rows_of_date(lines)
    to_sublanes(blocks, per, date_rows, lambda date, row: place_of(date, row, per, date_rows), recv, x)


def split(value):
    high = value.astype(jnp.bfloat16)
    return high, (value - high.astype(jnp.float32)).astype(jnp.bfloat16)


def pair_kernel(
    blocks, per, lines, chunk, group, x, low, high, order, az, rg, weights, send, sums, below, above, edges, turned, left, power
):
    dates = blocks * per
    out_rows = lines // STEP
    cols = chunk // STEP
    wide = out_rows * cols
    me = lax.axis_index("date")
    depth = out_rows * 2 * LANES

    to_sublanes(blocks, per, GROUP, lambda date, row: date * GROUP + row, low, below)
    to_sublanes(blocks, per, GROUP, lambda date, row: date * GROUP + row, high, above)
    lane = iota((dates, LANES), 1)
    turn = lane % (LANES // 2)
    for k in range(EDGE):
        at = (2 * HALO + k) * dates
        lower_part = pltpu.roll(below[at : at + dates, :], lines, 1)
        upper_part = pltpu.roll(above[at : at + dates, :], lines, 1)
        value = jnp.where(turn < lines, x[at : at + dates, :], jnp.where(turn < lines + HALO, upper_part, lower_part))
        edges[k * dates : (k + 1) * dates, :] = value
        value = pltpu.roll(value, LANES // 2, 1)
        turned[k * dates : (k + 1) * dates, :] = jnp.where(lane < LANES // 2, value, -value)
    first = rg[me * cols]
    last = rg[me * cols + cols - 1]
    edge_on = (first <= 0, first <= 1, last >= 2, last >= 3)

    def where_line(part, line):
        if line < HALO:
            return below, part * HALO + line
        if line >= lines + HALO:
            return above, part * HALO + line - (lines + HALO)
        return x, row_of(part, line - HALO, lines)

    def one_date(first_date, step, carry):
        date = first_date + step
        target = (step // per * 2) * per + step % per
        for tile in range(dates // 16):

            def own(ref, row):
                return ref[pl.ds(row * dates + date, 1), :]

            def others(ref, row):
                return ref[row * dates + tile * 16 : row * dates + tile * 16 + 16, :]

            real, imag = [], []
            for line in range(lines + 2 * HALO):
                at_re, at_im = where_line(0, line), where_line(1, line)
                re_i, im_i = own(*at_re), own(*at_im)
                re_j, im_j = others(*at_re), others(*at_im)
                real.append(re_i * re_j + im_i * im_j)
                imag.append(im_i * re_j - re_i * im_j)
            for part, product in enumerate((real, imag)):
                start = pl.multiple_of((target + part * per) * dates + tile * 16, 16)
                at_rows = pl.ds(start, 16)
                quads = []
                for k in range(out_rows + 1):
                    q = product[STEP * k + 3 : STEP * k + 7]
                    quads.append((q[0] + q[1]) + (q[2] + q[3]))
                for o in range(out_rows):
                    total = quads[o] + quads[o + 1]
                    for k in range(3):
                        total += jnp.where(az[o] <= k, product[STEP * o + k], product[STEP * o + 11 + k])
                    upper, rest = split(total)
                    left[at_rows, 2 * o * LANES : (2 * o + 1) * LANES] = upper
                    left[at_rows, (2 * o + 1) * LANES : (2 * o + 2) * LANES] = rest
                for side in range(2):
                    total = jnp.zeros((16, LANES), jnp.float32)
                    for edge in (2 * side, 2 * side + 1):
                        mine = own(turned if part else edges, edge)
                        total += jnp.where(edge_on[edge], mine * others(edges, edge), 0.0)
                    upper, rest = split(total)
                    start_col = depth + 2 * side * LANES
                    left[at_rows, start_col : start_col + LANES] = upper
                    left[at_rows, start_col + LANES : start_col + 2 * LANES] = rest
        return carry

    for first_date in range(0, dates, group):
        lax.fori_loop(0, group, functools.partial(one_date, first_date), 0)
        found = jnp.dot(left[...], weights[...], preferred_element_type=jnp.float32)
        sums[first_date * 2 * dates : (first_date + group) * 2 * dates, :] = found
    for date in range(dates):
        at_row = (date // per * 2 * per + date % per) * dates + date
        power[date : date + 1, :] = sums[at_row : at_row + 1, :]
    scale = lax.rsqrt(power[...] + epsilon)
    power[...] = scale
    position = iota((dates, wide), 0)
    column = iota((dates, wide), 1)
    rank = jnp.zeros((dates, wide), jnp.int32)
    for block in range(blocks):
        rank = jnp.where(position // per == block, order[block] * per + position % per, rank)
    for date in range(dates):
        later = rank > order[date // per] * per + date % per
        factor = scale * power[date : date + 1, :]
        starts = [((date // per * 2 + part) * per + date % per) * dates for part in range(2)]
        values = [jnp.where(later, sums[start : start + dates, :] * factor, 0.0) for start in starts]
        largest = jnp.max(jnp.maximum(jnp.abs(values[0]), jnp.abs(values[1])), axis=1, keepdims=True)
        level = jnp.floor(jnp.log(largest) * (LEVELS / LOG_2)) + 1.0
        level = jnp.clip(level, LOWEST, HIGHEST)
        codes = [jnp.floor(value * (jnp.exp(level * (-LOG_2 / LEVELS)) * TOP) + 0.5) for value in values]
        header = jnp.sum(jnp.where(position == column, level, 0.0), axis=0, keepdims=True)
        codes[0] = jnp.where(position == date, header, codes[0])
        for start, code in zip(starts, codes):
            send[start : start + dates, :] = code.astype(jnp.int32).astype(jnp.int16)


def join_kernel(blocks, per, out_rows, cols, recv, out, halves):
    dates = blocks * per
    wide = out_rows * cols
    per_tile = LANES // cols
    me = lax.axis_index("date")
    step = pl.program_id(0)
    part = step // per
    own = me * per + step % per
    lane = iota((dates, LANES), 1) // cols
    position = iota((dates, wide), 0)
    column = iota((dates, wide), 1)
    values = []
    for block in range(blocks):
        codes = recv[block, pl.ds(pl.multiple_of(step * dates, 16), dates), :].astype(jnp.int32).astype(jnp.float32)
        heads = recv[block, pl.ds(pl.multiple_of(step % per * dates, 16), dates), :].astype(jnp.int32).astype(jnp.float32)
        header = jnp.sum(jnp.where(position == own, heads, 0.0), axis=0, keepdims=True)
        level = jnp.sum(jnp.where(position == column, header, 0.0), axis=1, keepdims=True)
        factor = jnp.exp(level * (LOG_2 / LEVELS)) * (1.0 / TOP)
        values.append(jnp.where(position == own, 0.0, codes * factor))
    for o_tile in range(out_rows // per_tile):
        for d_tile in range(blocks // per_tile):
            tiles = [
                values[d_tile * per_tile + d][:, o_tile * LANES : (o_tile + 1) * LANES] for d in range(per_tile)
            ]
            width = 1
            while width < per_tile:
                swap = [None] * per_tile
                upper = (lane // width) % 2 == 1
                shift = width * cols
                for a in range(per_tile):
                    if (a // width) % 2 == 0:
                        b = a + width
                        swap[a] = jnp.where(upper, pltpu.roll(tiles[b], shift, 1), tiles[a])
                        swap[b] = jnp.where(upper, tiles[b], pltpu.roll(tiles[a], LANES - shift, 1))
                tiles = swap
                width *= 2
            for o in range(per_tile):
                for start in range(0, dates, 8):
                    at = start * out_rows + o_tile * per_tile + o
                    halves[d_tile, pl.ds(at, 8, stride=out_rows), :] = tiles[o][start : start + 8]
    for d_tile in range(blocks // per_tile):
        out[:, d_tile * LANES : (d_tile + 1) * LANES] = halves[d_tile]


def decode(codes, me, per):
    values = codes.astype(jnp.float32)
    dates = codes.shape[3]
    own = (me * per + jnp.arange(per))[:, None] == jnp.arange(dates)[None]
    header = jnp.sum(jnp.where(own[None, :, :, None], values[:, 0], 0.0), axis=2)
    factor = jnp.exp(header[:, :, :dates] * (LOG_2 / LEVELS)) * (1.0 / TOP)
    return jnp.where(own[None, None, :, :, None], 0.0, values * factor[:, None, :, :, None])


def on_device(slc, block_order, az_offset, rg_offset):
    blocks = lax.axis_size("date")
    strips = lax.axis_size("strip")
    per, lines, span = slc.shape[1:]
    dates = blocks * per
    chunk = span // blocks
    out_rows = lines // STEP
    cols = chunk // STEP
    wide = out_rows * cols
    date_rows = rows_of_date(lines)
    depth = (out_rows + 2) * 2 * LANES
    group = max(per, 256 // dates)
    me = lax.axis_index("date")

    send = pl.pallas_call(
        functools.partial(pack_kernel, blocks, per, lines, chunk),
        out_shape=jax.ShapeDtypeStruct((blocks, per * date_rows, LANES), jnp.bfloat16),
        in_specs=[VMEM],
        out_specs=VMEM,
        scratch_shapes=[pltpu.VMEM((per * date_rows, span), jnp.float32)],
        compiler_params=PARAMS,
        name="pack",
    )(slc)
    recv = lax.all_to_all(send, "date", 0, 0, tiled=True)
    tiled = jnp.tile(lax.dynamic_slice_in_dim(rg_offset, me * cols, cols), out_rows)[None]
    weights = pl.pallas_call(
        functools.partial(weight_kernel, lines, chunk),
        out_shape=jax.ShapeDtypeStruct((depth, wide), jnp.bfloat16),
        in_specs=[SMEM, VMEM],
        out_specs=VMEM,
        compiler_params=PARAMS,
        cost_estimate=pl.CostEstimate(flops=0, bytes_accessed=4 * 1024 * 1024, transcendentals=0),
        name="weights",
    )(az_offset, tiled)

    forward = [(i, i + 1) for i in range(strips - 1)]
    backward = [(target, source) for source, target in forward]
    edge_rows = per * GROUP
    low = lax.ppermute(recv[:, edge_rows : 2 * edge_rows], "strip", forward)
    high = lax.ppermute(recv[:, :edge_rows], "strip", backward)
    x = pl.pallas_call(
        functools.partial(spread_kernel, blocks, per, lines),
        out_shape=jax.ShapeDtypeStruct((date_rows * dates, LANES), jnp.float32),
        in_specs=[VMEM],
        out_specs=VMEM,
        compiler_params=PARAMS,
        cost_estimate=pl.CostEstimate(flops=0, bytes_accessed=4 * 1024 * 1024, transcendentals=0),
        name="spread",
    )(recv)
    pairs = pl.pallas_call(
        functools.partial(pair_kernel, blocks, per, lines, chunk, group),
        out_shape=jax.ShapeDtypeStruct((dates * 2 * dates, wide), jnp.int16),
        in_specs=[VMEM, VMEM, VMEM, SMEM, SMEM, SMEM, VMEM],
        out_specs=VMEM,
        scratch_shapes=[
            pltpu.VMEM((dates * 2 * dates, wide), jnp.float32),
            pltpu.VMEM((GROUP * dates, LANES), jnp.float32),
            pltpu.VMEM((GROUP * dates, LANES), jnp.float32),
            pltpu.VMEM((EDGE * dates, LANES), jnp.float32),
            pltpu.VMEM((EDGE * dates, LANES), jnp.float32),
            pltpu.VMEM((group * 2 * dates, depth), jnp.bfloat16),
            pltpu.VMEM((dates, wide), jnp.float32),
        ],
        compiler_params=PARAMS,
        name="pairs",
    )(x, low, high, block_order, az_offset, rg_offset, weights)
    count = 2 * per * dates
    back = lax.all_to_all(pairs.reshape(blocks, count, wide), "date", 0, 0, tiled=True)
    if LANES % cols == 0 and out_rows * cols % LANES == 0 and blocks * cols % LANES == 0:
        out = pl.pallas_call(
            functools.partial(join_kernel, blocks, per, out_rows, cols),
            grid=(2 * per,),
            out_shape=jax.ShapeDtypeStruct((count * out_rows, blocks * cols), jnp.float32),
            in_specs=[pl.BlockSpec((blocks, count, wide), lambda step: (0, 0, 0))],
            out_specs=pl.BlockSpec((dates * out_rows, blocks * cols), lambda step: (step, 0)),
            scratch_shapes=[pltpu.VMEM((blocks * cols // LANES, dates * out_rows, LANES), jnp.float32)],
            compiler_params=PARAMS,
            name="join",
        )(back)
    else:
        values = decode(back.reshape(blocks, 2, per, dates, wide), me, per)
        out = values.reshape(blocks, count, out_rows, cols).transpose(1, 2, 0, 3)
    return out.reshape(2, per, dates, out_rows, blocks * cols)


def solution(mesh):
    placed = (P(None, "date", "strip", None), P(), P("strip"), P())
    return jax.shard_map(
        on_device,
        mesh=mesh,
        in_specs=placed,
        out_specs=P(None, "date", None, "strip", None),
        check_vma=False,
    )
```

```python
import functools

import jax
import jax.numpy as jnp
from jax import lax
from jax.experimental import pallas as pl
from jax.experimental.pallas import tpu as pltpu
from jax.sharding import PartitionSpec as P

STEP = 4
HALO = 5
REACH = 2
EDGE = 4
LANES = 128
GROUP = 16
VMEM = pl.BlockSpec(memory_space=pltpu.VMEM)
SMEM = pl.BlockSpec(memory_space=pltpu.SMEM)
PARAMS = pltpu.CompilerParams(vmem_limit_bytes=48 * 1024 * 1024)

epsilon = 1e-06
LEVELS = 8.0
LOWEST, HIGHEST = -880.0, 64.0
TOP = 32760.0
LOG_2 = 0.6931471805599453


def iota(shape, dim):
    return lax.broadcasted_iota(jnp.int32, shape, dim)


def row_of(part, line, lines):
    if line < HALO:
        return part * HALO + line
    if line >= lines - HALO:
        return GROUP + part * HALO + line - (lines - HALO)
    middle = part * (lines - 2 * HALO) + line - HALO
    spare = GROUP - 2 * HALO - EDGE
    if middle < spare:
        return 2 * HALO + EDGE + middle
    if middle < 2 * spare:
        return GROUP + 2 * HALO + EDGE + middle - spare
    return 2 * GROUP + middle - 2 * spare


def place_of(date, row, per, date_rows):
    if row < GROUP:
        return date * GROUP + row
    if row < 2 * GROUP:
        return (per + date - 1) * GROUP + row
    return 2 * per * GROUP + date * (date_rows - 2 * GROUP) + row - 2 * GROUP


def rows_of_date(lines):
    return 2 * GROUP + 2 * (lines - 2 * HALO) - 2 * (GROUP - 2 * HALO - EDGE)


def runs(part, lines):
    found = []
    for line in range(lines):
        row = row_of(part, line, lines)
        if line and row == row_of(part, line - 1, lines) + 1 and row % GROUP:
            found[-1][1] += 1
        else:
            found.append([line, 1])
    return found


def pack_kernel(blocks, per, lines, chunk, slc, send, stage):
    date_rows = rows_of_date(lines)
    edge_rows = per * GROUP
    turn = 1 - lax.axis_index("strip") % 2
    span = blocks * chunk
    shape = (EDGE * blocks, span)
    place = iota(shape, 0) % EDGE
    wanted = iota(shape, 0) // EDGE * chunk + jnp.where(place < REACH, place - REACH, place - REACH + chunk)
    picks = (iota(shape, 1) == wanted).astype(jnp.bfloat16)
    lane = iota((EDGE * blocks, LANES), 1)
    edges = []
    for date in range(per):
        mine = jnp.zeros((EDGE * blocks, LANES), jnp.float32)
        for part in range(2):
            samples = slc[part, date]
            for first, count in runs(part, lines):
                at = place_of(date, row_of(part, first, lines), per, date_rows)
                stage[at : at + count, :] = samples[first : first + count].astype(jnp.float32)
            found = lax.dot_general(picks, samples, (((1,), (1,)), ((), ())), preferred_element_type=jnp.float32)
            found = jnp.concatenate([found, jnp.zeros((EDGE * blocks, LANES - lines), jnp.float32)], axis=1)
            mine += pltpu.roll(found, part * (LANES // 2), 1) if part else found
        edges.append(mine)
    for block in range(blocks):
        for date in range(per):
            for group in range(2):
                at = place_of(date, group * GROUP + 2 * HALO, per, date_rows)
                value = edges[date][block * EDGE : (block + 1) * EDGE]
                if chunk == LANES:
                    stage[at : at + EDGE, block * LANES : (block + 1) * LANES] = value
        if chunk == LANES:
            piece = stage[:, block * chunk : (block + 1) * chunk]
        else:
            piece = stage[:, block * chunk : (block + 1) * chunk]
            piece = jnp.concatenate([piece, jnp.zeros((per * date_rows, LANES - chunk), jnp.float32)], axis=1)
            row = iota((per * date_rows, LANES), 0)
            for date in range(per):
                for group in range(2):
                    at = place_of(date, group * GROUP + 2 * HALO, per, date_rows)
                    for k in range(EDGE):
                        value = edges[date][block * EDGE + k : block * EDGE + k + 1]
                        piece = jnp.where(row == at + k, value, piece)
        piece = piece.astype(jnp.bfloat16)
        send[block, pl.ds(pl.multiple_of(turn * edge_rows, 16), edge_rows), :] = piece[:edge_rows]
        send[block, pl.ds(pl.multiple_of((1 - turn) * edge_rows, 16), edge_rows), :] = piece[edge_rows : 2 * edge_rows]
        send[block, 2 * edge_rows :, :] = piece[2 * edge_rows :]


def weight_kernel(lines, chunk, az, tiled, weights):
    out_rows = lines // STEP
    cols = chunk // STEP
    wide = out_rows * cols
    depth = out_rows * 2 * LANES
    shape = (LANES, wide)
    col = iota(shape, 1) % cols
    out_row = iota(shape, 1) // cols
    box = jnp.abs(iota(shape, 0) - STEP * col - tiled[...]) <= REACH
    for o in range(out_rows):
        mine = (box & (out_row == o)).astype(jnp.bfloat16)
        weights[2 * o * LANES : (2 * o + 1) * LANES, :] = mine
        weights[(2 * o + 1) * LANES : (2 * o + 2) * LANES, :] = mine
    turn = iota(shape, 0) % (LANES // 2)
    line = jnp.where(turn < lines + HALO, turn + HALO, turn + HALO - LANES // 2)
    lower = jnp.zeros(shape, jnp.int32)
    for o in range(out_rows):
        lower = jnp.where(out_row == o, STEP * o + az[o], lower)
    window = (line >= lower) & (line <= lower + 2 * HALO)
    for side, edge_col in ((0, 0), (1, cols - 1)):
        mine = (window & (col == edge_col)).astype(jnp.bfloat16)
        for term in range(2):
            start = depth + (2 * side + term) * LANES
            weights[start : start + LANES, :] = mine


def to_sublanes(blocks, per, rows, first_row, date_stride, source, target):
    dates = blocks * per
    for block in range(blocks):
        for date in range(per):
            at = first_row + date * date_stride
            if not isinstance(at, int):
                at = pl.multiple_of(at, 8)
            value = source[block, pl.ds(at, rows), :].astype(jnp.float32)
            for row in range(0, rows, 8):
                target[pl.ds(row * dates + block * per + date, 8, stride=dates), :] = value[row : row + 8]


def spread_kernel(blocks, per, lines, recv, x):
    dates = blocks * per
    date_rows = rows_of_date(lines)
    edge_rows = per * GROUP
    turn = 1 - lax.axis_index("strip") % 2
    to_sublanes(blocks, per, GROUP, turn * edge_rows, GROUP, recv, x)
    to_sublanes(blocks, per, GROUP, (1 - turn) * edge_rows, GROUP, recv, x.at[GROUP * dates :])
    rest = date_rows - 2 * GROUP
    to_sublanes(blocks, per, rest, 2 * edge_rows, rest, recv, x.at[2 * GROUP * dates :])


def split(value):
    high = value.astype(jnp.bfloat16)
    return high, (value - high.astype(jnp.float32)).astype(jnp.bfloat16)


def pair_kernel(
    blocks, per, lines, chunk, group, x, paired, other, order, az, rg, weights, send, sums, halo, edges, turned, left, power
):
    dates = blocks * per
    out_rows = lines // STEP
    cols = chunk // STEP
    wide = out_rows * cols
    me = lax.axis_index("date")
    depth = out_rows * 2 * LANES

    odd = lax.axis_index("strip") % 2
    to_sublanes(blocks, per, GROUP, 0, GROUP, paired, halo.at[1 - odd])
    to_sublanes(blocks, per, GROUP, 0, GROUP, other, halo.at[odd])
    below, above = halo.at[0], halo.at[1]
    lane = iota((dates, LANES), 1)
    turn = lane % (LANES // 2)
    for k in range(EDGE):
        at = (2 * HALO + k) * dates
        lower_part = pltpu.roll(below[at : at + dates, :], lines, 1)
        upper_part = pltpu.roll(above[at : at + dates, :], lines, 1)
        value = jnp.where(turn < lines, x[at : at + dates, :], jnp.where(turn < lines + HALO, upper_part, lower_part))
        edges[k * dates : (k + 1) * dates, :] = value
        value = pltpu.roll(value, LANES // 2, 1)
        turned[k * dates : (k + 1) * dates, :] = jnp.where(lane < LANES // 2, value, -value)
    first = rg[me * cols]
    last = rg[me * cols + cols - 1]
    edge_on = (first <= 0, first <= 1, last >= 2, last >= 3)

    def where_line(part, line):
        if line < HALO:
            return below, part * HALO + line
        if line >= lines + HALO:
            return above, part * HALO + line - (lines + HALO)
        return x, row_of(part, line - HALO, lines)

    def one_date(first_date, step, carry):
        date = first_date + step
        target = (step // per * 2) * per + step % per
        for tile in range(dates // 16):

            def own(ref, row):
                return ref[pl.ds(row * dates + date, 1), :]

            def others(ref, row):
                return ref[row * dates + tile * 16 : row * dates + tile * 16 + 16, :]

            real, imag = [], []
            for line in range(lines + 2 * HALO):
                at_re, at_im = where_line(0, line), where_line(1, line)
                re_i, im_i = own(*at_re), own(*at_im)
                re_j, im_j = others(*at_re), others(*at_im)
                real.append(re_i * re_j + im_i * im_j)
                imag.append(im_i * re_j - re_i * im_j)
            for part, product in enumerate((real, imag)):
                start = pl.multiple_of((target + part * per) * dates + tile * 16, 16)
                at_rows = pl.ds(start, 16)
                quads = []
                for k in range(out_rows + 1):
                    q = product[STEP * k + 3 : STEP * k + 7]
                    quads.append((q[0] + q[1]) + (q[2] + q[3]))
                for o in range(out_rows):
                    total = quads[o] + quads[o + 1]
                    for k in range(3):
                        total += jnp.where(az[o] <= k, product[STEP * o + k], product[STEP * o + 11 + k])
                    upper, rest = split(total)
                    left[at_rows, 2 * o * LANES : (2 * o + 1) * LANES] = upper
                    left[at_rows, (2 * o + 1) * LANES : (2 * o + 2) * LANES] = rest
                for side in range(2):
                    total = jnp.zeros((16, LANES), jnp.float32)
                    for edge in (2 * side, 2 * side + 1):
                        mine = own(turned if part else edges, edge)
                        total += jnp.where(edge_on[edge], mine * others(edges, edge), 0.0)
                    upper, rest = split(total)
                    start_col = depth + 2 * side * LANES
                    left[at_rows, start_col : start_col + LANES] = upper
                    left[at_rows, start_col + LANES : start_col + 2 * LANES] = rest
        return carry

    for first_date in range(0, dates, group):
        lax.fori_loop(0, group, functools.partial(one_date, first_date), 0)
        found = jnp.dot(left[...], weights[...], preferred_element_type=jnp.float32)
        sums[first_date * 2 * dates : (first_date + group) * 2 * dates, :] = found
    for date in range(dates):
        at_row = (date // per * 2 * per + date % per) * dates + date
        power[date : date + 1, :] = sums[at_row : at_row + 1, :]
    scale = lax.rsqrt(power[...] + epsilon)
    power[...] = scale
    position = iota((dates, wide), 0)
    column = iota((dates, wide), 1)
    rank = jnp.zeros((dates, wide), jnp.int32)
    for block in range(blocks):
        rank = jnp.where(position // per == block, order[block] * per + position % per, rank)
    for date in range(dates):
        later = rank > order[date // per] * per + date % per
        factor = scale * power[date : date + 1, :]
        starts = [((date // per * 2 + part) * per + date % per) * dates for part in range(2)]
        values = [jnp.where(later, sums[start : start + dates, :] * factor, 0.0) for start in starts]
        largest = jnp.max(jnp.maximum(jnp.abs(values[0]), jnp.abs(values[1])), axis=1, keepdims=True)
        level = jnp.floor(jnp.log(largest) * (LEVELS / LOG_2)) + 1.0
        level = jnp.clip(level, LOWEST, HIGHEST)
        codes = [jnp.floor(value * (jnp.exp(level * (-LOG_2 / LEVELS)) * TOP) + 0.5) for value in values]
        header = jnp.sum(jnp.where(position == column, level, 0.0), axis=0, keepdims=True)
        codes[0] = jnp.where(position == date, header, codes[0])
        for start, code in zip(starts, codes):
            send[start : start + dates, :] = code.astype(jnp.int32).astype(jnp.int16)


def join_kernel(blocks, per, out_rows, cols, recv, out, halves, done):
    dates = blocks * per
    wide = out_rows * cols
    per_tile = LANES // cols
    me = lax.axis_index("date")
    lane = iota((dates, LANES), 1) // cols
    position = iota((dates, wide), 0)
    column = iota((dates, wide), 1)
    factors = [[None] * blocks for _ in range(per)]
    copies = []
    for step in range(2 * per):
        own = me * per + step % per
        values = []
        for block in range(blocks):
            codes = recv[block, step * dates : (step + 1) * dates, :].astype(jnp.int32).astype(jnp.float32)
            if step < per:
                header = jnp.sum(jnp.where(position == own, codes, 0.0), axis=0, keepdims=True)
                level = jnp.sum(jnp.where(position == column, header, 0.0), axis=1, keepdims=True)
                factors[step][block] = jnp.exp(level * (LOG_2 / LEVELS)) * (1.0 / TOP)
            values.append(jnp.where(position == own, 0.0, codes * factors[step % per][block]))
        for d_tile in range(blocks // per_tile):
            for o_tile in range(out_rows // per_tile):
                tiles = [
                    values[d_tile * per_tile + d][:, o_tile * LANES : (o_tile + 1) * LANES] for d in range(per_tile)
                ]
                width = 1
                while width < per_tile:
                    swap = [None] * per_tile
                    upper = (lane // width) % 2 == 1
                    shift = width * cols
                    for a in range(per_tile):
                        if (a // width) % 2 == 0:
                            b = a + width
                            swap[a] = jnp.where(upper, pltpu.roll(tiles[b], shift, 1), tiles[a])
                            swap[b] = jnp.where(upper, tiles[b], pltpu.roll(tiles[a], LANES - shift, 1))
                    tiles = swap
                    width *= 2
                for o in range(per_tile):
                    for start in range(0, dates, 8):
                        at = start * out_rows + o_tile * per_tile + o
                        halves[step, d_tile, pl.ds(at, 8, stride=out_rows), :] = tiles[o][start : start + 8]
            rows = slice(step * dates * out_rows, (step + 1) * dates * out_rows)
            target = out.at[rows, d_tile * LANES : (d_tile + 1) * LANES]
            copies.append(pltpu.make_async_copy(halves.at[step, d_tile], target, done.at[step, d_tile]))
            copies[-1].start()
    for copy in copies:
        copy.wait()


def decode(codes, me, per):
    values = codes.astype(jnp.float32)
    dates = codes.shape[3]
    own = (me * per + jnp.arange(per))[:, None] == jnp.arange(dates)[None]
    header = jnp.sum(jnp.where(own[None, :, :, None], values[:, 0], 0.0), axis=2)
    factor = jnp.exp(header[:, :, :dates] * (LOG_2 / LEVELS)) * (1.0 / TOP)
    return jnp.where(own[None, None, :, :, None], 0.0, values * factor[:, None, :, :, None])


def on_device(slc, block_order, az_offset, rg_offset):
    blocks = lax.axis_size("date")
    strips = lax.axis_size("strip")
    per, lines, span = slc.shape[1:]
    dates = blocks * per
    chunk = span // blocks
    out_rows = lines // STEP
    cols = chunk // STEP
    wide = out_rows * cols
    date_rows = rows_of_date(lines)
    depth = (out_rows + 2) * 2 * LANES
    group = max(per, 256 // dates)
    me = lax.axis_index("date")

    send = pl.pallas_call(
        functools.partial(pack_kernel, blocks, per, lines, chunk),
        out_shape=jax.ShapeDtypeStruct((blocks, per * date_rows, LANES), jnp.bfloat16),
        in_specs=[VMEM],
        out_specs=VMEM,
        scratch_shapes=[pltpu.VMEM((per * date_rows, span), jnp.float32)],
        compiler_params=PARAMS,
        name="pack",
    )(slc)
    recv = lax.all_to_all(send, "date", 0, 0, tiled=True)
    tiled = jnp.tile(lax.dynamic_slice_in_dim(rg_offset, me * cols, cols), out_rows)[None]
    weights = pl.pallas_call(
        functools.partial(weight_kernel, lines, chunk),
        out_shape=jax.ShapeDtypeStruct((depth, wide), jnp.bfloat16),
        in_specs=[SMEM, VMEM],
        out_specs=VMEM,
        compiler_params=PARAMS,
        cost_estimate=pl.CostEstimate(flops=0, bytes_accessed=4 * 1024 * 1024, transcendentals=0),
        name="weights",
    )(az_offset, tiled)

    recv, weights = lax.optimization_barrier((recv, weights))
    edge_rows = per * GROUP

    def swaps(first):
        pairs = [(i, i + 1) for i in range(first, strips - 1, 2)]
        return pairs + [(target, source) for source, target in pairs]

    paired = lax.ppermute(recv[:, :edge_rows], "strip", swaps(0))
    other = lax.ppermute(recv[:, edge_rows : 2 * edge_rows], "strip", swaps(1))
    x = pl.pallas_call(
        functools.partial(spread_kernel, blocks, per, lines),
        out_shape=jax.ShapeDtypeStruct((date_rows * dates, LANES), jnp.float32),
        in_specs=[VMEM],
        out_specs=VMEM,
        compiler_params=PARAMS,
        cost_estimate=pl.CostEstimate(flops=0, bytes_accessed=4 * 1024 * 1024, transcendentals=0),
        name="spread",
    )(recv)
    pairs = pl.pallas_call(
        functools.partial(pair_kernel, blocks, per, lines, chunk, group),
        out_shape=jax.ShapeDtypeStruct((dates * 2 * dates, wide), jnp.int16),
        in_specs=[VMEM, VMEM, VMEM, SMEM, SMEM, SMEM, VMEM],
        out_specs=VMEM,
        scratch_shapes=[
            pltpu.VMEM((dates * 2 * dates, wide), jnp.float32),
            pltpu.VMEM((2, GROUP * dates, LANES), jnp.float32),
            pltpu.VMEM((EDGE * dates, LANES), jnp.float32),
            pltpu.VMEM((EDGE * dates, LANES), jnp.float32),
            pltpu.VMEM((group * 2 * dates, depth), jnp.bfloat16),
            pltpu.VMEM((dates, wide), jnp.float32),
        ],
        compiler_params=PARAMS,
        name="pairs",
    )(x, paired, other, block_order, az_offset, rg_offset, weights)
    count = 2 * per * dates
    back = lax.all_to_all(pairs.reshape(blocks, count, wide), "date", 0, 0, tiled=True)
    if LANES % cols == 0 and out_rows * cols % LANES == 0 and blocks * cols % LANES == 0:
        out = pl.pallas_call(
            functools.partial(join_kernel, blocks, per, out_rows, cols),
            out_shape=jax.ShapeDtypeStruct((count * out_rows, blocks * cols), jnp.float32),
            in_specs=[VMEM],
            out_specs=pl.BlockSpec(memory_space=pl.ANY),
            scratch_shapes=[
                pltpu.VMEM((2 * per, blocks * cols // LANES, dates * out_rows, LANES), jnp.float32),
                pltpu.SemaphoreType.DMA((2 * per, blocks * cols // LANES)),
            ],
            compiler_params=PARAMS,
            name="join",
        )(back)
    else:
        values = decode(back.reshape(blocks, 2, per, dates, wide), me, per)
        out = values.reshape(blocks, count, out_rows, cols).transpose(1, 2, 0, 3)
    return out.reshape(2, per, dates, out_rows, blocks * cols)


def solution(mesh):
    placed = (P(None, "date", "strip", None), P(), P("strip"), P())
    return jax.shard_map(
        on_device,
        mesh=mesh,
        in_specs=placed,
        out_specs=P(None, "date", None, "strip", None),
        check_vma=False,
    )
```

```python
import functools

import jax
import jax.numpy as jnp
from jax import lax
from jax.experimental import pallas as pl
from jax.experimental.pallas import tpu as pltpu
from jax.sharding import PartitionSpec as P

STEP = 4
HALO = 5
REACH = 2
EDGE = 4
LANES = 128
GROUP = 16
VMEM = pl.BlockSpec(memory_space=pltpu.VMEM)
SMEM = pl.BlockSpec(memory_space=pltpu.SMEM)
PARAMS = pltpu.CompilerParams(vmem_limit_bytes=48 * 1024 * 1024)

epsilon = 1e-06
LEVELS = 8.0
LOWEST, HIGHEST = -880.0, 64.0
TOP = 32760.0
LOG_2 = 0.6931471805599453


def iota(shape, dim):
    return lax.broadcasted_iota(jnp.int32, shape, dim)


def row_of(part, line, lines):
    if line < HALO:
        return part * HALO + line
    if line >= lines - HALO:
        return GROUP + part * HALO + line - (lines - HALO)
    middle = part * (lines - 2 * HALO) + line - HALO
    spare = GROUP - 2 * HALO - EDGE
    if middle < spare:
        return 2 * HALO + EDGE + middle
    if middle < 2 * spare:
        return GROUP + 2 * HALO + EDGE + middle - spare
    return 2 * GROUP + middle - 2 * spare


def place_of(date, row, per, date_rows):
    if row < GROUP:
        return date * GROUP + row
    if row < 2 * GROUP:
        return (per + date - 1) * GROUP + row
    return 2 * per * GROUP + date * (date_rows - 2 * GROUP) + row - 2 * GROUP


def rows_of_date(lines):
    return 2 * GROUP + 2 * (lines - 2 * HALO) - 2 * (GROUP - 2 * HALO - EDGE)


def runs(part, lines):
    found = []
    for line in range(lines):
        row = row_of(part, line, lines)
        if line and row == row_of(part, line - 1, lines) + 1 and row % GROUP:
            found[-1][1] += 1
        else:
            found.append([line, 1])
    return found


def pack_kernel(blocks, per, lines, chunk, slc, send, stage):
    date_rows = rows_of_date(lines)
    edge_rows = per * GROUP
    turn = 1 - lax.axis_index("strip") % 2
    span = blocks * chunk
    shape = (EDGE * blocks, span)
    place = iota(shape, 0) % EDGE
    wanted = iota(shape, 0) // EDGE * chunk + jnp.where(place < REACH, place - REACH, place - REACH + chunk)
    picks = (iota(shape, 1) == wanted).astype(jnp.bfloat16)
    lane = iota((EDGE * blocks, LANES), 1)
    edges = []
    for date in range(per):
        mine = jnp.zeros((EDGE * blocks, LANES), jnp.float32)
        for part in range(2):
            samples = slc[part, date]
            for first, count in runs(part, lines):
                at = place_of(date, row_of(part, first, lines), per, date_rows)
                stage[at : at + count, :] = samples[first : first + count].astype(jnp.float32)
            found = lax.dot_general(picks, samples, (((1,), (1,)), ((), ())), preferred_element_type=jnp.float32)
            found = jnp.concatenate([found, jnp.zeros((EDGE * blocks, LANES - lines), jnp.float32)], axis=1)
            mine += pltpu.roll(found, part * (LANES // 2), 1) if part else found
        edges.append(mine)
    for block in range(blocks):
        for date in range(per):
            for group in range(2):
                at = place_of(date, group * GROUP + 2 * HALO, per, date_rows)
                value = edges[date][block * EDGE : (block + 1) * EDGE]
                if chunk == LANES:
                    stage[at : at + EDGE, block * LANES : (block + 1) * LANES] = value
        if chunk == LANES:
            piece = stage[:, block * chunk : (block + 1) * chunk]
        else:
            piece = stage[:, block * chunk : (block + 1) * chunk]
            piece = jnp.concatenate([piece, jnp.zeros((per * date_rows, LANES - chunk), jnp.float32)], axis=1)
            row = iota((per * date_rows, LANES), 0)
            for date in range(per):
                for group in range(2):
                    at = place_of(date, group * GROUP + 2 * HALO, per, date_rows)
                    for k in range(EDGE):
                        value = edges[date][block * EDGE + k : block * EDGE + k + 1]
                        piece = jnp.where(row == at + k, value, piece)
        piece = piece.astype(jnp.bfloat16)
        send[block, pl.ds(pl.multiple_of(turn * edge_rows, 16), edge_rows), :] = piece[:edge_rows]
        send[block, pl.ds(pl.multiple_of((1 - turn) * edge_rows, 16), edge_rows), :] = piece[edge_rows : 2 * edge_rows]
        send[block, 2 * edge_rows :, :] = piece[2 * edge_rows :]


def weight_kernel(lines, chunk, az, tiled, weights):
    out_rows = lines // STEP
    cols = chunk // STEP
    wide = out_rows * cols
    depth = out_rows * 2 * LANES
    shape = (LANES, wide)
    col = iota(shape, 1) % cols
    out_row = iota(shape, 1) // cols
    box = jnp.abs(iota(shape, 0) - STEP * col - tiled[...]) <= REACH
    for o in range(out_rows):
        mine = (box & (out_row == o)).astype(jnp.bfloat16)
        weights[2 * o * LANES : (2 * o + 1) * LANES, :] = mine
        weights[(2 * o + 1) * LANES : (2 * o + 2) * LANES, :] = mine
    turn = iota(shape, 0) % (LANES // 2)
    line = jnp.where(turn < lines + HALO, turn + HALO, turn + HALO - LANES // 2)
    lower = jnp.zeros(shape, jnp.int32)
    for o in range(out_rows):
        lower = jnp.where(out_row == o, STEP * o + az[o], lower)
    window = (line >= lower) & (line <= lower + 2 * HALO)
    for side, edge_col in ((0, 0), (1, cols - 1)):
        mine = (window & (col == edge_col)).astype(jnp.bfloat16)
        for term in range(2):
            start = depth + (2 * side + term) * LANES
            weights[start : start + LANES, :] = mine


def to_sublanes(blocks, per, rows, first_row, date_stride, source, target):
    dates = blocks * per
    for block in range(blocks):
        for date in range(per):
            at = first_row + date * date_stride
            if not isinstance(at, int):
                at = pl.multiple_of(at, 8)
            value = source[block, pl.ds(at, rows), :].astype(jnp.float32)
            for row in range(0, rows, 8):
                target[pl.ds(row * dates + block * per + date, 8, stride=dates), :] = value[row : row + 8]


def spread_kernel(blocks, per, lines, recv, x):
    dates = blocks * per
    date_rows = rows_of_date(lines)
    edge_rows = per * GROUP
    turn = 1 - lax.axis_index("strip") % 2
    to_sublanes(blocks, per, GROUP, turn * edge_rows, GROUP, recv, x)
    to_sublanes(blocks, per, GROUP, (1 - turn) * edge_rows, GROUP, recv, x.at[GROUP * dates :])
    rest = date_rows - 2 * GROUP
    to_sublanes(blocks, per, rest, 2 * edge_rows, rest, recv, x.at[2 * GROUP * dates :])


def split(value):
    high = value.astype(jnp.bfloat16)
    return high, (value - high.astype(jnp.float32)).astype(jnp.bfloat16)


def pair_kernel(
    blocks, per, lines, chunk, group, x, paired, other, order, az, rg, weights, send, sums, halo, edges, turned, left, power
):
    dates = blocks * per
    out_rows = lines // STEP
    cols = chunk // STEP
    wide = out_rows * cols
    me = lax.axis_index("date")
    depth = out_rows * 2 * LANES

    odd = lax.axis_index("strip") % 2
    to_sublanes(blocks, per, GROUP, 0, GROUP, paired, halo.at[1 - odd])
    to_sublanes(blocks, per, GROUP, 0, GROUP, other, halo.at[odd])
    below, above = halo.at[0], halo.at[1]
    lane = iota((dates, LANES), 1)
    turn = lane % (LANES // 2)
    for k in range(EDGE):
        at = (2 * HALO + k) * dates
        lower_part = pltpu.roll(below[at : at + dates, :], lines, 1)
        upper_part = pltpu.roll(above[at : at + dates, :], lines, 1)
        value = jnp.where(turn < lines, x[at : at + dates, :], jnp.where(turn < lines + HALO, upper_part, lower_part))
        edges[k * dates : (k + 1) * dates, :] = value
        value = pltpu.roll(value, LANES // 2, 1)
        turned[k * dates : (k + 1) * dates, :] = jnp.where(lane < LANES // 2, value, -value)
    first = rg[me * cols]
    last = rg[me * cols + cols - 1]
    edge_on = (first <= 0, first <= 1, last >= 2, last >= 3)

    def where_line(part, line):
        if line < HALO:
            return below, part * HALO + line
        if line >= lines + HALO:
            return above, part * HALO + line - (lines + HALO)
        return x, row_of(part, line - HALO, lines)

    def one_date(first_date, step, carry):
        date = first_date + step
        target = (step // per * 2) * per + step % per
        for tile in range(dates // 16):

            def own(ref, row):
                return ref[pl.ds(row * dates + date, 1), :]

            def others(ref, row):
                return ref[row * dates + tile * 16 : row * dates + tile * 16 + 16, :]

            real, imag = [], []
            for line in range(lines + 2 * HALO):
                at_re, at_im = where_line(0, line), where_line(1, line)
                re_i, im_i = own(*at_re), own(*at_im)
                re_j, im_j = others(*at_re), others(*at_im)
                real.append(re_i * re_j + im_i * im_j)
                imag.append(im_i * re_j - re_i * im_j)
            for part, product in enumerate((real, imag)):
                start = pl.multiple_of((target + part * per) * dates + tile * 16, 16)
                at_rows = pl.ds(start, 16)
                quads = []
                for k in range(out_rows + 1):
                    q = product[STEP * k + 3 : STEP * k + 7]
                    quads.append((q[0] + q[1]) + (q[2] + q[3]))
                for o in range(out_rows):
                    total = quads[o] + quads[o + 1]
                    for k in range(3):
                        total += jnp.where(az[o] <= k, product[STEP * o + k], product[STEP * o + 11 + k])
                    upper, rest = split(total)
                    left[at_rows, 2 * o * LANES : (2 * o + 1) * LANES] = upper
                    left[at_rows, (2 * o + 1) * LANES : (2 * o + 2) * LANES] = rest
                for side in range(2):
                    total = jnp.zeros((16, LANES), jnp.float32)
                    for edge in (2 * side, 2 * side + 1):
                        mine = own(turned if part else edges, edge)
                        total += jnp.where(edge_on[edge], mine * others(edges, edge), 0.0)
                    upper, rest = split(total)
                    start_col = depth + 2 * side * LANES
                    left[at_rows, start_col : start_col + LANES] = upper
                    left[at_rows, start_col + LANES : start_col + 2 * LANES] = rest
        return carry

    for first_date in range(0, dates, group):
        lax.fori_loop(0, group, functools.partial(one_date, first_date), 0)
        found = jnp.dot(left[...], weights[...], preferred_element_type=jnp.float32)
        sums[first_date * 2 * dates : (first_date + group) * 2 * dates, :] = found
    for date in range(dates):
        at_row = (date // per * 2 * per + date % per) * dates + date
        power[date : date + 1, :] = sums[at_row : at_row + 1, :]
    scale = lax.rsqrt(power[...] + epsilon)
    power[...] = scale
    position = iota((dates, wide), 0)
    column = iota((dates, wide), 1)
    rank = jnp.zeros((dates, wide), jnp.int32)
    for block in range(blocks):
        rank = jnp.where(position // per == block, order[block] * per + position % per, rank)
    for date in range(dates):
        later = rank > order[date // per] * per + date % per
        factor = scale * power[date : date + 1, :]
        starts = [((date // per * 2 + part) * per + date % per) * dates for part in range(2)]
        values = [jnp.where(later, sums[start : start + dates, :] * factor, 0.0) for start in starts]
        largest = jnp.max(jnp.maximum(jnp.abs(values[0]), jnp.abs(values[1])), axis=1, keepdims=True)
        level = jnp.floor(jnp.log(largest) * (LEVELS / LOG_2)) + 1.0
        level = jnp.clip(level, LOWEST, HIGHEST)
        codes = [jnp.floor(value * (jnp.exp(level * (-LOG_2 / LEVELS)) * TOP) + 0.5) for value in values]
        header = jnp.sum(jnp.where(position == column, level, 0.0), axis=0, keepdims=True)
        codes[0] = jnp.where(position == date, header, codes[0])
        for start, code in zip(starts, codes):
            send[start : start + dates, :] = code.astype(jnp.int32).astype(jnp.int16)


def join_kernel(blocks, per, out_rows, cols, recv, out, halves, done):
    dates = blocks * per
    wide = out_rows * cols
    per_tile = LANES // cols
    me = lax.axis_index("date")
    lane = iota((dates, LANES), 1) // cols
    position = iota((dates, wide), 0)
    column = iota((dates, wide), 1)
    factors = [[None] * blocks for _ in range(per)]
    copies = []
    for step in range(2 * per):
        own = me * per + step % per
        values = []
        for block in range(blocks):
            codes = recv[block, step * dates : (step + 1) * dates, :].astype(jnp.int32).astype(jnp.float32)
            if step < per:
                header = jnp.sum(jnp.where(position == own, codes, 0.0), axis=0, keepdims=True)
                level = jnp.sum(jnp.where(position == column, header, 0.0), axis=1, keepdims=True)
                factors[step][block] = jnp.exp(level * (LOG_2 / LEVELS)) * (1.0 / TOP)
            values.append(jnp.where(position == own, 0.0, codes * factors[step % per][block]))
        for d_tile in range(blocks // per_tile):
            for o_tile in range(out_rows // per_tile):
                tiles = [
                    values[d_tile * per_tile + d][:, o_tile * LANES : (o_tile + 1) * LANES] for d in range(per_tile)
                ]
                width = 1
                while width < per_tile:
                    swap = [None] * per_tile
                    upper = (lane // width) % 2 == 1
                    shift = width * cols
                    for a in range(per_tile):
                        if (a // width) % 2 == 0:
                            b = a + width
                            swap[a] = jnp.where(upper, pltpu.roll(tiles[b], shift, 1), tiles[a])
                            swap[b] = jnp.where(upper, tiles[b], pltpu.roll(tiles[a], LANES - shift, 1))
                    tiles = swap
                    width *= 2
                for o in range(per_tile):
                    for start in range(0, dates, 8):
                        at = start * out_rows + o_tile * per_tile + o
                        halves[step, d_tile, pl.ds(at, 8, stride=out_rows), :] = tiles[o][start : start + 8]
            rows = slice(step * dates * out_rows, (step + 1) * dates * out_rows)
            target = out.at[rows, d_tile * LANES : (d_tile + 1) * LANES]
            copies.append(pltpu.make_async_copy(halves.at[step, d_tile], target, done.at[step, d_tile]))
            copies[-1].start()
    for copy in copies:
        copy.wait()


def decode(codes, me, per):
    values = codes.astype(jnp.float32)
    dates = codes.shape[3]
    own = (me * per + jnp.arange(per))[:, None] == jnp.arange(dates)[None]
    header = jnp.sum(jnp.where(own[None, :, :, None], values[:, 0], 0.0), axis=2)
    factor = jnp.exp(header[:, :, :dates] * (LOG_2 / LEVELS)) * (1.0 / TOP)
    return jnp.where(own[None, None, :, :, None], 0.0, values * factor[:, None, :, :, None])


def on_device(slc, block_order, az_offset, rg_offset):
    blocks = lax.axis_size("date")
    strips = lax.axis_size("strip")
    per, lines, span = slc.shape[1:]
    dates = blocks * per
    chunk = span // blocks
    out_rows = lines // STEP
    cols = chunk // STEP
    wide = out_rows * cols
    date_rows = rows_of_date(lines)
    depth = (out_rows + 2) * 2 * LANES
    group = max(per, 256 // dates)
    me = lax.axis_index("date")

    send = pl.pallas_call(
        functools.partial(pack_kernel, blocks, per, lines, chunk),
        out_shape=jax.ShapeDtypeStruct((blocks, per * date_rows, LANES), jnp.bfloat16),
        in_specs=[VMEM],
        out_specs=VMEM,
        scratch_shapes=[pltpu.VMEM((per * date_rows, span), jnp.float32)],
        compiler_params=PARAMS,
        name="pack",
    )(slc)
    recv = lax.all_to_all(send, "date", 0, 0, tiled=True)
    tiled = jnp.tile(lax.dynamic_slice_in_dim(rg_offset, me * cols, cols), out_rows)[None]
    weights = pl.pallas_call(
        functools.partial(weight_kernel, lines, chunk),
        out_shape=jax.ShapeDtypeStruct((depth, wide), jnp.bfloat16),
        in_specs=[SMEM, VMEM],
        out_specs=VMEM,
        compiler_params=PARAMS,
        cost_estimate=pl.CostEstimate(flops=0, bytes_accessed=4 * 1024 * 1024, transcendentals=0),
        name="weights",
    )(az_offset, tiled)

    edge_rows = per * GROUP

    def swaps(first):
        pairs = [(i, i + 1) for i in range(first, strips - 1, 2)]
        return pairs + [(target, source) for source, target in pairs]

    other = lax.ppermute(recv[:, edge_rows : 2 * edge_rows], "strip", swaps(1))
    paired = lax.ppermute(recv[:, :edge_rows], "strip", swaps(0))
    x = pl.pallas_call(
        functools.partial(spread_kernel, blocks, per, lines),
        out_shape=jax.ShapeDtypeStruct((date_rows * dates, LANES), jnp.float32),
        in_specs=[VMEM],
        out_specs=VMEM,
        compiler_params=PARAMS,
        cost_estimate=pl.CostEstimate(flops=0, bytes_accessed=4 * 1024 * 1024, transcendentals=0),
        name="spread",
    )(recv)
    pairs = pl.pallas_call(
        functools.partial(pair_kernel, blocks, per, lines, chunk, group),
        out_shape=jax.ShapeDtypeStruct((dates * 2 * dates, wide), jnp.int16),
        in_specs=[VMEM, VMEM, VMEM, SMEM, SMEM, SMEM, VMEM],
        out_specs=VMEM,
        scratch_shapes=[
            pltpu.VMEM((dates * 2 * dates, wide), jnp.float32),
            pltpu.VMEM((2, GROUP * dates, LANES), jnp.float32),
            pltpu.VMEM((EDGE * dates, LANES), jnp.float32),
            pltpu.VMEM((EDGE * dates, LANES), jnp.float32),
            pltpu.VMEM((group * 2 * dates, depth), jnp.bfloat16),
            pltpu.VMEM((dates, wide), jnp.float32),
        ],
        compiler_params=PARAMS,
        name="pairs",
    )(x, paired, other, block_order, az_offset, rg_offset, weights)
    count = 2 * per * dates
    back = lax.all_to_all(pairs.reshape(blocks, count, wide), "date", 0, 0, tiled=True)
    if LANES % cols == 0 and out_rows * cols % LANES == 0 and blocks * cols % LANES == 0:
        out = pl.pallas_call(
            functools.partial(join_kernel, blocks, per, out_rows, cols),
            out_shape=jax.ShapeDtypeStruct((count * out_rows, blocks * cols), jnp.float32),
            in_specs=[VMEM],
            out_specs=pl.BlockSpec(memory_space=pl.ANY),
            scratch_shapes=[
                pltpu.VMEM((2 * per, blocks * cols // LANES, dates * out_rows, LANES), jnp.float32),
                pltpu.SemaphoreType.DMA((2 * per, blocks * cols // LANES)),
            ],
            compiler_params=PARAMS,
            name="join",
        )(back)
    else:
        values = decode(back.reshape(blocks, 2, per, dates, wide), me, per)
        out = values.reshape(blocks, count, out_rows, cols).transpose(1, 2, 0, 3)
    return out.reshape(2, per, dates, out_rows, blocks * cols)


def solution(mesh):
    placed = (P(None, "date", "strip", None), P(), P("strip"), P())
    return jax.shard_map(
        on_device,
        mesh=mesh,
        in_specs=placed,
        out_specs=P(None, "date", None, "strip", None),
        check_vma=False,
    )
```

```python
import functools

import jax
import jax.numpy as jnp
from jax import lax
from jax.experimental import pallas as pl
from jax.experimental.pallas import tpu as pltpu
from jax.sharding import PartitionSpec as P

STEP = 4
HALO = 5
REACH = 2
EDGE = 4
LANES = 128
GROUP = 16
VMEM = pl.BlockSpec(memory_space=pltpu.VMEM)
SMEM = pl.BlockSpec(memory_space=pltpu.SMEM)
PARAMS = pltpu.CompilerParams(vmem_limit_bytes=48 * 1024 * 1024)

epsilon = 1e-06
LEVELS = 8.0
LOWEST, HIGHEST = -880.0, 64.0
TOP = 32760.0
LOG_2 = 0.6931471805599453


def iota(shape, dim):
    return lax.broadcasted_iota(jnp.int32, shape, dim)


def row_of(part, line, lines):
    if line < HALO:
        return part * HALO + line
    if line >= lines - HALO:
        return GROUP + part * HALO + line - (lines - HALO)
    middle = part * (lines - 2 * HALO) + line - HALO
    spare = GROUP - 2 * HALO - EDGE
    if middle < spare:
        return 2 * HALO + EDGE + middle
    if middle < 2 * spare:
        return GROUP + 2 * HALO + EDGE + middle - spare
    return 2 * GROUP + middle - 2 * spare


def place_of(date, row, per, date_rows):
    if row < GROUP:
        return date * GROUP + row
    if row < 2 * GROUP:
        return (per + date - 1) * GROUP + row
    return 2 * per * GROUP + date * (date_rows - 2 * GROUP) + row - 2 * GROUP


def rows_of_date(lines):
    return 2 * GROUP + 2 * (lines - 2 * HALO) - 2 * (GROUP - 2 * HALO - EDGE)


def runs(part, lines):
    found = []
    for line in range(lines):
        row = row_of(part, line, lines)
        if line and row == row_of(part, line - 1, lines) + 1 and row % GROUP:
            found[-1][1] += 1
        else:
            found.append([line, 1])
    return found


def pack_kernel(blocks, per, lines, chunk, slc, send, stage):
    date_rows = rows_of_date(lines)
    edge_rows = per * GROUP
    turn = 1 - lax.axis_index("strip") % 2
    span = blocks * chunk
    shape = (EDGE * blocks, span)
    place = iota(shape, 0) % EDGE
    wanted = iota(shape, 0) // EDGE * chunk + jnp.where(place < REACH, place - REACH, place - REACH + chunk)
    picks = (iota(shape, 1) == wanted).astype(jnp.bfloat16)
    lane = iota((EDGE * blocks, LANES), 1)
    edges = []
    for date in range(per):
        mine = jnp.zeros((EDGE * blocks, LANES), jnp.float32)
        for part in range(2):
            samples = slc[part, date]
            for first, count in runs(part, lines):
                at = place_of(date, row_of(part, first, lines), per, date_rows)
                stage[at : at + count, :] = samples[first : first + count].astype(jnp.float32)
            found = lax.dot_general(picks, samples, (((1,), (1,)), ((), ())), preferred_element_type=jnp.float32)
            found = jnp.concatenate([found, jnp.zeros((EDGE * blocks, LANES - lines), jnp.float32)], axis=1)
            mine += pltpu.roll(found, part * (LANES // 2), 1) if part else found
        edges.append(mine)
    for block in range(blocks):
        for date in range(per):
            for group in range(2):
                at = place_of(date, group * GROUP + 2 * HALO, per, date_rows)
                value = edges[date][block * EDGE : (block + 1) * EDGE]
                if chunk == LANES:
                    stage[at : at + EDGE, block * LANES : (block + 1) * LANES] = value
        if chunk == LANES:
            piece = stage[:, block * chunk : (block + 1) * chunk]
        else:
            piece = stage[:, block * chunk : (block + 1) * chunk]
            piece = jnp.concatenate([piece, jnp.zeros((per * date_rows, LANES - chunk), jnp.float32)], axis=1)
            row = iota((per * date_rows, LANES), 0)
            for date in range(per):
                for group in range(2):
                    at = place_of(date, group * GROUP + 2 * HALO, per, date_rows)
                    for k in range(EDGE):
                        value = edges[date][block * EDGE + k : block * EDGE + k + 1]
                        piece = jnp.where(row == at + k, value, piece)
        piece = piece.astype(jnp.bfloat16)
        send[block, pl.ds(pl.multiple_of(turn * edge_rows, 16), edge_rows), :] = piece[:edge_rows]
        send[block, pl.ds(pl.multiple_of((1 - turn) * edge_rows, 16), edge_rows), :] = piece[edge_rows : 2 * edge_rows]
        send[block, 2 * edge_rows :, :] = piece[2 * edge_rows :]


def weight_kernel(lines, chunk, az, tiled, weights):
    out_rows = lines // STEP
    cols = chunk // STEP
    wide = out_rows * cols
    depth = out_rows * 2 * LANES
    shape = (LANES, wide)
    col = iota(shape, 1) % cols
    out_row = iota(shape, 1) // cols
    box = jnp.abs(iota(shape, 0) - STEP * col - tiled[...]) <= REACH
    for o in range(out_rows):
        mine = (box & (out_row == o)).astype(jnp.bfloat16)
        weights[2 * o * LANES : (2 * o + 1) * LANES, :] = mine
        weights[(2 * o + 1) * LANES : (2 * o + 2) * LANES, :] = mine
    turn = iota(shape, 0) % (LANES // 2)
    line = jnp.where(turn < lines + HALO, turn + HALO, turn + HALO - LANES // 2)
    lower = jnp.zeros(shape, jnp.int32)
    for o in range(out_rows):
        lower = jnp.where(out_row == o, STEP * o + az[o], lower)
    window = (line >= lower) & (line <= lower + 2 * HALO)
    for side, edge_col in ((0, 0), (1, cols - 1)):
        mine = (window & (col == edge_col)).astype(jnp.bfloat16)
        for term in range(2):
            start = depth + (2 * side + term) * LANES
            weights[start : start + LANES, :] = mine


def to_sublanes(blocks, per, rows, first_row, date_stride, source, target):
    dates = blocks * per
    for block in range(blocks):
        for date in range(per):
            at = first_row + date * date_stride
            if not isinstance(at, int):
                at = pl.multiple_of(at, 8)
            value = source[block, pl.ds(at, rows), :].astype(jnp.float32)
            for row in range(0, rows, 8):
                target[pl.ds(row * dates + block * per + date, 8, stride=dates), :] = value[row : row + 8]


def spread_kernel(blocks, per, lines, recv, x):
    dates = blocks * per
    date_rows = rows_of_date(lines)
    edge_rows = per * GROUP
    turn = 1 - lax.axis_index("strip") % 2
    to_sublanes(blocks, per, GROUP, turn * edge_rows, GROUP, recv, x)
    to_sublanes(blocks, per, GROUP, (1 - turn) * edge_rows, GROUP, recv, x.at[GROUP * dates :])
    rest = date_rows - 2 * GROUP
    to_sublanes(blocks, per, rest, 2 * edge_rows, rest, recv, x.at[2 * GROUP * dates :])


def split(value):
    high = value.astype(jnp.bfloat16)
    return high, (value - high.astype(jnp.float32)).astype(jnp.bfloat16)


def pair_kernel(
    blocks, per, lines, chunk, group, x, other, paired, order, az, rg, weights, send, sums, halo, edges, turned, left, power
):
    dates = blocks * per
    out_rows = lines // STEP
    cols = chunk // STEP
    wide = out_rows * cols
    me = lax.axis_index("date")
    depth = out_rows * 2 * LANES

    odd = lax.axis_index("strip") % 2
    to_sublanes(blocks, per, GROUP, 0, GROUP, paired, halo.at[1 - odd])
    to_sublanes(blocks, per, GROUP, 0, GROUP, other, halo.at[odd])
    below, above = halo.at[0], halo.at[1]
    lane = iota((dates, LANES), 1)
    turn = lane % (LANES // 2)
    for k in range(EDGE):
        at = (2 * HALO + k) * dates
        lower_part = pltpu.roll(below[at : at + dates, :], lines, 1)
        upper_part = pltpu.roll(above[at : at + dates, :], lines, 1)
        value = jnp.where(turn < lines, x[at : at + dates, :], jnp.where(turn < lines + HALO, upper_part, lower_part))
        edges[k * dates : (k + 1) * dates, :] = value
        value = pltpu.roll(value, LANES // 2, 1)
        turned[k * dates : (k + 1) * dates, :] = jnp.where(lane < LANES // 2, value, -value)
    first = rg[me * cols]
    last = rg[me * cols + cols - 1]
    edge_on = (first <= 0, first <= 1, last >= 2, last >= 3)

    def where_line(part, line):
        if line < HALO:
            return below, part * HALO + line
        if line >= lines + HALO:
            return above, part * HALO + line - (lines + HALO)
        return x, row_of(part, line - HALO, lines)

    def one_date(first_date, step, carry):
        date = first_date + step
        target = (step // per * 2) * per + step % per
        for tile in range(dates // 16):

            def own(ref, row):
                return ref[pl.ds(row * dates + date, 1), :]

            def others(ref, row):
                return ref[row * dates + tile * 16 : row * dates + tile * 16 + 16, :]

            real, imag = [], []
            for line in range(lines + 2 * HALO):
                at_re, at_im = where_line(0, line), where_line(1, line)
                re_i, im_i = own(*at_re), own(*at_im)
                re_j, im_j = others(*at_re), others(*at_im)
                real.append(re_i * re_j + im_i * im_j)
                imag.append(im_i * re_j - re_i * im_j)
            for part, product in enumerate((real, imag)):
                start = pl.multiple_of((target + part * per) * dates + tile * 16, 16)
                at_rows = pl.ds(start, 16)
                quads = []
                for k in range(out_rows + 1):
                    q = product[STEP * k + 3 : STEP * k + 7]
                    quads.append((q[0] + q[1]) + (q[2] + q[3]))
                for o in range(out_rows):
                    total = quads[o] + quads[o + 1]
                    for k in range(3):
                        total += jnp.where(az[o] <= k, product[STEP * o + k], product[STEP * o + 11 + k])
                    upper, rest = split(total)
                    left[at_rows, 2 * o * LANES : (2 * o + 1) * LANES] = upper
                    left[at_rows, (2 * o + 1) * LANES : (2 * o + 2) * LANES] = rest
                for side in range(2):
                    total = jnp.zeros((16, LANES), jnp.float32)
                    for edge in (2 * side, 2 * side + 1):
                        mine = own(turned if part else edges, edge)
                        total += jnp.where(edge_on[edge], mine * others(edges, edge), 0.0)
                    upper, rest = split(total)
                    start_col = depth + 2 * side * LANES
                    left[at_rows, start_col : start_col + LANES] = upper
                    left[at_rows, start_col + LANES : start_col + 2 * LANES] = rest
        return carry

    for first_date in range(0, dates, group):
        lax.fori_loop(0, group, functools.partial(one_date, first_date), 0)
        found = jnp.dot(left[...], weights[...], preferred_element_type=jnp.float32)
        sums[first_date * 2 * dates : (first_date + group) * 2 * dates, :] = found
    for date in range(dates):
        at_row = (date // per * 2 * per + date % per) * dates + date
        power[date : date + 1, :] = sums[at_row : at_row + 1, :]
    scale = lax.rsqrt(power[...] + epsilon)
    power[...] = scale
    position = iota((dates, wide), 0)
    column = iota((dates, wide), 1)
    rank = jnp.zeros((dates, wide), jnp.int32)
    for block in range(blocks):
        rank = jnp.where(position // per == block, order[block] * per + position % per, rank)
    for date in range(dates):
        later = rank > order[date // per] * per + date % per
        factor = scale * power[date : date + 1, :]
        starts = [((date // per * 2 + part) * per + date % per) * dates for part in range(2)]
        values = [jnp.where(later, sums[start : start + dates, :] * factor, 0.0) for start in starts]
        largest = jnp.max(jnp.maximum(jnp.abs(values[0]), jnp.abs(values[1])), axis=1, keepdims=True)
        level = jnp.floor(jnp.log(largest) * (LEVELS / LOG_2)) + 1.0
        level = jnp.clip(level, LOWEST, HIGHEST)
        codes = [jnp.floor(value * (jnp.exp(level * (-LOG_2 / LEVELS)) * TOP) + 0.5) for value in values]
        header = jnp.sum(jnp.where(position == column, level, 0.0), axis=0, keepdims=True)
        codes[0] = jnp.where(position == date, header, codes[0])
        for start, code in zip(starts, codes):
            send[start : start + dates, :] = code.astype(jnp.int32).astype(jnp.int16)


def join_kernel(blocks, per, out_rows, cols, recv, out, halves, done):
    dates = blocks * per
    wide = out_rows * cols
    per_tile = LANES // cols
    me = lax.axis_index("date")
    lane = iota((dates, LANES), 1) // cols
    position = iota((dates, wide), 0)
    column = iota((dates, wide), 1)
    factors = [[None] * blocks for _ in range(per)]
    copies = []
    for step in range(2 * per):
        own = me * per + step % per
        values = []
        for block in range(blocks):
            codes = recv[block, step * dates : (step + 1) * dates, :].astype(jnp.int32).astype(jnp.float32)
            if step < per:
                header = jnp.sum(jnp.where(position == own, codes, 0.0), axis=0, keepdims=True)
                level = jnp.sum(jnp.where(position == column, header, 0.0), axis=1, keepdims=True)
                factors[step][block] = jnp.exp(level * (LOG_2 / LEVELS)) * (1.0 / TOP)
            values.append(jnp.where(position == own, 0.0, codes * factors[step % per][block]))
        for d_tile in range(blocks // per_tile):
            for o_tile in range(out_rows // per_tile):
                tiles = [
                    values[d_tile * per_tile + d][:, o_tile * LANES : (o_tile + 1) * LANES] for d in range(per_tile)
                ]
                width = 1
                while width < per_tile:
                    swap = [None] * per_tile
                    upper = (lane // width) % 2 == 1
                    shift = width * cols
                    for a in range(per_tile):
                        if (a // width) % 2 == 0:
                            b = a + width
                            swap[a] = jnp.where(upper, pltpu.roll(tiles[b], shift, 1), tiles[a])
                            swap[b] = jnp.where(upper, tiles[b], pltpu.roll(tiles[a], LANES - shift, 1))
                    tiles = swap
                    width *= 2
                for o in range(per_tile):
                    for start in range(0, dates, 8):
                        at = start * out_rows + o_tile * per_tile + o
                        halves[step, d_tile, pl.ds(at, 8, stride=out_rows), :] = tiles[o][start : start + 8]
            rows = slice(step * dates * out_rows, (step + 1) * dates * out_rows)
            target = out.at[rows, d_tile * LANES : (d_tile + 1) * LANES]
            copies.append(pltpu.make_async_copy(halves.at[step, d_tile], target, done.at[step, d_tile]))
            copies[-1].start()
    for copy in copies:
        copy.wait()


def decode(codes, me, per):
    values = codes.astype(jnp.float32)
    dates = codes.shape[3]
    own = (me * per + jnp.arange(per))[:, None] == jnp.arange(dates)[None]
    header = jnp.sum(jnp.where(own[None, :, :, None], values[:, 0], 0.0), axis=2)
    factor = jnp.exp(header[:, :, :dates] * (LOG_2 / LEVELS)) * (1.0 / TOP)
    return jnp.where(own[None, None, :, :, None], 0.0, values * factor[:, None, :, :, None])


def on_device(slc, block_order, az_offset, rg_offset):
    blocks = lax.axis_size("date")
    strips = lax.axis_size("strip")
    per, lines, span = slc.shape[1:]
    dates = blocks * per
    chunk = span // blocks
    out_rows = lines // STEP
    cols = chunk // STEP
    wide = out_rows * cols
    date_rows = rows_of_date(lines)
    depth = (out_rows + 2) * 2 * LANES
    group = max(per, 256 // dates)
    me = lax.axis_index("date")

    send = pl.pallas_call(
        functools.partial(pack_kernel, blocks, per, lines, chunk),
        out_shape=jax.ShapeDtypeStruct((blocks, per * date_rows, LANES), jnp.bfloat16),
        in_specs=[VMEM],
        out_specs=VMEM,
        scratch_shapes=[pltpu.VMEM((per * date_rows, span), jnp.float32)],
        compiler_params=PARAMS,
        name="pack",
    )(slc)
    recv = lax.all_to_all(send, "date", 0, 0, tiled=True)
    tiled = jnp.tile(lax.dynamic_slice_in_dim(rg_offset, me * cols, cols), out_rows)[None]
    weights = pl.pallas_call(
        functools.partial(weight_kernel, lines, chunk),
        out_shape=jax.ShapeDtypeStruct((depth, wide), jnp.bfloat16),
        in_specs=[SMEM, VMEM],
        out_specs=VMEM,
        compiler_params=PARAMS,
        cost_estimate=pl.CostEstimate(flops=0, bytes_accessed=4 * 1024 * 1024, transcendentals=0),
        name="weights",
    )(az_offset, tiled)

    edge_rows = per * GROUP

    def swaps(first):
        pairs = [(i, i + 1) for i in range(first, strips - 1, 2)]
        return pairs + [(target, source) for source, target in pairs]

    other = lax.ppermute(recv[:, edge_rows : 2 * edge_rows], "strip", swaps(1))
    paired = lax.ppermute(recv[:, :edge_rows], "strip", swaps(0))
    x = pl.pallas_call(
        functools.partial(spread_kernel, blocks, per, lines),
        out_shape=jax.ShapeDtypeStruct((date_rows * dates, LANES), jnp.float32),
        in_specs=[VMEM],
        out_specs=VMEM,
        compiler_params=PARAMS,
        cost_estimate=pl.CostEstimate(flops=0, bytes_accessed=4 * 1024 * 1024, transcendentals=0),
        name="spread",
    )(recv)
    pairs = pl.pallas_call(
        functools.partial(pair_kernel, blocks, per, lines, chunk, group),
        out_shape=jax.ShapeDtypeStruct((dates * 2 * dates, wide), jnp.int16),
        in_specs=[VMEM, VMEM, VMEM, SMEM, SMEM, SMEM, VMEM],
        out_specs=VMEM,
        scratch_shapes=[
            pltpu.VMEM((dates * 2 * dates, wide), jnp.float32),
            pltpu.VMEM((2, GROUP * dates, LANES), jnp.float32),
            pltpu.VMEM((EDGE * dates, LANES), jnp.float32),
            pltpu.VMEM((EDGE * dates, LANES), jnp.float32),
            pltpu.VMEM((group * 2 * dates, depth), jnp.bfloat16),
            pltpu.VMEM((dates, wide), jnp.float32),
        ],
        compiler_params=PARAMS,
        name="pairs",
    )(x, other, paired, block_order, az_offset, rg_offset, weights)
    count = 2 * per * dates
    back = lax.all_to_all(pairs.reshape(blocks, count, wide), "date", 0, 0, tiled=True)
    if LANES % cols == 0 and out_rows * cols % LANES == 0 and blocks * cols % LANES == 0:
        out = pl.pallas_call(
            functools.partial(join_kernel, blocks, per, out_rows, cols),
            out_shape=jax.ShapeDtypeStruct((count * out_rows, blocks * cols), jnp.float32),
            in_specs=[VMEM],
            out_specs=pl.BlockSpec(memory_space=pl.ANY),
            scratch_shapes=[
                pltpu.VMEM((2 * per, blocks * cols // LANES, dates * out_rows, LANES), jnp.float32),
                pltpu.SemaphoreType.DMA((2 * per, blocks * cols // LANES)),
            ],
            compiler_params=PARAMS,
            name="join",
        )(back)
    else:
        values = decode(back.reshape(blocks, 2, per, dates, wide), me, per)
        out = values.reshape(blocks, count, out_rows, cols).transpose(1, 2, 0, 3)
    return out.reshape(2, per, dates, out_rows, blocks * cols)


def solution(mesh):
    placed = (P(None, "date", "strip", None), P(), P("strip"), P())
    return jax.shard_map(
        on_device,
        mesh=mesh,
        in_specs=placed,
        out_specs=P(None, "date", None, "strip", None),
        check_vma=False,
    )
```

```python
import functools

import jax
import jax.numpy as jnp
from jax import lax
from jax.experimental import pallas as pl
from jax.experimental.pallas import tpu as pltpu
from jax.sharding import PartitionSpec as P

STEP = 4
HALO = 5
REACH = 2
EDGE = 4
LANES = 128
VMEM = pl.BlockSpec(memory_space=pltpu.VMEM)
SMEM = pl.BlockSpec(memory_space=pltpu.SMEM)
PARAMS = pltpu.CompilerParams(vmem_limit_bytes=48 * 1024 * 1024)

epsilon = 1e-06
LEVELS = 8.0
LOWEST, HIGHEST = -880.0, 64.0
TOP = 32760.0
LOG_2 = 0.6931471805599453


def iota(shape, dim):
    return lax.broadcasted_iota(jnp.int32, shape, dim)


def row_of(part, line, lines):
    if line < HALO:
        return 2 * lines + part * 2 * HALO + line
    if line < HALO + lines:
        return part * lines + line - HALO
    return 2 * lines + part * 2 * HALO + line - lines


def pack_kernel(blocks, per, lines, chunk, slc, other, paired, send, stage, piece):
    rows = 2 * (lines + 2 * HALO)
    date_rows = rows + EDGE
    span = blocks * chunk
    odd = lax.axis_index("strip") % 2 == 1
    for date in range(per):
        base = date * date_rows
        for part in range(2):
            with_pair, with_other = paired[part, date].astype(jnp.float32), other[part, date].astype(jnp.float32)
            edge = base + 2 * lines + part * 2 * HALO
            stage[base + part * lines : base + (part + 1) * lines, :] = slc[part, date].astype(jnp.float32)
            stage[edge : edge + HALO, :] = jnp.where(odd, with_pair, with_other)
            stage[edge + HALO : edge + 2 * HALO, :] = jnp.where(odd, with_other, with_pair)
        stage[base + rows : base + date_rows, :] = jnp.zeros((EDGE, span), jnp.float32)
    samples = stage[...].astype(jnp.bfloat16)
    shape = (EDGE * blocks, span)
    place = iota(shape, 0) % EDGE
    wanted = iota(shape, 0) // EDGE * chunk + jnp.where(place < REACH, place - REACH, place - REACH + chunk)
    picks = (iota(shape, 1) == wanted).astype(jnp.bfloat16)
    edges = lax.dot_general(picks, samples, (((1,), (1,)), ((), ())), preferred_element_type=jnp.float32)
    for block in range(blocks):
        if chunk == LANES:
            piece[...] = stage[:, block * chunk : (block + 1) * chunk]
        else:
            piece[...] = jnp.zeros(piece.shape, jnp.float32)
            piece[:, :chunk] = stage[:, block * chunk : (block + 1) * chunk]
        for date in range(per):
            base = date * date_rows
            mine = edges[block * EDGE : (block + 1) * EDGE, base : base + date_rows]
            piece[base + rows : base + date_rows, :] = jnp.zeros((EDGE, LANES), jnp.float32)
            piece[base + rows : base + date_rows, :date_rows] = mine
        send[block] = piece[...].astype(jnp.bfloat16)


def weight_kernel(lines, chunk, az, tiled, weights):
    out_rows = lines // STEP
    cols = chunk // STEP
    wide = out_rows * cols
    depth = out_rows * 2 * LANES
    shape = (LANES, wide)
    col = iota(shape, 1) % cols
    out_row = iota(shape, 1) // cols
    box = jnp.abs(iota(shape, 0) - STEP * col - tiled[...]) <= REACH
    for o in range(out_rows):
        mine = (box & (out_row == o)).astype(jnp.bfloat16)
        weights[2 * o * LANES : (2 * o + 1) * LANES, :] = mine
        weights[(2 * o + 1) * LANES : (2 * o + 2) * LANES, :] = mine
    rows = 2 * (lines + 2 * HALO)
    at = iota(shape, 0)
    turn = (at - 2 * lines) % (2 * HALO)
    line = jnp.where(at < 2 * lines, at % lines + HALO, jnp.where(turn < HALO, turn, turn + lines))
    line = jnp.where(at < rows, line, -100)
    lower = jnp.zeros(shape, jnp.int32)
    for o in range(out_rows):
        lower = jnp.where(out_row == o, STEP * o + az[o], lower)
    window = (line >= lower) & (line <= lower + 2 * HALO)
    for side, edge_col in ((0, 0), (1, cols - 1)):
        mine = (window & (col == edge_col)).astype(jnp.bfloat16)
        for term in range(2):
            start = depth + (2 * side + term) * LANES
            weights[start : start + LANES, :] = mine


def spread_kernel(blocks, per, date_rows, recv, x):
    dates = blocks * per
    for block in range(blocks):
        value = recv[block].astype(jnp.float32)
        for date in range(per):
            for row in range(0, date_rows, 8):
                part = value[date * date_rows + row : date * date_rows + row + 8]
                x[pl.ds(row * dates + block * per + date, 8, stride=dates), :] = part


def split(value):
    high = value.astype(jnp.bfloat16)
    return high, (value - high.astype(jnp.float32)).astype(jnp.bfloat16)


def pair_kernel(blocks, per, lines, chunk, group, x, order, az, rg, weights, send, sums, turned, left, power):
    dates = blocks * per
    out_rows = lines // STEP
    cols = chunk // STEP
    wide = out_rows * cols
    rows = 2 * (lines + 2 * HALO)
    me = lax.axis_index("date")
    depth = out_rows * 2 * LANES

    lane = iota((dates, LANES), 1)
    real = (lane < lines) | ((lane >= 2 * lines) & (lane < 2 * lines + 2 * HALO))
    for edge in range(EDGE):
        value = x[(rows + edge) * dates : (rows + edge + 1) * dates, :]
        up = jnp.where(lane < lines, pltpu.roll(value, LANES - lines, 1), pltpu.roll(value, LANES - 2 * HALO, 1))
        down = jnp.where(lane < 2 * lines, pltpu.roll(value, lines, 1), pltpu.roll(value, 2 * HALO, 1))
        turned[edge * dates : (edge + 1) * dates, :] = jnp.where(real, up, -down)
    first = rg[me * cols]
    last = rg[me * cols + cols - 1]
    edge_on = (first <= 0, first <= 1, last >= 2, last >= 3)

    def one_date(first_date, step, carry):
        date = first_date + step
        target = (step // per * 2) * per + step % per
        for tile in range(dates // 16):

            def own(row, ref=x):
                return ref[pl.ds(row * dates + date, 1), :]

            def others(row):
                return x[row * dates + tile * 16 : row * dates + tile * 16 + 16, :]

            real, imag = [], []
            for line in range(lines + 2 * HALO):
                at_re, at_im = row_of(0, line, lines), row_of(1, line, lines)
                re_i, im_i = own(at_re), own(at_im)
                re_j, im_j = others(at_re), others(at_im)
                real.append(re_i * re_j + im_i * im_j)
                imag.append(im_i * re_j - re_i * im_j)
            for part, product in enumerate((real, imag)):
                start = pl.multiple_of((target + part * per) * dates + tile * 16, 16)
                at_rows = pl.ds(start, 16)
                quads = []
                for k in range(out_rows + 1):
                    q = product[STEP * k + 3 : STEP * k + 7]
                    quads.append((q[0] + q[1]) + (q[2] + q[3]))
                for o in range(out_rows):
                    total = quads[o] + quads[o + 1]
                    for k in range(3):
                        total += jnp.where(az[o] <= k, product[STEP * o + k], product[STEP * o + 11 + k])
                    upper, rest = split(total)
                    left[at_rows, 2 * o * LANES : (2 * o + 1) * LANES] = upper
                    left[at_rows, (2 * o + 1) * LANES : (2 * o + 2) * LANES] = rest
                for side in range(2):
                    total = jnp.zeros((16, LANES), jnp.float32)
                    for edge in (2 * side, 2 * side + 1):
                        mine = own(edge, turned) if part else own(rows + edge)
                        total += jnp.where(edge_on[edge], mine * others(rows + edge), 0.0)
                    upper, rest = split(total)
                    start_col = depth + 2 * side * LANES
                    left[at_rows, start_col : start_col + LANES] = upper
                    left[at_rows, start_col + LANES : start_col + 2 * LANES] = rest
        return carry

    for first_date in range(0, dates, group):
        lax.fori_loop(0, group, functools.partial(one_date, first_date), 0)
        found = jnp.dot(left[...], weights[...], preferred_element_type=jnp.float32)
        sums[first_date * 2 * dates : (first_date + group) * 2 * dates, :] = found
    for date in range(dates):
        at_row = (date // per * 2 * per + date % per) * dates + date
        power[date : date + 1, :] = sums[at_row : at_row + 1, :]
    scale = lax.rsqrt(power[...] + epsilon)
    power[...] = scale
    position = iota((dates, wide), 0)
    column = iota((dates, wide), 1)
    rank = jnp.zeros((dates, wide), jnp.int32)
    for block in range(blocks):
        rank = jnp.where(position // per == block, order[block] * per + position % per, rank)
    for date in range(dates):
        later = rank > order[date // per] * per + date % per
        factor = scale * power[date : date + 1, :]
        starts = [((date // per * 2 + part) * per + date % per) * dates for part in range(2)]
        values = [jnp.where(later, sums[start : start + dates, :] * factor, 0.0) for start in starts]
        largest = jnp.max(jnp.maximum(jnp.abs(values[0]), jnp.abs(values[1])), axis=1, keepdims=True)
        level = jnp.floor(jnp.log(largest) * (LEVELS / LOG_2)) + 1.0
        level = jnp.clip(level, LOWEST, HIGHEST)
        codes = [jnp.floor(value * (jnp.exp(level * (-LOG_2 / LEVELS)) * TOP) + 0.5) for value in values]
        header = jnp.sum(jnp.where(position == column, level, 0.0), axis=0, keepdims=True)
        codes[0] = jnp.where(position == date, header, codes[0])
        for start, code in zip(starts, codes):
            send[start : start + dates, :] = code.astype(jnp.int32).astype(jnp.int16)


def join_kernel(blocks, per, out_rows, cols, recv, out, halves, done):
    dates = blocks * per
    wide = out_rows * cols
    per_tile = LANES // cols
    me = lax.axis_index("date")
    lane = iota((dates, LANES), 1) // cols
    position = iota((dates, wide), 0)
    column = iota((dates, wide), 1)
    factors = [[None] * blocks for _ in range(per)]
    copies = []
    for step in range(2 * per):
        own = me * per + step % per
        values = []
        for block in range(blocks):
            codes = recv[block, step * dates : (step + 1) * dates, :].astype(jnp.int32).astype(jnp.float32)
            if step < per:
                header = jnp.sum(jnp.where(position == own, codes, 0.0), axis=0, keepdims=True)
                level = jnp.sum(jnp.where(position == column, header, 0.0), axis=1, keepdims=True)
                factors[step][block] = jnp.exp(level * (LOG_2 / LEVELS)) * (1.0 / TOP)
            values.append(jnp.where(position == own, 0.0, codes * factors[step % per][block]))
        for d_tile in range(blocks // per_tile):
            for o_tile in range(out_rows // per_tile):
                tiles = [
                    values[d_tile * per_tile + d][:, o_tile * LANES : (o_tile + 1) * LANES] for d in range(per_tile)
                ]
                width = 1
                while width < per_tile:
                    swap = [None] * per_tile
                    upper = (lane // width) % 2 == 1
                    shift = width * cols
                    for a in range(per_tile):
                        if (a // width) % 2 == 0:
                            b = a + width
                            swap[a] = jnp.where(upper, pltpu.roll(tiles[b], shift, 1), tiles[a])
                            swap[b] = jnp.where(upper, tiles[b], pltpu.roll(tiles[a], LANES - shift, 1))
                    tiles = swap
                    width *= 2
                for o in range(per_tile):
                    for start in range(0, dates, 8):
                        at = start * out_rows + o_tile * per_tile + o
                        halves[step, d_tile, pl.ds(at, 8, stride=out_rows), :] = tiles[o][start : start + 8]
            rows = slice(step * dates * out_rows, (step + 1) * dates * out_rows)
            target = out.at[rows, d_tile * LANES : (d_tile + 1) * LANES]
            copies.append(pltpu.make_async_copy(halves.at[step, d_tile], target, done.at[step, d_tile]))
            copies[-1].start()
    for copy in copies:
        copy.wait()


def decode(codes, me, per):
    values = codes.astype(jnp.float32)
    dates = codes.shape[3]
    own = (me * per + jnp.arange(per))[:, None] == jnp.arange(dates)[None]
    header = jnp.sum(jnp.where(own[None, :, :, None], values[:, 0], 0.0), axis=2)
    factor = jnp.exp(header[:, :, :dates] * (LOG_2 / LEVELS)) * (1.0 / TOP)
    return jnp.where(own[None, None, :, :, None], 0.0, values * factor[:, None, :, :, None])


def on_device(slc, block_order, az_offset, rg_offset):
    blocks = lax.axis_size("date")
    strips = lax.axis_size("strip")
    per, lines, span = slc.shape[1:]
    dates = blocks * per
    chunk = span // blocks
    out_rows = lines // STEP
    cols = chunk // STEP
    wide = out_rows * cols
    date_rows = 2 * (lines + 2 * HALO) + EDGE
    depth = (out_rows + 2) * 2 * LANES
    group = max(per, 256 // dates)
    me = lax.axis_index("date")
    odd = lax.axis_index("strip") % 2

    def swaps(first):
        pairs = [(i, i + 1) for i in range(first, strips - 1, 2)]
        return pairs + [(target, source) for source, target in pairs]

    inner = lines - HALO
    other = lax.ppermute(lax.dynamic_slice_in_dim(slc, inner * odd, HALO, 2), "strip", swaps(1))
    paired = lax.ppermute(lax.dynamic_slice_in_dim(slc, inner * (1 - odd), HALO, 2), "strip", swaps(0))
    tiled = jnp.tile(lax.dynamic_slice_in_dim(rg_offset, me * cols, cols), out_rows)[None]
    weights = pl.pallas_call(
        functools.partial(weight_kernel, lines, chunk),
        out_shape=jax.ShapeDtypeStruct((depth, wide), jnp.bfloat16),
        in_specs=[SMEM, VMEM],
        out_specs=VMEM,
        compiler_params=PARAMS,
        cost_estimate=pl.CostEstimate(flops=0, bytes_accessed=4 * 1024 * 1024, transcendentals=0),
        name="weights",
    )(az_offset, tiled)
    other, paired, weights = lax.optimization_barrier((other, paired, weights))
    send = pl.pallas_call(
        functools.partial(pack_kernel, blocks, per, lines, chunk),
        out_shape=jax.ShapeDtypeStruct((blocks, per * date_rows, LANES), jnp.bfloat16),
        in_specs=[VMEM] * 3,
        out_specs=VMEM,
        scratch_shapes=[
            pltpu.VMEM((per * date_rows, span), jnp.float32),
            pltpu.VMEM((per * date_rows, LANES), jnp.float32),
        ],
        compiler_params=PARAMS,
        name="pack",
    )(slc, other, paired)
    recv = lax.all_to_all(send, "date", 0, 0, tiled=True)
    x = pl.pallas_call(
        functools.partial(spread_kernel, blocks, per, date_rows),
        out_shape=jax.ShapeDtypeStruct((date_rows * dates, LANES), jnp.float32),
        in_specs=[VMEM],
        out_specs=VMEM,
        compiler_params=PARAMS,
        name="spread",
    )(recv)
    pairs = pl.pallas_call(
        functools.partial(pair_kernel, blocks, per, lines, chunk, group),
        out_shape=jax.ShapeDtypeStruct((dates * 2 * dates, wide), jnp.int16),
        in_specs=[VMEM, SMEM, SMEM, SMEM, VMEM],
        out_specs=VMEM,
        scratch_shapes=[
            pltpu.VMEM((dates * 2 * dates, wide), jnp.float32),
            pltpu.VMEM((EDGE * dates, LANES), jnp.float32),
            pltpu.VMEM((group * 2 * dates, depth), jnp.bfloat16),
            pltpu.VMEM((dates, wide), jnp.float32),
        ],
        compiler_params=PARAMS,
        name="pairs",
    )(x, block_order, az_offset, rg_offset, weights)
    count = 2 * per * dates
    back = lax.all_to_all(pairs.reshape(blocks, count, wide), "date", 0, 0, tiled=True)
    if LANES % cols == 0 and out_rows * cols % LANES == 0 and blocks * cols % LANES == 0:
        out = pl.pallas_call(
            functools.partial(join_kernel, blocks, per, out_rows, cols),
            out_shape=jax.ShapeDtypeStruct((count * out_rows, blocks * cols), jnp.float32),
            in_specs=[VMEM],
            out_specs=pl.BlockSpec(memory_space=pl.ANY),
            scratch_shapes=[
                pltpu.VMEM((2 * per, blocks * cols // LANES, dates * out_rows, LANES), jnp.float32),
                pltpu.SemaphoreType.DMA((2 * per, blocks * cols // LANES)),
            ],
            compiler_params=PARAMS,
            name="join",
        )(back)
    else:
        values = decode(back.reshape(blocks, 2, per, dates, wide), me, per)
        out = values.reshape(blocks, count, out_rows, cols).transpose(1, 2, 0, 3)
    return out.reshape(2, per, dates, out_rows, blocks * cols)


def solution(mesh):
    placed = (P(None, "date", "strip", None), P(), P("strip"), P())
    return jax.shard_map(
        on_device,
        mesh=mesh,
        in_specs=placed,
        out_specs=P(None, "date", None, "strip", None),
        check_vma=False,
    )
```

```python
import functools

import jax
import jax.numpy as jnp
from jax import lax
from jax.experimental import pallas as pl
from jax.experimental.pallas import tpu as pltpu
from jax.sharding import PartitionSpec as P

STEP = 4
HALO = 5
REACH = 2
EDGE = 4
LANES = 128
GROUP = 16
VMEM = pl.BlockSpec(memory_space=pltpu.VMEM)
SMEM = pl.BlockSpec(memory_space=pltpu.SMEM)
PARAMS = pltpu.CompilerParams(vmem_limit_bytes=48 * 1024 * 1024)

epsilon = 1e-06
LEVELS = 8.0
LOWEST, HIGHEST = -880.0, 64.0
TOP = 32760.0
LOG_2 = 0.6931471805599453


def iota(shape, dim):
    return lax.broadcasted_iota(jnp.int32, shape, dim)


def row_of(part, line, lines):
    if line < HALO:
        return part * HALO + line
    if line >= lines - HALO:
        return GROUP + part * HALO + line - (lines - HALO)
    middle = part * (lines - 2 * HALO) + line - HALO
    spare = GROUP - 2 * HALO - EDGE
    if middle < spare:
        return 2 * HALO + EDGE + middle
    if middle < 2 * spare:
        return GROUP + 2 * HALO + EDGE + middle - spare
    return 2 * GROUP + middle - 2 * spare


def place_of(date, row, per, date_rows):
    if row < GROUP:
        return date * GROUP + row
    if row < 2 * GROUP:
        return (per + date - 1) * GROUP + row
    return 2 * per * GROUP + date * (date_rows - 2 * GROUP) + row - 2 * GROUP


def rows_of_date(lines):
    return 2 * GROUP + 2 * (lines - 2 * HALO) - 2 * (GROUP - 2 * HALO - EDGE)


def runs(part, lines):
    found = []
    for line in range(lines):
        row = row_of(part, line, lines)
        if line and row == row_of(part, line - 1, lines) + 1 and row % GROUP:
            found[-1][1] += 1
        else:
            found.append([line, 1])
    return found


def partners(blocks):
    return [0] + sorted(range(1, blocks), key=lambda k: (k & 1, -k))


def swap_blocks(pieces):
    blocks = len(pieces)
    found = list(pieces)
    for at, k in enumerate(partners(blocks)):
        if k:
            found[at] = lax.ppermute(pieces[at], "date", [(i, i ^ k) for i in range(blocks)])
    return found


def pack_kernel(blocks, per, lines, chunk, slc, *refs):
    pieces, (send, stage) = refs[:blocks], refs[blocks:]
    me = lax.axis_index("date")
    date_rows = rows_of_date(lines)
    edge_rows = per * GROUP
    turn = 1 - lax.axis_index("strip") % 2
    span = blocks * chunk
    shape = (EDGE * blocks, span)
    place = iota(shape, 0) % EDGE
    wanted = iota(shape, 0) // EDGE * chunk + jnp.where(place < REACH, place - REACH, place - REACH + chunk)
    picks = (iota(shape, 1) == wanted).astype(jnp.bfloat16)
    lane = iota((EDGE * blocks, LANES), 1)
    edges = []
    for date in range(per):
        mine = jnp.zeros((EDGE * blocks, LANES), jnp.float32)
        for part in range(2):
            samples = slc[part, date]
            for first, count in runs(part, lines):
                at = place_of(date, row_of(part, first, lines), per, date_rows)
                stage[at : at + count, :] = samples[first : first + count].astype(jnp.float32)
            found = lax.dot_general(picks, samples, (((1,), (1,)), ((), ())), preferred_element_type=jnp.float32)
            found = jnp.concatenate([found, jnp.zeros((EDGE * blocks, LANES - lines), jnp.float32)], axis=1)
            mine += pltpu.roll(found, part * (LANES // 2), 1) if part else found
        edges.append(mine)
    for block in range(blocks):
        for date in range(per):
            for group in range(2):
                at = place_of(date, group * GROUP + 2 * HALO, per, date_rows)
                value = edges[date][block * EDGE : (block + 1) * EDGE]
                if chunk == LANES:
                    stage[at : at + EDGE, block * LANES : (block + 1) * LANES] = value
        if chunk == LANES:
            piece = stage[:, block * chunk : (block + 1) * chunk]
        else:
            piece = stage[:, block * chunk : (block + 1) * chunk]
            piece = jnp.concatenate([piece, jnp.zeros((per * date_rows, LANES - chunk), jnp.float32)], axis=1)
            row = iota((per * date_rows, LANES), 0)
            for date in range(per):
                for group in range(2):
                    at = place_of(date, group * GROUP + 2 * HALO, per, date_rows)
                    for k in range(EDGE):
                        value = edges[date][block * EDGE + k : block * EDGE + k + 1]
                        piece = jnp.where(row == at + k, value, piece)
        piece = piece.astype(jnp.bfloat16)
        send[block, pl.ds(pl.multiple_of(turn * edge_rows, 16), edge_rows), :] = piece[:edge_rows]
        send[block, pl.ds(pl.multiple_of((1 - turn) * edge_rows, 16), edge_rows), :] = piece[edge_rows : 2 * edge_rows]
        send[block, 2 * edge_rows :, :] = piece[2 * edge_rows :]
    for piece, k in zip(pieces, partners(blocks)):
        piece[...] = send[me ^ k]


def weight_kernel(lines, chunk, az, tiled, weights):
    out_rows = lines // STEP
    cols = chunk // STEP
    wide = out_rows * cols
    depth = out_rows * 2 * LANES
    shape = (LANES, wide)
    col = iota(shape, 1) % cols
    out_row = iota(shape, 1) // cols
    box = jnp.abs(iota(shape, 0) - STEP * col - tiled[...]) <= REACH
    for o in range(out_rows):
        mine = (box & (out_row == o)).astype(jnp.bfloat16)
        weights[2 * o * LANES : (2 * o + 1) * LANES, :] = mine
        weights[(2 * o + 1) * LANES : (2 * o + 2) * LANES, :] = mine
    turn = iota(shape, 0) % (LANES // 2)
    line = jnp.where(turn < lines + HALO, turn + HALO, turn + HALO - LANES // 2)
    lower = jnp.zeros(shape, jnp.int32)
    for o in range(out_rows):
        lower = jnp.where(out_row == o, STEP * o + az[o], lower)
    window = (line >= lower) & (line <= lower + 2 * HALO)
    for side, edge_col in ((0, 0), (1, cols - 1)):
        mine = (window & (col == edge_col)).astype(jnp.bfloat16)
        for term in range(2):
            start = depth + (2 * side + term) * LANES
            weights[start : start + LANES, :] = mine


def to_sublanes(source, first_row, date_stride, rows, block, dates, per, target):
    for date in range(per):
        at = first_row + date * date_stride
        if not isinstance(at, int):
            at = pl.multiple_of(at, 8)
        value = source[pl.ds(at, rows), :].astype(jnp.float32)
        for row in range(0, rows, 8):
            target[pl.ds(row * dates + block * per + date, 8, stride=dates), :] = value[row : row + 8]


def spread_kernel(blocks, per, lines, *refs):
    recv, (x, paired, other) = refs[:blocks], refs[blocks:]
    dates = blocks * per
    date_rows = rows_of_date(lines)
    edge_rows = per * GROUP
    me = lax.axis_index("date")
    turn = 1 - lax.axis_index("strip") % 2
    rest = date_rows - 2 * GROUP
    for piece, k in zip(recv, partners(blocks)):
        block = me ^ k
        paired[block] = piece[:edge_rows]
        other[block] = piece[edge_rows : 2 * edge_rows]
        to_sublanes(piece, turn * edge_rows, GROUP, GROUP, block, dates, per, x)
        to_sublanes(piece, (1 - turn) * edge_rows, GROUP, GROUP, block, dates, per, x.at[GROUP * dates :])
        to_sublanes(piece, 2 * edge_rows, rest, rest, block, dates, per, x.at[2 * GROUP * dates :])


def split(value):
    high = value.astype(jnp.bfloat16)
    return high, (value - high.astype(jnp.float32)).astype(jnp.bfloat16)


def pair_kernel(
    blocks, per, lines, chunk, group, x, paired, other, order, az, rg, weights, *refs
):
    pieces, (send, sums, halo, edges, turned, left, power) = refs[:blocks], refs[blocks:]
    dates = blocks * per
    out_rows = lines // STEP
    cols = chunk // STEP
    wide = out_rows * cols
    me = lax.axis_index("date")
    depth = out_rows * 2 * LANES

    odd = lax.axis_index("strip") % 2
    for block in range(blocks):
        to_sublanes(paired.at[block], 0, GROUP, GROUP, block, dates, per, halo.at[1 - odd])
        to_sublanes(other.at[block], 0, GROUP, GROUP, block, dates, per, halo.at[odd])
    below, above = halo.at[0], halo.at[1]
    lane = iota((dates, LANES), 1)
    turn = lane % (LANES // 2)
    for k in range(EDGE):
        at = (2 * HALO + k) * dates
        lower_part = pltpu.roll(below[at : at + dates, :], lines, 1)
        upper_part = pltpu.roll(above[at : at + dates, :], lines, 1)
        value = jnp.where(turn < lines, x[at : at + dates, :], jnp.where(turn < lines + HALO, upper_part, lower_part))
        edges[k * dates : (k + 1) * dates, :] = value
        value = pltpu.roll(value, LANES // 2, 1)
        turned[k * dates : (k + 1) * dates, :] = jnp.where(lane < LANES // 2, value, -value)
    first = rg[me * cols]
    last = rg[me * cols + cols - 1]
    edge_on = (first <= 0, first <= 1, last >= 2, last >= 3)

    def where_line(part, line):
        if line < HALO:
            return below, part * HALO + line
        if line >= lines + HALO:
            return above, part * HALO + line - (lines + HALO)
        return x, row_of(part, line - HALO, lines)

    def one_date(first_date, step, carry):
        date = first_date + step
        target = (step // per * 2) * per + step % per
        for tile in range(dates // 16):

            def own(ref, row):
                return ref[pl.ds(row * dates + date, 1), :]

            def others(ref, row):
                return ref[row * dates + tile * 16 : row * dates + tile * 16 + 16, :]

            real, imag = [], []
            for line in range(lines + 2 * HALO):
                at_re, at_im = where_line(0, line), where_line(1, line)
                re_i, im_i = own(*at_re), own(*at_im)
                re_j, im_j = others(*at_re), others(*at_im)
                real.append(re_i * re_j + im_i * im_j)
                imag.append(im_i * re_j - re_i * im_j)
            for part, product in enumerate((real, imag)):
                start = pl.multiple_of((target + part * per) * dates + tile * 16, 16)
                at_rows = pl.ds(start, 16)
                quads = []
                for k in range(out_rows + 1):
                    q = product[STEP * k + 3 : STEP * k + 7]
                    quads.append((q[0] + q[1]) + (q[2] + q[3]))
                for o in range(out_rows):
                    total = quads[o] + quads[o + 1]
                    for k in range(3):
                        total += jnp.where(az[o] <= k, product[STEP * o + k], product[STEP * o + 11 + k])
                    upper, rest = split(total)
                    left[at_rows, 2 * o * LANES : (2 * o + 1) * LANES] = upper
                    left[at_rows, (2 * o + 1) * LANES : (2 * o + 2) * LANES] = rest
                for side in range(2):
                    total = jnp.zeros((16, LANES), jnp.float32)
                    for edge in (2 * side, 2 * side + 1):
                        mine = own(turned if part else edges, edge)
                        total += jnp.where(edge_on[edge], mine * others(edges, edge), 0.0)
                    upper, rest = split(total)
                    start_col = depth + 2 * side * LANES
                    left[at_rows, start_col : start_col + LANES] = upper
                    left[at_rows, start_col + LANES : start_col + 2 * LANES] = rest
        return carry

    for first_date in range(0, dates, group):
        lax.fori_loop(0, group, functools.partial(one_date, first_date), 0)
        found = jnp.dot(left[...], weights[...], preferred_element_type=jnp.float32)
        sums[first_date * 2 * dates : (first_date + group) * 2 * dates, :] = found
    for date in range(dates):
        at_row = (date // per * 2 * per + date % per) * dates + date
        power[date : date + 1, :] = sums[at_row : at_row + 1, :]
    scale = lax.rsqrt(power[...] + epsilon)
    power[...] = scale
    position = iota((dates, wide), 0)
    column = iota((dates, wide), 1)
    rank = jnp.zeros((dates, wide), jnp.int32)
    for block in range(blocks):
        rank = jnp.where(position // per == block, order[block] * per + position % per, rank)
    for date in range(dates):
        later = rank > order[date // per] * per + date % per
        factor = scale * power[date : date + 1, :]
        starts = [((date // per * 2 + part) * per + date % per) * dates for part in range(2)]
        values = [jnp.where(later, sums[start : start + dates, :] * factor, 0.0) for start in starts]
        largest = jnp.max(jnp.maximum(jnp.abs(values[0]), jnp.abs(values[1])), axis=1, keepdims=True)
        level = jnp.floor(jnp.log(largest) * (LEVELS / LOG_2)) + 1.0
        level = jnp.clip(level, LOWEST, HIGHEST)
        codes = [jnp.floor(value * (jnp.exp(level * (-LOG_2 / LEVELS)) * TOP) + 0.5) for value in values]
        header = jnp.sum(jnp.where(position == column, level, 0.0), axis=0, keepdims=True)
        codes[0] = jnp.where(position == date, header, codes[0])
        for start, code in zip(starts, codes):
            send[start : start + dates, :] = code.astype(jnp.int32).astype(jnp.int16)
    count = 2 * per * dates
    for piece, k in zip(pieces, partners(blocks)):
        piece[...] = send[pl.ds(pl.multiple_of((me ^ k) * count, 16), count), :]


def join_kernel(blocks, per, out_rows, cols, *refs):
    pieces, (out, recv, halves, done) = refs[:blocks], refs[blocks:]
    dates = blocks * per
    wide = out_rows * cols
    per_tile = LANES // cols
    me = lax.axis_index("date")
    lane = iota((dates, LANES), 1) // cols
    position = iota((dates, wide), 0)
    column = iota((dates, wide), 1)
    for piece, k in zip(pieces, partners(blocks)):
        recv[me ^ k] = piece[...]
    factors = [[None] * blocks for _ in range(per)]
    copies = []
    for step in range(2 * per):
        own = me * per + step % per
        values = []
        for block in range(blocks):
            codes = recv[block, step * dates : (step + 1) * dates, :].astype(jnp.int32).astype(jnp.float32)
            if step < per:
                header = jnp.sum(jnp.where(position == own, codes, 0.0), axis=0, keepdims=True)
                level = jnp.sum(jnp.where(position == column, header, 0.0), axis=1, keepdims=True)
                factors[step][block] = jnp.exp(level * (LOG_2 / LEVELS)) * (1.0 / TOP)
            values.append(jnp.where(position == own, 0.0, codes * factors[step % per][block]))
        for d_tile in range(blocks // per_tile):
            for o_tile in range(out_rows // per_tile):
                tiles = [
                    values[d_tile * per_tile + d][:, o_tile * LANES : (o_tile + 1) * LANES] for d in range(per_tile)
                ]
                width = 1
                while width < per_tile:
                    swap = [None] * per_tile
                    upper = (lane // width) % 2 == 1
                    shift = width * cols
                    for a in range(per_tile):
                        if (a // width) % 2 == 0:
                            b = a + width
                            swap[a] = jnp.where(upper, pltpu.roll(tiles[b], shift, 1), tiles[a])
                            swap[b] = jnp.where(upper, tiles[b], pltpu.roll(tiles[a], LANES - shift, 1))
                    tiles = swap
                    width *= 2
                for o in range(per_tile):
                    for start in range(0, dates, 8):
                        at = start * out_rows + o_tile * per_tile + o
                        halves[step, d_tile, pl.ds(at, 8, stride=out_rows), :] = tiles[o][start : start + 8]
            rows = slice(step * dates * out_rows, (step + 1) * dates * out_rows)
            target = out.at[rows, d_tile * LANES : (d_tile + 1) * LANES]
            copies.append(pltpu.make_async_copy(halves.at[step, d_tile], target, done.at[step, d_tile]))
            copies[-1].start()
    for copy in copies:
        copy.wait()


def decode(codes, me, per):
    values = codes.astype(jnp.float32)
    dates = codes.shape[3]
    own = (me * per + jnp.arange(per))[:, None] == jnp.arange(dates)[None]
    header = jnp.sum(jnp.where(own[None, :, :, None], values[:, 0], 0.0), axis=2)
    factor = jnp.exp(header[:, :, :dates] * (LOG_2 / LEVELS)) * (1.0 / TOP)
    return jnp.where(own[None, None, :, :, None], 0.0, values * factor[:, None, :, :, None])


def on_device(slc, block_order, az_offset, rg_offset):
    blocks = lax.axis_size("date")
    strips = lax.axis_size("strip")
    per, lines, span = slc.shape[1:]
    dates = blocks * per
    chunk = span // blocks
    out_rows = lines // STEP
    cols = chunk // STEP
    wide = out_rows * cols
    date_rows = rows_of_date(lines)
    depth = (out_rows + 2) * 2 * LANES
    group = max(per, 256 // dates)
    me = lax.axis_index("date")

    edge_rows = per * GROUP
    piece = jax.ShapeDtypeStruct((per * date_rows, LANES), jnp.bfloat16)
    send = pl.pallas_call(
        functools.partial(pack_kernel, blocks, per, lines, chunk),
        out_shape=[piece] * blocks,
        in_specs=[VMEM],
        out_specs=[VMEM] * blocks,
        scratch_shapes=[
            pltpu.VMEM((blocks, per * date_rows, LANES), jnp.bfloat16),
            pltpu.VMEM((per * date_rows, span), jnp.float32),
        ],
        compiler_params=PARAMS,
        name="pack",
    )(slc)
    recv = swap_blocks(send)
    tiled = jnp.tile(lax.dynamic_slice_in_dim(rg_offset, me * cols, cols), out_rows)[None]
    weights = pl.pallas_call(
        functools.partial(weight_kernel, lines, chunk),
        out_shape=jax.ShapeDtypeStruct((depth, wide), jnp.bfloat16),
        in_specs=[SMEM, VMEM],
        out_specs=VMEM,
        compiler_params=PARAMS,
        cost_estimate=pl.CostEstimate(flops=0, bytes_accessed=4 * 1024 * 1024, transcendentals=0),
        name="weights",
    )(az_offset, tiled)

    edge = jax.ShapeDtypeStruct((blocks, edge_rows, LANES), jnp.bfloat16)
    x, to_pair, to_other = pl.pallas_call(
        functools.partial(spread_kernel, blocks, per, lines),
        out_shape=[jax.ShapeDtypeStruct((date_rows * dates, LANES), jnp.float32), edge, edge],
        in_specs=[VMEM] * blocks,
        out_specs=[VMEM] * 3,
        compiler_params=PARAMS,
        name="spread",
    )(*recv)

    def swaps(first):
        pairs = [(i, i + 1) for i in range(first, strips - 1, 2)]
        return pairs + [(target, source) for source, target in pairs]

    other = lax.ppermute(to_other, "strip", swaps(1))
    paired = lax.ppermute(to_pair, "strip", swaps(0))
    pairs = pl.pallas_call(
        functools.partial(pair_kernel, blocks, per, lines, chunk, group),
        out_shape=[jax.ShapeDtypeStruct((2 * per * dates, wide), jnp.int16)] * blocks,
        in_specs=[VMEM, VMEM, VMEM, SMEM, SMEM, SMEM, VMEM],
        out_specs=[VMEM] * blocks,
        scratch_shapes=[
            pltpu.VMEM((dates * 2 * dates, wide), jnp.int16),
            pltpu.VMEM((dates * 2 * dates, wide), jnp.float32),
            pltpu.VMEM((2, GROUP * dates, LANES), jnp.float32),
            pltpu.VMEM((EDGE * dates, LANES), jnp.float32),
            pltpu.VMEM((EDGE * dates, LANES), jnp.float32),
            pltpu.VMEM((group * 2 * dates, depth), jnp.bfloat16),
            pltpu.VMEM((dates, wide), jnp.float32),
        ],
        compiler_params=PARAMS,
        name="pairs",
    )(x, paired, other, block_order, az_offset, rg_offset, weights)
    count = 2 * per * dates
    back = swap_blocks(pairs)
    if LANES % cols == 0 and out_rows * cols % LANES == 0 and blocks * cols % LANES == 0:
        out = pl.pallas_call(
            functools.partial(join_kernel, blocks, per, out_rows, cols),
            out_shape=jax.ShapeDtypeStruct((count * out_rows, blocks * cols), jnp.float32),
            in_specs=[VMEM] * blocks,
            out_specs=pl.BlockSpec(memory_space=pl.ANY),
            scratch_shapes=[
                pltpu.VMEM((blocks, count, wide), jnp.int16),
                pltpu.VMEM((2 * per, blocks * cols // LANES, dates * out_rows, LANES), jnp.float32),
                pltpu.SemaphoreType.DMA((2 * per, blocks * cols // LANES)),
            ],
            compiler_params=PARAMS,
            name="join",
        )(*back)
    else:
        place = [partners(blocks).index(k) for k in range(blocks)]
        back = jnp.stack([back[at] for at in place])[me ^ jnp.arange(blocks)]
        values = decode(back.reshape(blocks, 2, per, dates, wide), me, per)
        out = values.reshape(blocks, count, out_rows, cols).transpose(1, 2, 0, 3)
    return out.reshape(2, per, dates, out_rows, blocks * cols)


def solution(mesh):
    placed = (P(None, "date", "strip", None), P(), P("strip"), P())
    return jax.shard_map(
        on_device,
        mesh=mesh,
        in_specs=placed,
        out_specs=P(None, "date", None, "strip", None),
        check_vma=False,
    )
```

```python
import functools

import jax
import jax.numpy as jnp
from jax import lax
from jax.experimental import pallas as pl
from jax.experimental.pallas import tpu as pltpu
from jax.sharding import PartitionSpec as P

STEP = 4
HALO = 5
REACH = 2
EDGE = 4
LANES = 128
GROUP = 16
VMEM = pl.BlockSpec(memory_space=pltpu.VMEM)
SMEM = pl.BlockSpec(memory_space=pltpu.SMEM)
PARAMS = pltpu.CompilerParams(vmem_limit_bytes=48 * 1024 * 1024)

epsilon = 1e-06
LEVELS = 8.0
LOWEST, HIGHEST = -880.0, 64.0
TOP = 32760.0
LOG_2 = 0.6931471805599453


def iota(shape, dim):
    return lax.broadcasted_iota(jnp.int32, shape, dim)


def row_of(part, line, lines):
    if line < HALO:
        return part * HALO + line
    if line >= lines - HALO:
        return GROUP + part * HALO + line - (lines - HALO)
    middle = part * (lines - 2 * HALO) + line - HALO
    spare = GROUP - 2 * HALO - EDGE
    if middle < spare:
        return 2 * HALO + EDGE + middle
    if middle < 2 * spare:
        return GROUP + 2 * HALO + EDGE + middle - spare
    return 2 * GROUP + middle - 2 * spare


def place_of(date, row, per, date_rows):
    if row < GROUP:
        return date * GROUP + row
    if row < 2 * GROUP:
        return (per + date - 1) * GROUP + row
    return 2 * per * GROUP + date * (date_rows - 2 * GROUP) + row - 2 * GROUP


def rows_of_date(lines):
    return 2 * GROUP + 2 * (lines - 2 * HALO) - 2 * (GROUP - 2 * HALO - EDGE)


def runs(part, lines):
    found = []
    for line in range(lines):
        row = row_of(part, line, lines)
        if line and row == row_of(part, line - 1, lines) + 1 and row % GROUP:
            found[-1][1] += 1
        else:
            found.append([line, 1])
    return found


def partners(blocks):
    return [0] + sorted(range(1, blocks), key=lambda k: (k & 1, -k))


def swap_blocks(pieces):
    blocks = len(pieces)
    found = list(pieces)
    for at, k in enumerate(partners(blocks)):
        if k:
            found[at] = lax.ppermute(pieces[at], "date", [(i, i ^ k) for i in range(blocks)])
    return found


def pack_kernel(blocks, per, lines, chunk, slc, *refs):
    pieces, (send, stage) = refs[:blocks], refs[blocks:]
    me = lax.axis_index("date")
    date_rows = rows_of_date(lines)
    edge_rows = per * GROUP
    turn = 1 - lax.axis_index("strip") % 2
    span = blocks * chunk
    shape = (EDGE * blocks, span)
    place = iota(shape, 0) % EDGE
    wanted = iota(shape, 0) // EDGE * chunk + jnp.where(place < REACH, place - REACH, place - REACH + chunk)
    picks = (iota(shape, 1) == wanted).astype(jnp.bfloat16)
    lane = iota((EDGE * blocks, LANES), 1)
    edges = []
    for date in range(per):
        mine = jnp.zeros((EDGE * blocks, LANES), jnp.float32)
        for part in range(2):
            samples = slc[part, date]
            for first, count in runs(part, lines):
                at = place_of(date, row_of(part, first, lines), per, date_rows)
                stage[at : at + count, :] = samples[first : first + count].astype(jnp.float32)
            found = lax.dot_general(picks, samples, (((1,), (1,)), ((), ())), preferred_element_type=jnp.float32)
            found = jnp.concatenate([found, jnp.zeros((EDGE * blocks, LANES - lines), jnp.float32)], axis=1)
            mine += pltpu.roll(found, part * (LANES // 2), 1) if part else found
        edges.append(mine)
    for block in range(blocks):
        for date in range(per):
            for group in range(2):
                at = place_of(date, group * GROUP + 2 * HALO, per, date_rows)
                value = edges[date][block * EDGE : (block + 1) * EDGE]
                if chunk == LANES:
                    stage[at : at + EDGE, block * LANES : (block + 1) * LANES] = value
        if chunk == LANES:
            piece = stage[:, block * chunk : (block + 1) * chunk]
        else:
            piece = stage[:, block * chunk : (block + 1) * chunk]
            piece = jnp.concatenate([piece, jnp.zeros((per * date_rows, LANES - chunk), jnp.float32)], axis=1)
            row = iota((per * date_rows, LANES), 0)
            for date in range(per):
                for group in range(2):
                    at = place_of(date, group * GROUP + 2 * HALO, per, date_rows)
                    for k in range(EDGE):
                        value = edges[date][block * EDGE + k : block * EDGE + k + 1]
                        piece = jnp.where(row == at + k, value, piece)
        piece = piece.astype(jnp.bfloat16)
        send[block, pl.ds(pl.multiple_of(turn * edge_rows, 16), edge_rows), :] = piece[:edge_rows]
        send[block, pl.ds(pl.multiple_of((1 - turn) * edge_rows, 16), edge_rows), :] = piece[edge_rows : 2 * edge_rows]
        send[block, 2 * edge_rows :, :] = piece[2 * edge_rows :]
    for piece, k in zip(pieces, partners(blocks)):
        piece[...] = send[me ^ k]


def kinds_of_rows(out_rows):
    return list(range(2, out_rows - 2)), [0, 1, out_rows - 2, out_rows - 1]


def weight_kernel(lines, chunk, az, tiled, *weights):
    cols = chunk // STEP
    for rows, target in zip(kinds_of_rows(lines // STEP), weights):
        count = len(rows)
        depth = count * 2 * LANES
        shape = (LANES, count * cols)
        col = iota(shape, 1) % cols
        slot = iota(shape, 1) // cols
        box = jnp.abs(iota(shape, 0) - STEP * col - tiled[:, : count * cols]) <= REACH
        for o in range(count):
            mine = (box & (slot == o)).astype(jnp.bfloat16)
            target[2 * o * LANES : (2 * o + 1) * LANES, :] = mine
            target[(2 * o + 1) * LANES : (2 * o + 2) * LANES, :] = mine
        turn = iota(shape, 0) % (LANES // 2)
        line = jnp.where(turn < lines + HALO, turn + HALO, turn + HALO - LANES // 2)
        lower = jnp.zeros(shape, jnp.int32)
        for place, o in enumerate(rows):
            lower = jnp.where(slot == place, STEP * o + az[o], lower)
        window = (line >= lower) & (line <= lower + 2 * HALO)
        for side, edge_col in ((0, 0), (1, cols - 1)):
            mine = (window & (col == edge_col)).astype(jnp.bfloat16)
            for term in range(2):
                start = depth + (2 * side + term) * LANES
                target[start : start + LANES, :] = mine


def to_sublanes(source, first_row, date_stride, rows, block, dates, per, target):
    for date in range(per):
        at = first_row + date * date_stride
        if not isinstance(at, int):
            at = pl.multiple_of(at, 8)
        value = source[pl.ds(at, rows), :].astype(jnp.float32)
        for row in range(0, rows, 8):
            target[pl.ds(row * dates + block * per + date, 8, stride=dates), :] = value[row : row + 8]


def spread_kernel(blocks, per, lines, *refs):
    recv, (x, paired, other) = refs[:blocks], refs[blocks:]
    dates = blocks * per
    date_rows = rows_of_date(lines)
    edge_rows = per * GROUP
    me = lax.axis_index("date")
    turn = 1 - lax.axis_index("strip") % 2
    rest = date_rows - 2 * GROUP
    for piece, k in zip(recv, partners(blocks)):
        block = me ^ k
        paired[block] = piece[:edge_rows]
        other[block] = piece[edge_rows : 2 * edge_rows]
        to_sublanes(piece, turn * edge_rows, GROUP, GROUP, block, dates, per, x)
        to_sublanes(piece, (1 - turn) * edge_rows, GROUP, GROUP, block, dates, per, x.at[GROUP * dates :])
        to_sublanes(piece, 2 * edge_rows, rest, rest, block, dates, per, x.at[2 * GROUP * dates :])


def split(value):
    high = value.astype(jnp.bfloat16)
    return high, (value - high.astype(jnp.float32)).astype(jnp.bfloat16)


def plus(total, value):
    return value if total is None else total + value


def window_sums(product, rows, out_rows, az):
    quads = [None] * (out_rows + 1)
    for k in range(out_rows + 1):
        for line in range(STEP * k + 3, STEP * k + 7):
            if product[line] is not None:
                quads[k] = plus(quads[k], product[line])
    sums = []
    for o in rows:
        total = None
        for quad in (quads[o], quads[o + 1]):
            if quad is not None:
                total = plus(total, quad)
        for k in range(3):
            early, late = product[STEP * o + k], product[STEP * o + 11 + k]
            if early is None and late is None:
                continue
            early = jnp.zeros_like(late) if early is None else early
            late = jnp.zeros_like(early) if late is None else late
            total = plus(total, jnp.where(az[o] <= k, early, late))
        sums.append(total)
    return sums


def products(places, date, tile, dates):
    real, imag = [], []
    for line in places:
        if line is None:
            real.append(None)
            imag.append(None)
            continue
        (ref, at_re), (_, at_im) = line
        re_i, im_i = (ref[pl.ds(row * dates + date, 1), :] for row in (at_re, at_im))
        re_j, im_j = (ref[row * dates + tile * 16 : row * dates + tile * 16 + 16, :] for row in (at_re, at_im))
        real.append(re_i * re_j + im_i * im_j)
        imag.append(im_i * re_j - re_i * im_j)
    return real, imag


def store_split(target, rows, start, value):
    upper, rest = split(value)
    target[rows, start : start + LANES] = upper
    target[rows, start + LANES : start + 2 * LANES] = rest


def store_edges(target, rows, depth, edges, turned, part, date, tile, dates, edge_on):
    for side in range(2):
        total = jnp.zeros((16, LANES), jnp.float32)
        for edge in (2 * side, 2 * side + 1):
            mine = (turned if part else edges)[pl.ds(edge * dates + date, 1), :]
            others = edges[edge * dates + tile * 16 : edge * dates + tile * 16 + 16, :]
            total += jnp.where(edge_on[edge], mine * others, 0.0)
        store_split(target, rows, depth + 2 * side * LANES, total)


def turn_edges(edges, turned, dates):
    lane = iota((dates, LANES), 1)
    for k in range(EDGE):
        value = pltpu.roll(edges[k * dates : (k + 1) * dates, :], LANES // 2, 1)
        turned[k * dates : (k + 1) * dates, :] = jnp.where(lane < LANES // 2, value, -value)


def edges_in_use(rg, cols):
    me = lax.axis_index("date")
    first = rg[me * cols]
    last = rg[me * cols + cols - 1]
    return first <= 0, first <= 1, last >= 2, last >= 3


def inner_kernel(blocks, per, lines, chunk, group, x, order, az, rg, weights, found, partial, turned, left):
    dates = blocks * per
    out_rows = lines // STEP
    inner, outer = kinds_of_rows(out_rows)
    depth = len(inner) * 2 * LANES
    edge_on = edges_in_use(rg, chunk // STEP)
    edges = x.at[2 * HALO * dates : (2 * HALO + EDGE) * dates]
    turn_edges(edges, turned, dates)
    places = [None] * HALO
    places += [[(x, row_of(part, line, lines)) for part in range(2)] for line in range(lines)]
    places += [None] * HALO

    def one_date(first_date, step, carry):
        date = first_date + step
        target = (step // per * 2) * per + step % per
        for tile in range(dates // 16):
            for part, product in enumerate(products(places, date, tile, dates)):
                start = pl.multiple_of((target + part * per) * dates + tile * 16, 16)
                at_rows = pl.ds(start, 16)
                sums = window_sums(product, range(out_rows), out_rows, az)
                for slot, o in enumerate(inner):
                    store_split(left, at_rows, 2 * slot * LANES, sums[o])
                whole = pl.ds(pl.multiple_of(first_date * 2 * dates + start, 16), 16)
                for slot, o in enumerate(outer):
                    partial[whole, slot * LANES : (slot + 1) * LANES] = sums[o]
                store_edges(left, at_rows, depth, edges, turned, part, date, tile, dates, edge_on)
        return carry

    for first_date in range(0, dates, group):
        lax.fori_loop(0, group, functools.partial(one_date, first_date), 0)
        result = jnp.dot(left[...], weights[...], preferred_element_type=jnp.float32)
        found[first_date * 2 * dates : (first_date + group) * 2 * dates, :] = result


def outer_kernel(
    blocks, per, lines, chunk, group, x, paired, other, partial, found, order, az, rg, weights, *refs
):
    pieces, (send, sums, halo, edges, turned, left, power) = refs[:blocks], refs[blocks:]
    dates = blocks * per
    out_rows = lines // STEP
    cols = chunk // STEP
    wide = out_rows * cols
    me = lax.axis_index("date")
    inner, outer = kinds_of_rows(out_rows)
    depth = len(outer) * 2 * LANES
    edge_on = edges_in_use(rg, cols)

    odd = lax.axis_index("strip") % 2
    for block in range(blocks):
        to_sublanes(paired.at[block], 0, GROUP, GROUP, block, dates, per, halo.at[1 - odd])
        to_sublanes(other.at[block], 0, GROUP, GROUP, block, dates, per, halo.at[odd])
    below, above = halo.at[0], halo.at[1]
    lane = iota((dates, LANES), 1)
    turn = lane % (LANES // 2)
    for k in range(EDGE):
        at = (2 * HALO + k) * dates
        lower_part = pltpu.roll(below[at : at + dates, :], lines, 1)
        upper_part = pltpu.roll(above[at : at + dates, :], lines, 1)
        value = jnp.where(turn < lines, x[at : at + dates, :], jnp.where(turn < lines + HALO, upper_part, lower_part))
        edges[k * dates : (k + 1) * dates, :] = value
    turn_edges(edges, turned, dates)
    places = [[(below, part * HALO + line) for part in range(2)] for line in range(HALO)]
    places += [None] * lines
    places += [[(above, part * HALO + line) for part in range(2)] for line in range(HALO)]

    def one_date(first_date, step, carry):
        date = first_date + step
        target = (step // per * 2) * per + step % per
        for tile in range(dates // 16):
            for part, product in enumerate(products(places, date, tile, dates)):
                start = pl.multiple_of((target + part * per) * dates + tile * 16, 16)
                at_rows = pl.ds(start, 16)
                whole = pl.ds(pl.multiple_of(first_date * 2 * dates + start, 16), 16)
                for slot, total in enumerate(window_sums(product, outer, out_rows, az)):
                    total += partial[whole, slot * LANES : (slot + 1) * LANES]
                    store_split(left, at_rows, 2 * slot * LANES, total)
                store_edges(left, at_rows, depth, edges, turned, part, date, tile, dates, edge_on)
        return carry

    sums[:, : len(inner) * cols] = found[...]
    for first_date in range(0, dates, group):
        lax.fori_loop(0, group, functools.partial(one_date, first_date), 0)
        result = jnp.dot(left[...], weights[...], preferred_element_type=jnp.float32)
        sums[first_date * 2 * dates : (first_date + group) * 2 * dates, len(inner) * cols :] = result
    for date in range(dates):
        at_row = (date // per * 2 * per + date % per) * dates + date
        power[date : date + 1, :] = sums[at_row : at_row + 1, :]
    scale = lax.rsqrt(power[...] + epsilon)
    power[...] = scale
    position = iota((dates, wide), 0)
    column = iota((dates, wide), 1)
    rank = jnp.zeros((dates, wide), jnp.int32)
    for block in range(blocks):
        rank = jnp.where(position // per == block, order[block] * per + position % per, rank)
    for date in range(dates):
        later = rank > order[date // per] * per + date % per
        factor = scale * power[date : date + 1, :]
        starts = [((date // per * 2 + part) * per + date % per) * dates for part in range(2)]
        values = [jnp.where(later, sums[start : start + dates, :] * factor, 0.0) for start in starts]
        largest = jnp.max(jnp.maximum(jnp.abs(values[0]), jnp.abs(values[1])), axis=1, keepdims=True)
        level = jnp.floor(jnp.log(largest) * (LEVELS / LOG_2)) + 1.0
        level = jnp.clip(level, LOWEST, HIGHEST)
        codes = [jnp.floor(value * (jnp.exp(level * (-LOG_2 / LEVELS)) * TOP) + 0.5) for value in values]
        header = jnp.sum(jnp.where(position == column, level, 0.0), axis=0, keepdims=True)
        codes[0] = jnp.where(position == date, header, codes[0])
        for start, code in zip(starts, codes):
            send[start : start + dates, :] = code.astype(jnp.int32).astype(jnp.int16)
    count = 2 * per * dates
    for piece, k in zip(pieces, partners(blocks)):
        piece[...] = send[pl.ds(pl.multiple_of((me ^ k) * count, 16), count), :]


def join_kernel(blocks, per, out_rows, cols, *refs):
    pieces, (out, recv, halves, done) = refs[:blocks], refs[blocks:]
    dates = blocks * per
    wide = out_rows * cols
    per_tile = LANES // cols
    me = lax.axis_index("date")
    lane = iota((dates, LANES), 1) // cols
    position = iota((dates, wide), 0)
    column = iota((dates, wide), 1)
    row_order = sum(kinds_of_rows(out_rows), [])
    for piece, k in zip(pieces, partners(blocks)):
        recv[me ^ k] = piece[...]
    factors = [[None] * blocks for _ in range(per)]
    copies = []
    for step in range(2 * per):
        own = me * per + step % per
        values = []
        for block in range(blocks):
            codes = recv[block, step * dates : (step + 1) * dates, :].astype(jnp.int32).astype(jnp.float32)
            if step < per:
                header = jnp.sum(jnp.where(position == own, codes, 0.0), axis=0, keepdims=True)
                level = jnp.sum(jnp.where(position == column, header, 0.0), axis=1, keepdims=True)
                factors[step][block] = jnp.exp(level * (LOG_2 / LEVELS)) * (1.0 / TOP)
            values.append(jnp.where(position == own, 0.0, codes * factors[step % per][block]))
        for d_tile in range(blocks // per_tile):
            for o_tile in range(out_rows // per_tile):
                tiles = [
                    values[d_tile * per_tile + d][:, o_tile * LANES : (o_tile + 1) * LANES] for d in range(per_tile)
                ]
                width = 1
                while width < per_tile:
                    swap = [None] * per_tile
                    upper = (lane // width) % 2 == 1
                    shift = width * cols
                    for a in range(per_tile):
                        if (a // width) % 2 == 0:
                            b = a + width
                            swap[a] = jnp.where(upper, pltpu.roll(tiles[b], shift, 1), tiles[a])
                            swap[b] = jnp.where(upper, tiles[b], pltpu.roll(tiles[a], LANES - shift, 1))
                    tiles = swap
                    width *= 2
                for o in range(per_tile):
                    for start in range(0, dates, 8):
                        at = start * out_rows + row_order[o_tile * per_tile + o]
                        halves[step, d_tile, pl.ds(at, 8, stride=out_rows), :] = tiles[o][start : start + 8]
            rows = slice(step * dates * out_rows, (step + 1) * dates * out_rows)
            target = out.at[rows, d_tile * LANES : (d_tile + 1) * LANES]
            copies.append(pltpu.make_async_copy(halves.at[step, d_tile], target, done.at[step, d_tile]))
            copies[-1].start()
    for copy in copies:
        copy.wait()


def decode(codes, me, per):
    values = codes.astype(jnp.float32)
    dates = codes.shape[3]
    own = (me * per + jnp.arange(per))[:, None] == jnp.arange(dates)[None]
    header = jnp.sum(jnp.where(own[None, :, :, None], values[:, 0], 0.0), axis=2)
    factor = jnp.exp(header[:, :, :dates] * (LOG_2 / LEVELS)) * (1.0 / TOP)
    return jnp.where(own[None, None, :, :, None], 0.0, values * factor[:, None, :, :, None])


def on_device(slc, block_order, az_offset, rg_offset):
    blocks = lax.axis_size("date")
    strips = lax.axis_size("strip")
    per, lines, span = slc.shape[1:]
    dates = blocks * per
    chunk = span // blocks
    out_rows = lines // STEP
    cols = chunk // STEP
    wide = out_rows * cols
    date_rows = rows_of_date(lines)
    group = max(per, 256 // dates)
    me = lax.axis_index("date")

    edge_rows = per * GROUP
    piece = jax.ShapeDtypeStruct((per * date_rows, LANES), jnp.bfloat16)
    send = pl.pallas_call(
        functools.partial(pack_kernel, blocks, per, lines, chunk),
        out_shape=[piece] * blocks,
        in_specs=[VMEM],
        out_specs=[VMEM] * blocks,
        scratch_shapes=[
            pltpu.VMEM((blocks, per * date_rows, LANES), jnp.bfloat16),
            pltpu.VMEM((per * date_rows, span), jnp.float32),
        ],
        compiler_params=PARAMS,
        name="pack",
    )(slc)
    recv = swap_blocks(send)
    tiled = jnp.tile(lax.dynamic_slice_in_dim(rg_offset, me * cols, cols), out_rows)[None]
    kinds = kinds_of_rows(out_rows)
    depths = [(len(rows) + 2) * 2 * LANES for rows in kinds]
    weights = pl.pallas_call(
        functools.partial(weight_kernel, lines, chunk),
        out_shape=[
            jax.ShapeDtypeStruct((depth, len(rows) * cols), jnp.bfloat16) for depth, rows in zip(depths, kinds)
        ],
        in_specs=[SMEM, VMEM],
        out_specs=[VMEM] * 2,
        compiler_params=PARAMS,
        cost_estimate=pl.CostEstimate(flops=0, bytes_accessed=4 * 1024 * 1024, transcendentals=0),
        name="weights",
    )(az_offset, tiled)
    recv, weights = lax.optimization_barrier((recv, weights))

    edge = jax.ShapeDtypeStruct((blocks, edge_rows, LANES), jnp.bfloat16)
    x, to_pair, to_other = pl.pallas_call(
        functools.partial(spread_kernel, blocks, per, lines),
        out_shape=[jax.ShapeDtypeStruct((date_rows * dates, LANES), jnp.float32), edge, edge],
        in_specs=[VMEM] * blocks,
        out_specs=[VMEM] * 3,
        compiler_params=PARAMS,
        name="spread",
    )(*recv)

    def swaps(first):
        pairs = [(i, i + 1) for i in range(first, strips - 1, 2)]
        return pairs + [(target, source) for source, target in pairs]

    other = lax.ppermute(to_other, "strip", swaps(1))
    paired = lax.ppermute(to_pair, "strip", swaps(0))
    count = dates * 2 * dates
    found, partial = pl.pallas_call(
        functools.partial(inner_kernel, blocks, per, lines, chunk, group),
        out_shape=[
            jax.ShapeDtypeStruct((count, len(kinds[0]) * cols), jnp.float32),
            jax.ShapeDtypeStruct((count, len(kinds[1]) * LANES), jnp.float32),
        ],
        in_specs=[VMEM, SMEM, SMEM, SMEM, VMEM],
        out_specs=[VMEM] * 2,
        scratch_shapes=[
            pltpu.VMEM((EDGE * dates, LANES), jnp.float32),
            pltpu.VMEM((group * 2 * dates, depths[0]), jnp.bfloat16),
        ],
        compiler_params=PARAMS,
        cost_estimate=pl.CostEstimate(flops=0, bytes_accessed=12 * 1024 * 1024, transcendentals=0),
        name="inner",
    )(x, block_order, az_offset, rg_offset, weights[0])
    pairs = pl.pallas_call(
        functools.partial(outer_kernel, blocks, per, lines, chunk, group),
        out_shape=[jax.ShapeDtypeStruct((2 * per * dates, wide), jnp.int16)] * blocks,
        in_specs=[VMEM] * 5 + [SMEM] * 3 + [VMEM],
        out_specs=[VMEM] * blocks,
        scratch_shapes=[
            pltpu.VMEM((count, wide), jnp.int16),
            pltpu.VMEM((count, wide), jnp.float32),
            pltpu.VMEM((2, GROUP * dates, LANES), jnp.float32),
            pltpu.VMEM((EDGE * dates, LANES), jnp.float32),
            pltpu.VMEM((EDGE * dates, LANES), jnp.float32),
            pltpu.VMEM((group * 2 * dates, depths[1]), jnp.bfloat16),
            pltpu.VMEM((dates, wide), jnp.float32),
        ],
        compiler_params=PARAMS,
        name="outer",
    )(x, paired, other, partial, found, block_order, az_offset, rg_offset, weights[1])
    count = 2 * per * dates
    back = swap_blocks(pairs)
    if LANES % cols == 0 and out_rows * cols % LANES == 0 and blocks * cols % LANES == 0:
        out = pl.pallas_call(
            functools.partial(join_kernel, blocks, per, out_rows, cols),
            out_shape=jax.ShapeDtypeStruct((count * out_rows, blocks * cols), jnp.float32),
            in_specs=[VMEM] * blocks,
            out_specs=pl.BlockSpec(memory_space=pl.ANY),
            scratch_shapes=[
                pltpu.VMEM((blocks, count, wide), jnp.int16),
                pltpu.VMEM((2 * per, blocks * cols // LANES, dates * out_rows, LANES), jnp.float32),
                pltpu.SemaphoreType.DMA((2 * per, blocks * cols // LANES)),
            ],
            compiler_params=PARAMS,
            name="join",
        )(*back)
    else:
        place = [partners(blocks).index(k) for k in range(blocks)]
        back = jnp.stack([back[at] for at in place])[me ^ jnp.arange(blocks)]
        values = decode(back.reshape(blocks, 2, per, dates, wide), me, per)
        values = values.reshape(blocks, count, out_rows, cols).transpose(1, 2, 0, 3)
        row_order = sum(kinds_of_rows(out_rows), [])
        out = jnp.stack([values[:, row_order.index(o)] for o in range(out_rows)], axis=1)
    return out.reshape(2, per, dates, out_rows, blocks * cols)


def solution(mesh):
    placed = (P(None, "date", "strip", None), P(), P("strip"), P())
    return jax.shard_map(
        on_device,
        mesh=mesh,
        in_specs=placed,
        out_specs=P(None, "date", None, "strip", None),
        check_vma=False,
    )
```

```python
import functools

import jax
import jax.numpy as jnp
from jax import lax
from jax.experimental import pallas as pl
from jax.experimental.pallas import tpu as pltpu
from jax.sharding import PartitionSpec as P

STEP = 4
HALO = 5
REACH = 2
EDGE = 4
LANES = 128
GROUP = 16
VMEM = pl.BlockSpec(memory_space=pltpu.VMEM)
SMEM = pl.BlockSpec(memory_space=pltpu.SMEM)
PARAMS = pltpu.CompilerParams(vmem_limit_bytes=48 * 1024 * 1024)

epsilon = 1e-06
LEVELS = 8.0
LOWEST, HIGHEST = -880.0, 64.0
TOP = 32760.0
LOG_2 = 0.6931471805599453


def iota(shape, dim):
    return lax.broadcasted_iota(jnp.int32, shape, dim)


def row_of(part, line, lines):
    if line < HALO:
        return part * HALO + line
    if line >= lines - HALO:
        return GROUP + part * HALO + line - (lines - HALO)
    middle = part * (lines - 2 * HALO) + line - HALO
    spare = GROUP - 2 * HALO - EDGE
    if middle < spare:
        return 2 * HALO + EDGE + middle
    if middle < 2 * spare:
        return GROUP + 2 * HALO + EDGE + middle - spare
    return 2 * GROUP + middle - 2 * spare


def place_of(date, row, per, date_rows):
    if row < GROUP:
        return date * GROUP + row
    if row < 2 * GROUP:
        return (per + date - 1) * GROUP + row
    return 2 * per * GROUP + date * (date_rows - 2 * GROUP) + row - 2 * GROUP


def rows_of_date(lines):
    return 2 * GROUP + 2 * (lines - 2 * HALO) - 2 * (GROUP - 2 * HALO - EDGE)


def runs(part, lines):
    found = []
    for line in range(lines):
        row = row_of(part, line, lines)
        if line and row == row_of(part, line - 1, lines) + 1 and row % GROUP:
            found[-1][1] += 1
        else:
            found.append([line, 1])
    return found


def partners(blocks):
    return [0] + sorted(range(1, blocks), key=lambda k: (k & 1, -k))


def swap_blocks(pieces):
    blocks = len(pieces)
    found = list(pieces)
    for at, k in enumerate(partners(blocks)):
        if k:
            found[at] = lax.ppermute(pieces[at], "date", [(i, i ^ k) for i in range(blocks)])
    return found


def pack_kernel(blocks, per, lines, chunk, slc, *refs):
    pieces, (send, stage) = refs[:blocks], refs[blocks:]
    me = lax.axis_index("date")
    date_rows = rows_of_date(lines)
    edge_rows = per * GROUP
    turn = 1 - lax.axis_index("strip") % 2
    span = blocks * chunk
    shape = (EDGE * blocks, span)
    place = iota(shape, 0) % EDGE
    wanted = iota(shape, 0) // EDGE * chunk + jnp.where(place < REACH, place - REACH, place - REACH + chunk)
    picks = (iota(shape, 1) == wanted).astype(jnp.bfloat16)
    lane = iota((EDGE * blocks, LANES), 1)
    edges = []
    for date in range(per):
        mine = jnp.zeros((EDGE * blocks, LANES), jnp.float32)
        for part in range(2):
            samples = slc[part, date]
            for first, count in runs(part, lines):
                at = place_of(date, row_of(part, first, lines), per, date_rows)
                stage[at : at + count, :] = samples[first : first + count].astype(jnp.float32)
            found = lax.dot_general(picks, samples, (((1,), (1,)), ((), ())), preferred_element_type=jnp.float32)
            found = jnp.concatenate([found, jnp.zeros((EDGE * blocks, LANES - lines), jnp.float32)], axis=1)
            mine += pltpu.roll(found, part * (LANES // 2), 1) if part else found
        edges.append(mine)
    for block in range(blocks):
        for date in range(per):
            for group in range(2):
                at = place_of(date, group * GROUP + 2 * HALO, per, date_rows)
                value = edges[date][block * EDGE : (block + 1) * EDGE]
                if chunk == LANES:
                    stage[at : at + EDGE, block * LANES : (block + 1) * LANES] = value
        if chunk == LANES:
            piece = stage[:, block * chunk : (block + 1) * chunk]
        else:
            piece = stage[:, block * chunk : (block + 1) * chunk]
            piece = jnp.concatenate([piece, jnp.zeros((per * date_rows, LANES - chunk), jnp.float32)], axis=1)
            row = iota((per * date_rows, LANES), 0)
            for date in range(per):
                for group in range(2):
                    at = place_of(date, group * GROUP + 2 * HALO, per, date_rows)
                    for k in range(EDGE):
                        value = edges[date][block * EDGE + k : block * EDGE + k + 1]
                        piece = jnp.where(row == at + k, value, piece)
        piece = piece.astype(jnp.bfloat16)
        send[block, pl.ds(pl.multiple_of(turn * edge_rows, 16), edge_rows), :] = piece[:edge_rows]
        send[block, pl.ds(pl.multiple_of((1 - turn) * edge_rows, 16), edge_rows), :] = piece[edge_rows : 2 * edge_rows]
        send[block, 2 * edge_rows :, :] = piece[2 * edge_rows :]
    for piece, k in zip(pieces, partners(blocks)):
        piece[...] = send[me ^ k]


def kinds_of_rows(out_rows):
    return list(range(2, out_rows - 2)), [0, 1, out_rows - 2, out_rows - 1]


def weight_kernel(lines, chunk, az, tiled, *weights):
    cols = chunk // STEP
    for rows, target in zip(kinds_of_rows(lines // STEP), weights):
        count = len(rows)
        depth = count * 2 * LANES
        shape = (LANES, count * cols)
        col = iota(shape, 1) % cols
        slot = iota(shape, 1) // cols
        box = jnp.abs(iota(shape, 0) - STEP * col - tiled[:, : count * cols]) <= REACH
        for o in range(count):
            mine = (box & (slot == o)).astype(jnp.bfloat16)
            target[2 * o * LANES : (2 * o + 1) * LANES, :] = mine
            target[(2 * o + 1) * LANES : (2 * o + 2) * LANES, :] = mine
        turn = iota(shape, 0) % (LANES // 2)
        line = jnp.where(turn < lines + HALO, turn + HALO, turn + HALO - LANES // 2)
        lower = jnp.zeros(shape, jnp.int32)
        for place, o in enumerate(rows):
            lower = jnp.where(slot == place, STEP * o + az[o], lower)
        window = (line >= lower) & (line <= lower + 2 * HALO)
        for side, edge_col in ((0, 0), (1, cols - 1)):
            mine = (window & (col == edge_col)).astype(jnp.bfloat16)
            for term in range(2):
                start = depth + (2 * side + term) * LANES
                target[start : start + LANES, :] = mine


def to_sublanes(source, first_row, date_stride, rows, block, dates, per, target):
    for date in range(per):
        at = first_row + date * date_stride
        if not isinstance(at, int):
            at = pl.multiple_of(at, 8)
        value = source[pl.ds(at, rows), :].astype(jnp.float32)
        for row in range(0, rows, 8):
            target[pl.ds(row * dates + block * per + date, 8, stride=dates), :] = value[row : row + 8]


def spread_kernel(blocks, per, lines, order, *refs):
    recv, (x, paired, other) = refs[:blocks], refs[blocks:]
    dates = blocks * per
    date_rows = rows_of_date(lines)
    edge_rows = per * GROUP
    me = lax.axis_index("date")
    turn = 1 - lax.axis_index("strip") % 2
    rest = date_rows - 2 * GROUP
    for piece, k in zip(recv, partners(blocks)):
        block = me ^ k
        paired[block] = piece[:edge_rows]
        other[block] = piece[edge_rows : 2 * edge_rows]
        block = order[block]
        to_sublanes(piece, turn * edge_rows, GROUP, GROUP, block, dates, per, x)
        to_sublanes(piece, (1 - turn) * edge_rows, GROUP, GROUP, block, dates, per, x.at[GROUP * dates :])
        to_sublanes(piece, 2 * edge_rows, rest, rest, block, dates, per, x.at[2 * GROUP * dates :])


def split(value):
    high = value.astype(jnp.bfloat16)
    return high, (value - high.astype(jnp.float32)).astype(jnp.bfloat16)


def plus(total, value):
    return value if total is None else total + value


def window_sums(product, rows, out_rows, az):
    quads = [None] * (out_rows + 1)
    for k in range(out_rows + 1):
        for line in range(STEP * k + 3, STEP * k + 7):
            if product[line] is not None:
                quads[k] = plus(quads[k], product[line])
    sums = []
    for o in rows:
        total = None
        for quad in (quads[o], quads[o + 1]):
            if quad is not None:
                total = plus(total, quad)
        for k in range(3):
            early, late = product[STEP * o + k], product[STEP * o + 11 + k]
            if early is None and late is None:
                continue
            early = jnp.zeros_like(late) if early is None else early
            late = jnp.zeros_like(early) if late is None else late
            total = plus(total, jnp.where(az[o] <= k, early, late))
        sums.append(total)
    return sums


def products(places, date, first, count, dates):
    real, imag = [], []
    for line in places:
        if line is None:
            real.append(None)
            imag.append(None)
            continue
        (ref, at_re), (_, at_im) = line
        re_i, im_i = (ref[pl.ds(row * dates + date, 1), :] for row in (at_re, at_im))
        re_j, im_j = (ref[row * dates + first : row * dates + first + count, :] for row in (at_re, at_im))
        real.append(re_i * re_j + im_i * im_j)
        imag.append(im_i * re_j - re_i * im_j)
    return real, imag


def store_split(target, rows, start, value):
    upper, rest = split(value)
    target[rows, start : start + LANES] = upper
    target[rows, start + LANES : start + 2 * LANES] = rest


def edge_sums(edges, own, date, first, count, dates, edge_on):
    sums = []
    for side in range(2):
        total = jnp.zeros((count, LANES), jnp.float32)
        for edge in (2 * side, 2 * side + 1):
            others = edges[edge * dates + first : edge * dates + first + count, :]
            total += jnp.where(edge_on[edge], own[pl.ds(edge * dates + date, 1), :] * others, 0.0)
        sums.append(total)
    return sums


def all_dates(dates, group, places, rows, out_rows, az, edges, turned, edge_on, store, finish):
    half = dates // 2
    group = min(group, half)

    def sums_of(date, first, count):
        found = []
        for part, product in enumerate(products(places, date, first, count, dates)):
            sums = window_sums(product, rows, out_rows, az)
            found.append(sums + edge_sums(edges, turned if part else edges, date, first, count, dates, edge_on))
        return found

    def early(first_date, step, carry):
        for tile in range(dates // 16):
            for part, sums in enumerate(sums_of(first_date + step, tile * 16, 16)):
                store(first_date * 2 * dates, step * 2 * dates + part * dates + tile * 16, sums)
        return carry

    def late(first_date, step, carry):
        for tile in range(half // 8):
            real, imag = sums_of(half + first_date + step, half + tile * 8, 8)
            both = [jnp.concatenate([re, im], axis=0) for re, im in zip(real, imag)]
            store((dates + first_date) * dates, step * dates + tile * 16, both)
        return carry

    for body, width in ((early, 2 * dates), (late, dates)):
        for first_date in range(0, half, group):
            lax.fori_loop(0, group, functools.partial(body, first_date), 0)
            start = first_date * width + (half * 2 * dates if body is late else 0)
            finish(start, group * width)


def turn_edges(edges, turned, dates):
    lane = iota((dates, LANES), 1)
    for k in range(EDGE):
        value = pltpu.roll(edges[k * dates : (k + 1) * dates, :], LANES // 2, 1)
        turned[k * dates : (k + 1) * dates, :] = jnp.where(lane < LANES // 2, value, -value)


def edges_in_use(rg, cols):
    me = lax.axis_index("date")
    first = rg[me * cols]
    last = rg[me * cols + cols - 1]
    return first <= 0, first <= 1, last >= 2, last >= 3


def inner_kernel(blocks, per, lines, chunk, group, x, order, az, rg, weights, found, partial, turned, left):
    dates = blocks * per
    out_rows = lines // STEP
    inner, outer = kinds_of_rows(out_rows)
    edges = x.at[2 * HALO * dates : (2 * HALO + EDGE) * dates]
    turn_edges(edges, turned, dates)
    places = [None] * HALO
    places += [[(x, row_of(part, line, lines)) for part in range(2)] for line in range(lines)]
    places += [None] * HALO
    rows = inner + outer

    def store(base, start, sums):
        at_rows = pl.ds(pl.multiple_of(start, 16), 16)
        whole = pl.ds(pl.multiple_of(base + start, 16), 16)
        for slot, total in enumerate(sums[: len(inner)] + sums[len(rows) :]):
            store_split(left, at_rows, 2 * slot * LANES, total)
        for slot, total in enumerate(sums[len(inner) : len(rows)]):
            partial[whole, slot * LANES : (slot + 1) * LANES] = total

    def finish(start, count):
        found[start : start + count, :] = jnp.dot(left[:count, :], weights[...], preferred_element_type=jnp.float32)

    edge_on = edges_in_use(rg, chunk // STEP)
    all_dates(dates, group, places, rows, out_rows, az, edges, turned, edge_on, store, finish)


def outer_kernel(
    blocks, per, lines, chunk, group, x, paired, other, partial, found, order, az, rg, weights, *refs
):
    pieces, (send, sums, halo, edges, turned, left, power) = refs[:blocks], refs[blocks:]
    dates = blocks * per
    half = dates // 2
    out_rows = lines // STEP
    cols = chunk // STEP
    wide = out_rows * cols
    me = lax.axis_index("date")
    inner, outer = kinds_of_rows(out_rows)
    split_at = len(inner) * cols

    odd = lax.axis_index("strip") % 2
    for block in range(blocks):
        to_sublanes(paired.at[block], 0, GROUP, GROUP, order[block], dates, per, halo.at[1 - odd])
        to_sublanes(other.at[block], 0, GROUP, GROUP, order[block], dates, per, halo.at[odd])
    below, above = halo.at[0], halo.at[1]
    lane = iota((dates, LANES), 1)
    turn = lane % (LANES // 2)
    for k in range(EDGE):
        at = (2 * HALO + k) * dates
        lower_part = pltpu.roll(below[at : at + dates, :], lines, 1)
        upper_part = pltpu.roll(above[at : at + dates, :], lines, 1)
        value = jnp.where(turn < lines, x[at : at + dates, :], jnp.where(turn < lines + HALO, upper_part, lower_part))
        edges[k * dates : (k + 1) * dates, :] = value
    turn_edges(edges, turned, dates)
    places = [[(below, part * HALO + line) for part in range(2)] for line in range(HALO)]
    places += [None] * lines
    places += [[(above, part * HALO + line) for part in range(2)] for line in range(HALO)]

    def store(base, start, totals):
        at_rows = pl.ds(pl.multiple_of(start, 16), 16)
        whole = pl.ds(pl.multiple_of(base + start, 16), 16)
        for slot, total in enumerate(totals):
            if slot < len(outer):
                total += partial[whole, slot * LANES : (slot + 1) * LANES]
            store_split(left, at_rows, 2 * slot * LANES, total)

    def finish(start, count):
        rows = slice(start, start + count)
        sums[rows, split_at:] = jnp.dot(left[:count, :], weights[...], preferred_element_type=jnp.float32)

    sums[:, :split_at] = found[...]
    edge_on = edges_in_use(rg, cols)
    all_dates(dates, group, places, outer, out_rows, az, edges, turned, edge_on, store, finish)

    def row_at(date, part, later):
        if date < half:
            return (date * 2 + part) * dates + later
        later -= half
        return (dates + date - half) * dates + later // 8 * 16 + part * 8 + later % 8

    for date in range(dates):
        at_row = row_at(date, 0, date)
        power[date : date + 1, :] = sums[at_row : at_row + 1, :]
    scale = lax.rsqrt(power[...] + epsilon)
    power[...] = scale
    position = iota((dates, wide), 0)
    column = iota((dates, wide), 1)
    for date in range(dates):
        factor = scale * power[date : date + 1, :]
        values = []
        for part in range(2):
            if date < half:
                value = sums[row_at(date, part, 0) : row_at(date, part, 0) + dates, :]
            else:
                tiles = [row_at(date, part, half + tile) for tile in range(0, half, 8)]
                value = [jnp.zeros((half, wide), jnp.float32)] + [sums[row : row + 8, :] for row in tiles]
                value = jnp.concatenate(value, axis=0)
            values.append(jnp.where(position > date, value * factor, 0.0))
        largest = jnp.max(jnp.maximum(jnp.abs(values[0]), jnp.abs(values[1])), axis=1, keepdims=True)
        level = jnp.floor(jnp.log(largest) * (LEVELS / LOG_2)) + 1.0
        level = jnp.clip(level, LOWEST, HIGHEST)
        codes = [jnp.floor(value * (jnp.exp(level * (-LOG_2 / LEVELS)) * TOP) + 0.5) for value in values]
        header = jnp.sum(jnp.where(position == column, level, 0.0), axis=0, keepdims=True)
        codes[0] = jnp.where(position == date, header, codes[0])
        for part, code in enumerate(codes):
            start = ((date // per * 2 + part) * per + date % per) * dates
            send[start : start + dates, :] = code.astype(jnp.int32).astype(jnp.int16)
    count = 2 * per * dates
    for piece, k in zip(pieces, partners(blocks)):
        piece[...] = send[pl.ds(pl.multiple_of(order[me ^ k] * count, 16), count), :]


def join_kernel(blocks, per, out_rows, cols, order, *refs):
    pieces, (out, recv, halves, placed, done) = refs[:blocks], refs[blocks:]
    dates = blocks * per
    wide = out_rows * cols
    per_tile = LANES // cols
    me = lax.axis_index("date")
    lane = iota((dates, LANES), 1) // cols
    position = iota((dates, wide), 0)
    column = iota((dates, wide), 1)
    row_order = sum(kinds_of_rows(out_rows), [])
    for piece, k in zip(pieces, partners(blocks)):
        recv[me ^ k] = piece[...]
    factors = [[None] * blocks for _ in range(per)]
    copies = []
    for step in range(2 * per):
        own = order[me] * per + step % per
        values = []
        for block in range(blocks):
            codes = recv[block, step * dates : (step + 1) * dates, :].astype(jnp.int32).astype(jnp.float32)
            if step < per:
                header = jnp.sum(jnp.where(position == own, codes, 0.0), axis=0, keepdims=True)
                level = jnp.sum(jnp.where(position == column, header, 0.0), axis=1, keepdims=True)
                factors[step][block] = jnp.exp(level * (LOG_2 / LEVELS)) * (1.0 / TOP)
            values.append(jnp.where(position == own, 0.0, codes * factors[step % per][block]))
        for d_tile in range(blocks // per_tile):
            for o_tile in range(out_rows // per_tile):
                tiles = [
                    values[d_tile * per_tile + d][:, o_tile * LANES : (o_tile + 1) * LANES] for d in range(per_tile)
                ]
                width = 1
                while width < per_tile:
                    swap = [None] * per_tile
                    upper = (lane // width) % 2 == 1
                    shift = width * cols
                    for a in range(per_tile):
                        if (a // width) % 2 == 0:
                            b = a + width
                            swap[a] = jnp.where(upper, pltpu.roll(tiles[b], shift, 1), tiles[a])
                            swap[b] = jnp.where(upper, tiles[b], pltpu.roll(tiles[a], LANES - shift, 1))
                    tiles = swap
                    width *= 2
                for o in range(per_tile):
                    for start in range(0, dates, 8):
                        at = start * out_rows + row_order[o_tile * per_tile + o]
                        halves[step, d_tile, pl.ds(at, 8, stride=out_rows), :] = tiles[o][start : start + 8]
            own_rows = per * out_rows
            for block in range(blocks):
                found = halves[step, d_tile, pl.ds(pl.multiple_of(order[block] * own_rows, 8), own_rows), :]
                placed[step, d_tile, block * own_rows : (block + 1) * own_rows, :] = found
            rows = slice(step * dates * out_rows, (step + 1) * dates * out_rows)
            target = out.at[rows, d_tile * LANES : (d_tile + 1) * LANES]
            copies.append(pltpu.make_async_copy(placed.at[step, d_tile], target, done.at[step, d_tile]))
            copies[-1].start()
    for copy in copies:
        copy.wait()


def decode(codes, me, per):
    values = codes.astype(jnp.float32)
    dates = codes.shape[3]
    own = (me * per + jnp.arange(per))[:, None] == jnp.arange(dates)[None]
    header = jnp.sum(jnp.where(own[None, :, :, None], values[:, 0], 0.0), axis=2)
    factor = jnp.exp(header[:, :, :dates] * (LOG_2 / LEVELS)) * (1.0 / TOP)
    return jnp.where(own[None, None, :, :, None], 0.0, values * factor[:, None, :, :, None])


def on_device(slc, block_order, az_offset, rg_offset):
    blocks = lax.axis_size("date")
    strips = lax.axis_size("strip")
    per, lines, span = slc.shape[1:]
    dates = blocks * per
    chunk = span // blocks
    out_rows = lines // STEP
    cols = chunk // STEP
    wide = out_rows * cols
    date_rows = rows_of_date(lines)
    group = max(per, 256 // dates)
    me = lax.axis_index("date")

    edge_rows = per * GROUP
    piece = jax.ShapeDtypeStruct((per * date_rows, LANES), jnp.bfloat16)
    send = pl.pallas_call(
        functools.partial(pack_kernel, blocks, per, lines, chunk),
        out_shape=[piece] * blocks,
        in_specs=[VMEM],
        out_specs=[VMEM] * blocks,
        scratch_shapes=[
            pltpu.VMEM((blocks, per * date_rows, LANES), jnp.bfloat16),
            pltpu.VMEM((per * date_rows, span), jnp.float32),
        ],
        compiler_params=PARAMS,
        name="pack",
    )(slc)
    recv = swap_blocks(send)
    tiled = jnp.tile(lax.dynamic_slice_in_dim(rg_offset, me * cols, cols), out_rows)[None]
    kinds = kinds_of_rows(out_rows)
    depths = [(len(rows) + 2) * 2 * LANES for rows in kinds]
    weights = pl.pallas_call(
        functools.partial(weight_kernel, lines, chunk),
        out_shape=[
            jax.ShapeDtypeStruct((depth, len(rows) * cols), jnp.bfloat16) for depth, rows in zip(depths, kinds)
        ],
        in_specs=[SMEM, VMEM],
        out_specs=[VMEM] * 2,
        compiler_params=PARAMS,
        cost_estimate=pl.CostEstimate(flops=0, bytes_accessed=4 * 1024 * 1024, transcendentals=0),
        name="weights",
    )(az_offset, tiled)
    recv, weights = lax.optimization_barrier((recv, weights))

    edge = jax.ShapeDtypeStruct((blocks, edge_rows, LANES), jnp.bfloat16)
    x, to_pair, to_other = pl.pallas_call(
        functools.partial(spread_kernel, blocks, per, lines),
        out_shape=[jax.ShapeDtypeStruct((date_rows * dates, LANES), jnp.float32), edge, edge],
        in_specs=[SMEM] + [VMEM] * blocks,
        out_specs=[VMEM] * 3,
        compiler_params=PARAMS,
        name="spread",
    )(block_order, *recv)

    def swaps(first):
        pairs = [(i, i + 1) for i in range(first, strips - 1, 2)]
        return pairs + [(target, source) for source, target in pairs]

    other = lax.ppermute(to_other, "strip", swaps(1))
    paired = lax.ppermute(to_pair, "strip", swaps(0))
    count = dates * dates * 3 // 2
    half_group = min(group, dates // 2)
    found, partial = pl.pallas_call(
        functools.partial(inner_kernel, blocks, per, lines, chunk, group),
        out_shape=[
            jax.ShapeDtypeStruct((count, len(kinds[0]) * cols), jnp.float32),
            jax.ShapeDtypeStruct((count, len(kinds[1]) * LANES), jnp.float32),
        ],
        in_specs=[VMEM, SMEM, SMEM, SMEM, VMEM],
        out_specs=[VMEM] * 2,
        scratch_shapes=[
            pltpu.VMEM((EDGE * dates, LANES), jnp.float32),
            pltpu.VMEM((half_group * 2 * dates, depths[0]), jnp.bfloat16),
        ],
        compiler_params=PARAMS,
        cost_estimate=pl.CostEstimate(flops=0, bytes_accessed=12 * 1024 * 1024, transcendentals=0),
        name="inner",
    )(x, block_order, az_offset, rg_offset, weights[0])
    pairs = pl.pallas_call(
        functools.partial(outer_kernel, blocks, per, lines, chunk, group),
        out_shape=[jax.ShapeDtypeStruct((2 * per * dates, wide), jnp.int16)] * blocks,
        in_specs=[VMEM] * 5 + [SMEM] * 3 + [VMEM],
        out_specs=[VMEM] * blocks,
        scratch_shapes=[
            pltpu.VMEM((dates * 2 * dates, wide), jnp.int16),
            pltpu.VMEM((count, wide), jnp.float32),
            pltpu.VMEM((2, GROUP * dates, LANES), jnp.float32),
            pltpu.VMEM((EDGE * dates, LANES), jnp.float32),
            pltpu.VMEM((EDGE * dates, LANES), jnp.float32),
            pltpu.VMEM((half_group * 2 * dates, depths[1]), jnp.bfloat16),
            pltpu.VMEM((dates, wide), jnp.float32),
        ],
        compiler_params=PARAMS,
        name="outer",
    )(x, paired, other, partial, found, block_order, az_offset, rg_offset, weights[1])
    count = 2 * per * dates
    back = swap_blocks(pairs)
    if LANES % cols == 0 and out_rows * cols % LANES == 0 and blocks * cols % LANES == 0:
        out = pl.pallas_call(
            functools.partial(join_kernel, blocks, per, out_rows, cols),
            out_shape=jax.ShapeDtypeStruct((count * out_rows, blocks * cols), jnp.float32),
            in_specs=[SMEM] + [VMEM] * blocks,
            out_specs=pl.BlockSpec(memory_space=pl.ANY),
            scratch_shapes=[
                pltpu.VMEM((blocks, count, wide), jnp.int16),
                pltpu.VMEM((2 * per, blocks * cols // LANES, dates * out_rows, LANES), jnp.float32),
                pltpu.VMEM((2 * per, blocks * cols // LANES, dates * out_rows, LANES), jnp.float32),
                pltpu.SemaphoreType.DMA((2 * per, blocks * cols // LANES)),
            ],
            compiler_params=PARAMS,
            name="join",
        )(block_order, *back)
    else:
        place = [partners(blocks).index(k) for k in range(blocks)]
        back = jnp.stack([back[at] for at in place])[me ^ jnp.arange(blocks)]
        values = decode(back.reshape(blocks, 2, per, dates, wide), block_order[me], per)
        values = values.reshape(blocks, 2, per, blocks, per, wide)[:, :, :, block_order]
        values = values.reshape(blocks, count, out_rows, cols).transpose(1, 2, 0, 3)
        row_order = sum(kinds_of_rows(out_rows), [])
        out = jnp.stack([values[:, row_order.index(o)] for o in range(out_rows)], axis=1)
    return out.reshape(2, per, dates, out_rows, blocks * cols)


def solution(mesh):
    placed = (P(None, "date", "strip", None), P(), P("strip"), P())
    return jax.shard_map(
        on_device,
        mesh=mesh,
        in_specs=placed,
        out_specs=P(None, "date", None, "strip", None),
        check_vma=False,
    )
```

```python
import functools

import jax
import jax.numpy as jnp
from jax import lax
from jax.experimental import pallas as pl
from jax.experimental.pallas import tpu as pltpu
from jax.sharding import PartitionSpec as P

STEP = 4
HALO = 5
REACH = 2
EDGE = 4
LANES = 128
GROUP = 16
VMEM = pl.BlockSpec(memory_space=pltpu.VMEM)
SMEM = pl.BlockSpec(memory_space=pltpu.SMEM)
PARAMS = pltpu.CompilerParams(vmem_limit_bytes=48 * 1024 * 1024)

epsilon = 1e-06
LEVELS = 8.0
LOWEST, HIGHEST = -880.0, 64.0
TOP = 32760.0
LOG_2 = 0.6931471805599453


def iota(shape, dim):
    return lax.broadcasted_iota(jnp.int32, shape, dim)


def row_of(part, line, lines):
    if line < HALO:
        return part * HALO + line
    if line >= lines - HALO:
        return GROUP + part * HALO + line - (lines - HALO)
    middle = part * (lines - 2 * HALO) + line - HALO
    spare = GROUP - 2 * HALO - EDGE
    if middle < spare:
        return 2 * HALO + EDGE + middle
    if middle < 2 * spare:
        return GROUP + 2 * HALO + EDGE + middle - spare
    return 2 * GROUP + middle - 2 * spare


def place_of(date, row, per, date_rows):
    if row < GROUP:
        return date * GROUP + row
    if row < 2 * GROUP:
        return (per + date - 1) * GROUP + row
    return 2 * per * GROUP + date * (date_rows - 2 * GROUP) + row - 2 * GROUP


def rows_of_date(lines):
    return 2 * GROUP + 2 * (lines - 2 * HALO) - 2 * (GROUP - 2 * HALO - EDGE)


def runs(part, lines):
    found = []
    for line in range(lines):
        row = row_of(part, line, lines)
        if line and row == row_of(part, line - 1, lines) + 1 and row % GROUP:
            found[-1][1] += 1
        else:
            found.append([line, 1])
    return found


def partners(blocks):
    return [0] + sorted(range(1, blocks), key=lambda k: (k & 1, -k))


def swap_blocks(pieces):
    blocks = len(pieces)
    found = list(pieces)
    for at, k in enumerate(partners(blocks)):
        if k:
            found[at] = lax.ppermute(pieces[at], "date", [(i, i ^ k) for i in range(blocks)])
    return found


def pack_kernel(blocks, per, lines, chunk, slc, *refs):
    pieces, (send, stage) = refs[:blocks], refs[blocks:]
    me = lax.axis_index("date")
    date_rows = rows_of_date(lines)
    edge_rows = per * GROUP
    turn = 1 - lax.axis_index("strip") % 2
    span = blocks * chunk
    shape = (EDGE * blocks, span)
    place = iota(shape, 0) % EDGE
    wanted = iota(shape, 0) // EDGE * chunk + jnp.where(place < REACH, place - REACH, place - REACH + chunk)
    picks = (iota(shape, 1) == wanted).astype(jnp.bfloat16)
    lane = iota((EDGE * blocks, LANES), 1)
    edges = []
    for date in range(per):
        mine = jnp.zeros((EDGE * blocks, LANES), jnp.float32)
        for part in range(2):
            samples = slc[part, date]
            for first, count in runs(part, lines):
                at = place_of(date, row_of(part, first, lines), per, date_rows)
                stage[at : at + count, :] = samples[first : first + count].astype(jnp.float32)
            found = lax.dot_general(picks, samples, (((1,), (1,)), ((), ())), preferred_element_type=jnp.float32)
            found = jnp.concatenate([found, jnp.zeros((EDGE * blocks, LANES - lines), jnp.float32)], axis=1)
            mine += pltpu.roll(found, part * (LANES // 2), 1) if part else found
        edges.append(mine)
    for block in range(blocks):
        for date in range(per):
            for group in range(2):
                at = place_of(date, group * GROUP + 2 * HALO, per, date_rows)
                value = edges[date][block * EDGE : (block + 1) * EDGE]
                if chunk == LANES:
                    stage[at : at + EDGE, block * LANES : (block + 1) * LANES] = value
        if chunk == LANES:
            piece = stage[:, block * chunk : (block + 1) * chunk]
        else:
            piece = stage[:, block * chunk : (block + 1) * chunk]
            piece = jnp.concatenate([piece, jnp.zeros((per * date_rows, LANES - chunk), jnp.float32)], axis=1)
            row = iota((per * date_rows, LANES), 0)
            for date in range(per):
                for group in range(2):
                    at = place_of(date, group * GROUP + 2 * HALO, per, date_rows)
                    for k in range(EDGE):
                        value = edges[date][block * EDGE + k : block * EDGE + k + 1]
                        piece = jnp.where(row == at + k, value, piece)
        piece = piece.astype(jnp.bfloat16)
        send[block, pl.ds(pl.multiple_of(turn * edge_rows, 16), edge_rows), :] = piece[:edge_rows]
        send[block, pl.ds(pl.multiple_of((1 - turn) * edge_rows, 16), edge_rows), :] = piece[edge_rows : 2 * edge_rows]
        send[block, 2 * edge_rows :, :] = piece[2 * edge_rows :]
    for piece, k in zip(pieces, partners(blocks)):
        piece[...] = send[me ^ k]


def kinds_of_rows(out_rows):
    return list(range(2, out_rows - 2)), [0, 1, out_rows - 2, out_rows - 1]


def weight_kernel(lines, chunk, az, tiled, *weights):
    cols = chunk // STEP
    for rows, target in zip(kinds_of_rows(lines // STEP), weights):
        count = len(rows)
        depth = count * 2 * LANES
        shape = (LANES, count * cols)
        col = iota(shape, 1) % cols
        slot = iota(shape, 1) // cols
        box = jnp.abs(iota(shape, 0) - STEP * col - tiled[:, : count * cols]) <= REACH
        for o in range(count):
            mine = (box & (slot == o)).astype(jnp.bfloat16)
            target[2 * o * LANES : (2 * o + 1) * LANES, :] = mine
            target[(2 * o + 1) * LANES : (2 * o + 2) * LANES, :] = mine
        turn = iota(shape, 0) % (LANES // 2)
        line = jnp.where(turn < lines + HALO, turn + HALO, turn + HALO - LANES // 2)
        lower = jnp.zeros(shape, jnp.int32)
        for place, o in enumerate(rows):
            lower = jnp.where(slot == place, STEP * o + az[o], lower)
        window = (line >= lower) & (line <= lower + 2 * HALO)
        for side, edge_col in ((0, 0), (1, cols - 1)):
            mine = (window & (col == edge_col)).astype(jnp.bfloat16)
            for term in range(2):
                start = depth + (2 * side + term) * LANES
                target[start : start + LANES, :] = mine


def to_sublanes(source, first_row, date_stride, rows, block, dates, per, target):
    for date in range(per):
        at = first_row + date * date_stride
        if not isinstance(at, int):
            at = pl.multiple_of(at, 8)
        value = source[pl.ds(at, rows), :].astype(jnp.float32)
        for row in range(0, rows, 8):
            target[pl.ds(row * dates + block * per + date, 8, stride=dates), :] = value[row : row + 8]


def halo_rows(per):
    return per * 2 * HALO + EDGE


def gather_kernel(blocks, per, lines, *refs):
    recv, (paired, other, stage) = refs[:blocks], refs[blocks:]
    me = lax.axis_index("date")
    tail = 2 * HALO - 8
    for piece, k in zip(recv, partners(blocks)):
        for group, target in enumerate((paired, other)):
            edges = jnp.zeros((EDGE, LANES), jnp.float32)
            for date in range(per):
                at = (group * per + date) * GROUP
                value = piece[at : at + GROUP].astype(jnp.float32)
                stage[date * 8 : date * 8 + 8, :] = value[:8]
                stage[per * 8 + date * tail : per * 8 + (date + 1) * tail, :] = value[8 : 2 * HALO]
                mine = value[2 * HALO : 2 * HALO + EDGE]
                edges += pltpu.roll(mine, date * lines, 1) if date else mine
            stage[per * 2 * HALO :, :] = edges
            target[me ^ k] = stage[...].astype(jnp.bfloat16)


def scatter_halo(source, block, lines, dates, per, target):
    value = source.astype(jnp.float32)
    tail = 2 * HALO - 8
    for date in range(per):
        place = block * per + date
        target[pl.ds(place, 8, stride=dates), :] = value[date * 8 : date * 8 + 8]
        rest = value[per * 8 + date * tail : per * 8 + (date + 1) * tail]
        target[pl.ds(8 * dates + place, tail, stride=dates), :] = rest
        mine = value[per * 2 * HALO :]
        mine = pltpu.roll(mine, LANES - date * lines, 1) if date else mine
        target[pl.ds(2 * HALO * dates + place, EDGE, stride=dates), :] = mine


def split(value):
    high = value.astype(jnp.bfloat16)
    return high, (value - high.astype(jnp.float32)).astype(jnp.bfloat16)


def plus(total, value):
    return value if total is None else total + value


def window_sums(product, rows, out_rows, az):
    quads = [None] * (out_rows + 1)
    for k in range(out_rows + 1):
        for line in range(STEP * k + 3, STEP * k + 7):
            if product[line] is not None:
                quads[k] = plus(quads[k], product[line])
    sums = []
    for o in rows:
        total = None
        for quad in (quads[o], quads[o + 1]):
            if quad is not None:
                total = plus(total, quad)
        for k in range(3):
            early, late = product[STEP * o + k], product[STEP * o + 11 + k]
            if early is None and late is None:
                continue
            early = jnp.zeros_like(late) if early is None else early
            late = jnp.zeros_like(early) if late is None else late
            total = plus(total, jnp.where(az[o] <= k, early, late))
        sums.append(total)
    return sums


def products(places, date, first, count, dates):
    real, imag = [], []
    for line in places:
        if line is None:
            real.append(None)
            imag.append(None)
            continue
        (ref, at_re), (_, at_im) = line
        re_i, im_i = (ref[pl.ds(row * dates + date, 1), :] for row in (at_re, at_im))
        re_j, im_j = (ref[row * dates + first : row * dates + first + count, :] for row in (at_re, at_im))
        real.append(re_i * re_j + im_i * im_j)
        imag.append(im_i * re_j - re_i * im_j)
    return real, imag


def store_split(target, rows, start, value):
    upper, rest = split(value)
    target[rows, start : start + LANES] = upper
    target[rows, start + LANES : start + 2 * LANES] = rest


def edge_sums(edges, own, date, first, count, dates, edge_on):
    sums = []
    for side in range(2):
        total = jnp.zeros((count, LANES), jnp.float32)
        for edge in (2 * side, 2 * side + 1):
            others = edges[edge * dates + first : edge * dates + first + count, :]
            total += jnp.where(edge_on[edge], own[pl.ds(edge * dates + date, 1), :] * others, 0.0)
        sums.append(total)
    return sums


def all_dates(dates, group, places, rows, out_rows, az, edges, turned, edge_on, store, finish):
    half = dates // 2
    group = min(group, half)

    def sums_of(date, first, count):
        found = []
        for part, product in enumerate(products(places, date, first, count, dates)):
            sums = window_sums(product, rows, out_rows, az)
            found.append(sums + edge_sums(edges, turned if part else edges, date, first, count, dates, edge_on))
        return found

    def early(first_date, step, carry):
        for tile in range(dates // 16):
            for part, sums in enumerate(sums_of(first_date + step, tile * 16, 16)):
                store(first_date * 2 * dates, step * 2 * dates + part * dates + tile * 16, sums)
        return carry

    def late(first_date, step, carry):
        for tile in range(half // 8):
            real, imag = sums_of(half + first_date + step, half + tile * 8, 8)
            both = [jnp.concatenate([re, im], axis=0) for re, im in zip(real, imag)]
            store((dates + first_date) * dates, step * dates + tile * 16, both)
        return carry

    for body, width in ((early, 2 * dates), (late, dates)):
        for first_date in range(0, half, group):
            lax.fori_loop(0, group, functools.partial(body, first_date), 0)
            start = first_date * width + (half * 2 * dates if body is late else 0)
            finish(start, group * width)


def turn_edges(edges, turned, dates):
    lane = iota((dates, LANES), 1)
    for k in range(EDGE):
        value = pltpu.roll(edges[k * dates : (k + 1) * dates, :], LANES // 2, 1)
        turned[k * dates : (k + 1) * dates, :] = jnp.where(lane < LANES // 2, value, -value)


def edges_in_use(rg, cols):
    me = lax.axis_index("date")
    first = rg[me * cols]
    last = rg[me * cols + cols - 1]
    return first <= 0, first <= 1, last >= 2, last >= 3


def inner_kernel(blocks, per, lines, chunk, group, order, az, rg, weights, *refs):
    recv, (found, partial, own_edges, x, turned, left) = refs[:blocks], refs[blocks:]
    dates = blocks * per
    date_rows = rows_of_date(lines)
    edge_rows = per * GROUP
    me = lax.axis_index("date")
    swap = 1 - lax.axis_index("strip") % 2
    rest = date_rows - 2 * GROUP
    for piece, k in zip(recv, partners(blocks)):
        block = order[me ^ k]
        to_sublanes(piece, swap * edge_rows, GROUP, GROUP, block, dates, per, x)
        to_sublanes(piece, (1 - swap) * edge_rows, GROUP, GROUP, block, dates, per, x.at[GROUP * dates :])
        to_sublanes(piece, 2 * edge_rows, rest, rest, block, dates, per, x.at[2 * GROUP * dates :])
    own_edges[...] = x[2 * HALO * dates : (2 * HALO + EDGE) * dates, :]
    out_rows = lines // STEP
    inner, outer = kinds_of_rows(out_rows)
    edges = x.at[2 * HALO * dates : (2 * HALO + EDGE) * dates]
    turn_edges(edges, turned, dates)
    places = [None] * HALO
    places += [[(x, row_of(part, line, lines)) for part in range(2)] for line in range(lines)]
    places += [None] * HALO
    rows = inner + outer

    def store(base, start, sums):
        at_rows = pl.ds(pl.multiple_of(start, 16), 16)
        whole = pl.ds(pl.multiple_of(base + start, 16), 16)
        for slot, total in enumerate(sums[: len(inner)] + sums[len(rows) :]):
            store_split(left, at_rows, 2 * slot * LANES, total)
        for slot, total in enumerate(sums[len(inner) : len(rows)]):
            partial[whole, slot * LANES : (slot + 1) * LANES] = total

    def finish(start, count):
        found[start : start + count, :] = jnp.dot(left[:count, :], weights[...], preferred_element_type=jnp.float32)

    edge_on = edges_in_use(rg, chunk // STEP)
    all_dates(dates, group, places, rows, out_rows, az, edges, turned, edge_on, store, finish)


def outer_kernel(
    blocks, per, lines, chunk, group, own_edges, paired, other, partial, found, order, az, rg, weights, *refs
):
    pieces, (send, sums, halo, edges, turned, left, power) = refs[:blocks], refs[blocks:]
    dates = blocks * per
    half = dates // 2
    out_rows = lines // STEP
    cols = chunk // STEP
    wide = out_rows * cols
    me = lax.axis_index("date")
    inner, outer = kinds_of_rows(out_rows)
    split_at = len(inner) * cols

    odd = lax.axis_index("strip") % 2
    for block in range(blocks):
        scatter_halo(paired[block], order[block], lines, dates, per, halo.at[1 - odd])
        scatter_halo(other[block], order[block], lines, dates, per, halo.at[odd])
    below, above = halo.at[0], halo.at[1]
    lane = iota((dates, LANES), 1)
    turn = lane % (LANES // 2)
    for k in range(EDGE):
        at = (2 * HALO + k) * dates
        lower_part = pltpu.roll(below[at : at + dates, :], lines, 1)
        upper_part = pltpu.roll(above[at : at + dates, :], lines, 1)
        mine = own_edges[k * dates : (k + 1) * dates, :]
        value = jnp.where(turn < lines, mine, jnp.where(turn < lines + HALO, upper_part, lower_part))
        edges[k * dates : (k + 1) * dates, :] = value
    turn_edges(edges, turned, dates)
    places = [[(below, part * HALO + line) for part in range(2)] for line in range(HALO)]
    places += [None] * lines
    places += [[(above, part * HALO + line) for part in range(2)] for line in range(HALO)]

    def store(base, start, totals):
        at_rows = pl.ds(pl.multiple_of(start, 16), 16)
        whole = pl.ds(pl.multiple_of(base + start, 16), 16)
        for slot, total in enumerate(totals):
            if slot < len(outer):
                total += partial[whole, slot * LANES : (slot + 1) * LANES]
            store_split(left, at_rows, 2 * slot * LANES, total)

    def finish(start, count):
        rows = slice(start, start + count)
        sums[rows, split_at:] = jnp.dot(left[:count, :], weights[...], preferred_element_type=jnp.float32)

    sums[:, :split_at] = found[...]
    edge_on = edges_in_use(rg, cols)
    all_dates(dates, group, places, outer, out_rows, az, edges, turned, edge_on, store, finish)

    def row_at(date, part, later):
        if date < half:
            return (date * 2 + part) * dates + later
        later -= half
        return (dates + date - half) * dates + later // 8 * 16 + part * 8 + later % 8

    for date in range(dates):
        at_row = row_at(date, 0, date)
        power[date : date + 1, :] = sums[at_row : at_row + 1, :]
    scale = lax.rsqrt(power[...] + epsilon)
    power[...] = scale
    position = iota((dates, wide), 0)
    column = iota((dates, wide), 1)
    for date in range(dates):
        factor = scale * power[date : date + 1, :]
        values = []
        for part in range(2):
            if date < half:
                value = sums[row_at(date, part, 0) : row_at(date, part, 0) + dates, :]
            else:
                tiles = [row_at(date, part, half + tile) for tile in range(0, half, 8)]
                value = [jnp.zeros((half, wide), jnp.float32)] + [sums[row : row + 8, :] for row in tiles]
                value = jnp.concatenate(value, axis=0)
            values.append(jnp.where(position > date, value * factor, 0.0))
        largest = jnp.max(jnp.maximum(jnp.abs(values[0]), jnp.abs(values[1])), axis=1, keepdims=True)
        level = jnp.floor(jnp.log(largest) * (LEVELS / LOG_2)) + 1.0
        level = jnp.clip(level, LOWEST, HIGHEST)
        codes = [jnp.floor(value * (jnp.exp(level * (-LOG_2 / LEVELS)) * TOP) + 0.5) for value in values]
        header = jnp.sum(jnp.where(position == column, level, 0.0), axis=0, keepdims=True)
        codes[0] = jnp.where(position == 0, header, codes[0])
        for part, code in enumerate(codes):
            start = ((date // per * 2 + part) * per + date % per) * dates
            send[start : start + dates, :] = code.astype(jnp.int32).astype(jnp.int16)
    count = 2 * per * dates
    for piece, k in zip(pieces, partners(blocks)):
        piece[...] = send[pl.ds(pl.multiple_of(order[me ^ k] * count, 16), count), :]


def join_kernel(blocks, per, out_rows, cols, order, *refs):
    pieces, (out, recv, halves, placed, done) = refs[:blocks], refs[blocks:]
    dates = blocks * per
    own_rows = per * out_rows
    chosen = [[jnp.broadcast_to(order[b : b + 1, :] == r, (own_rows, LANES)) for r in range(blocks)] for b in range(blocks)]
    wide = out_rows * cols
    per_tile = LANES // cols
    me = lax.axis_index("date")
    lane = iota((dates, LANES), 1) // cols
    position = iota((dates, wide), 0)
    column = iota((dates, wide), 1)
    row_order = sum(kinds_of_rows(out_rows), [])
    for piece, k in zip(pieces, partners(blocks)):
        recv[me ^ k] = piece[...]
    factors = [[None] * blocks for _ in range(per)]
    copies = []
    for step in range(2 * per):
        values = []
        for block in range(blocks):
            codes = recv[block, step * dates : (step + 1) * dates, :].astype(jnp.int32).astype(jnp.float32)
            if step < per:
                header = codes[:1]
                level = jnp.sum(jnp.where(position == column, header, 0.0), axis=1, keepdims=True)
                factors[step][block] = jnp.exp(level * (LOG_2 / LEVELS)) * (1.0 / TOP)
            values.append(jnp.where(position == 0, 0.0, codes * factors[step % per][block]))
        for d_tile in range(blocks // per_tile):
            for o_tile in range(out_rows // per_tile):
                tiles = [
                    values[d_tile * per_tile + d][:, o_tile * LANES : (o_tile + 1) * LANES] for d in range(per_tile)
                ]
                width = 1
                while width < per_tile:
                    swap = [None] * per_tile
                    upper = (lane // width) % 2 == 1
                    shift = width * cols
                    for a in range(per_tile):
                        if (a // width) % 2 == 0:
                            b = a + width
                            swap[a] = jnp.where(upper, pltpu.roll(tiles[b], shift, 1), tiles[a])
                            swap[b] = jnp.where(upper, tiles[b], pltpu.roll(tiles[a], LANES - shift, 1))
                    tiles = swap
                    width *= 2
                for o in range(per_tile):
                    for start in range(0, dates, 8):
                        at = start * out_rows + row_order[o_tile * per_tile + o]
                        halves[step, d_tile, pl.ds(at, 8, stride=out_rows), :] = tiles[o][start : start + 8]
            ranked = [halves[step, d_tile, r * own_rows : (r + 1) * own_rows, :] for r in range(blocks)]
            for block in range(blocks):
                found = ranked[0]
                for r in range(1, blocks):
                    found = jnp.where(chosen[block][r], ranked[r], found)
                placed[step, d_tile, block * own_rows : (block + 1) * own_rows, :] = found
            rows = slice(step * dates * out_rows, (step + 1) * dates * out_rows)
            target = out.at[rows, d_tile * LANES : (d_tile + 1) * LANES]
            copies.append(pltpu.make_async_copy(placed.at[step, d_tile], target, done.at[step, d_tile]))
            copies[-1].start()
    for copy in copies:
        copy.wait()


def decode(codes):
    values = codes.astype(jnp.float32)
    dates = codes.shape[3]
    factor = jnp.exp(values[:, 0, :, 0, :dates] * (LOG_2 / LEVELS)) * (1.0 / TOP)
    return (values * factor[:, None, :, :, None]).at[:, :, :, 0].set(0.0)


def on_device(slc, block_order, az_offset, rg_offset):
    blocks = lax.axis_size("date")
    strips = lax.axis_size("strip")
    per, lines, span = slc.shape[1:]
    dates = blocks * per
    chunk = span // blocks
    out_rows = lines // STEP
    cols = chunk // STEP
    wide = out_rows * cols
    date_rows = rows_of_date(lines)
    group = max(per, 256 // dates)
    me = lax.axis_index("date")

    edge_rows = per * GROUP
    piece = jax.ShapeDtypeStruct((per * date_rows, LANES), jnp.bfloat16)
    send = pl.pallas_call(
        functools.partial(pack_kernel, blocks, per, lines, chunk),
        out_shape=[piece] * blocks,
        in_specs=[VMEM],
        out_specs=[VMEM] * blocks,
        scratch_shapes=[
            pltpu.VMEM((blocks, per * date_rows, LANES), jnp.bfloat16),
            pltpu.VMEM((per * date_rows, span), jnp.float32),
        ],
        compiler_params=PARAMS,
        name="pack",
    )(slc)
    recv = swap_blocks(send)
    tiled = jnp.tile(lax.dynamic_slice_in_dim(rg_offset, me * cols, cols), out_rows)[None]
    kinds = kinds_of_rows(out_rows)
    depths = [(len(rows) + 2) * 2 * LANES for rows in kinds]
    weights = pl.pallas_call(
        functools.partial(weight_kernel, lines, chunk),
        out_shape=[
            jax.ShapeDtypeStruct((depth, len(rows) * cols), jnp.bfloat16) for depth, rows in zip(depths, kinds)
        ],
        in_specs=[SMEM, VMEM],
        out_specs=[VMEM] * 2,
        compiler_params=PARAMS,
        cost_estimate=pl.CostEstimate(flops=0, bytes_accessed=4 * 1024 * 1024, transcendentals=0),
        name="weights",
    )(az_offset, tiled)
    recv, weights = lax.optimization_barrier((recv, weights))

    edge = jax.ShapeDtypeStruct((blocks, halo_rows(per), LANES), jnp.bfloat16)
    to_pair, to_other = pl.pallas_call(
        functools.partial(gather_kernel, blocks, per, lines),
        out_shape=[edge] * 2,
        in_specs=[VMEM] * blocks,
        out_specs=[VMEM] * 2,
        scratch_shapes=[pltpu.VMEM((halo_rows(per), LANES), jnp.float32)],
        compiler_params=PARAMS,
        name="gather",
    )(*recv)

    def swaps(first):
        pairs = [(i, i + 1) for i in range(first, strips - 1, 2)]
        return pairs + [(target, source) for source, target in pairs]

    other = lax.ppermute(to_other, "strip", swaps(1))
    paired = lax.ppermute(to_pair, "strip", swaps(0))
    count = dates * dates * 3 // 2
    half_group = min(group, dates // 2)
    found, partial, own_edges = pl.pallas_call(
        functools.partial(inner_kernel, blocks, per, lines, chunk, group),
        out_shape=[
            jax.ShapeDtypeStruct((count, len(kinds[0]) * cols), jnp.float32),
            jax.ShapeDtypeStruct((count, len(kinds[1]) * LANES), jnp.float32),
            jax.ShapeDtypeStruct((EDGE * dates, LANES), jnp.float32),
        ],
        in_specs=[SMEM] * 3 + [VMEM] * (1 + blocks),
        out_specs=[VMEM] * 3,
        scratch_shapes=[
            pltpu.VMEM((date_rows * dates, LANES), jnp.float32),
            pltpu.VMEM((EDGE * dates, LANES), jnp.float32),
            pltpu.VMEM((half_group * 2 * dates, depths[0]), jnp.bfloat16),
        ],
        compiler_params=PARAMS,
        cost_estimate=pl.CostEstimate(flops=0, bytes_accessed=12 * 1024 * 1024, transcendentals=0),
        name="inner",
    )(block_order, az_offset, rg_offset, weights[0], *recv)
    pairs = pl.pallas_call(
        functools.partial(outer_kernel, blocks, per, lines, chunk, group),
        out_shape=[jax.ShapeDtypeStruct((2 * per * dates, wide), jnp.int16)] * blocks,
        in_specs=[VMEM] * 5 + [SMEM] * 3 + [VMEM],
        out_specs=[VMEM] * blocks,
        scratch_shapes=[
            pltpu.VMEM((dates * 2 * dates, wide), jnp.int16),
            pltpu.VMEM((count, wide), jnp.float32),
            pltpu.VMEM((2, GROUP * dates, LANES), jnp.float32),
            pltpu.VMEM((EDGE * dates, LANES), jnp.float32),
            pltpu.VMEM((EDGE * dates, LANES), jnp.float32),
            pltpu.VMEM((half_group * 2 * dates, depths[1]), jnp.bfloat16),
            pltpu.VMEM((dates, wide), jnp.float32),
        ],
        compiler_params=PARAMS,
        name="outer",
    )(own_edges, paired, other, partial, found, block_order, az_offset, rg_offset, weights[1])
    count = 2 * per * dates
    back = swap_blocks(pairs)
    if LANES % cols == 0 and out_rows * cols % LANES == 0 and blocks * cols % LANES == 0:
        out = pl.pallas_call(
            functools.partial(join_kernel, blocks, per, out_rows, cols),
            out_shape=jax.ShapeDtypeStruct((count * out_rows, blocks * cols), jnp.float32),
            in_specs=[VMEM] * (1 + blocks),
            out_specs=pl.BlockSpec(memory_space=pl.ANY),
            scratch_shapes=[
                pltpu.VMEM((blocks, count, wide), jnp.int16),
                pltpu.VMEM((2 * per, blocks * cols // LANES, dates * out_rows, LANES), jnp.float32),
                pltpu.VMEM((2 * per, blocks * cols // LANES, dates * out_rows, LANES), jnp.float32),
                pltpu.SemaphoreType.DMA((2 * per, blocks * cols // LANES)),
            ],
            compiler_params=PARAMS,
            name="join",
        )(jnp.broadcast_to(block_order[:, None], (blocks, LANES)), *back)
    else:
        place = [partners(blocks).index(k) for k in range(blocks)]
        back = jnp.stack([back[at] for at in place])[me ^ jnp.arange(blocks)]
        values = decode(back.reshape(blocks, 2, per, dates, wide))
        values = values.reshape(blocks, 2, per, blocks, per, wide)[:, :, :, block_order]
        values = values.reshape(blocks, count, out_rows, cols).transpose(1, 2, 0, 3)
        row_order = sum(kinds_of_rows(out_rows), [])
        out = jnp.stack([values[:, row_order.index(o)] for o in range(out_rows)], axis=1)
    return out.reshape(2, per, dates, out_rows, blocks * cols)


def solution(mesh):
    placed = (P(None, "date", "strip", None), P(), P("strip"), P())
    return jax.shard_map(
        on_device,
        mesh=mesh,
        in_specs=placed,
        out_specs=P(None, "date", None, "strip", None),
        check_vma=False,
    )
```

```python
import functools

import jax
import jax.numpy as jnp
from jax import lax
from jax.experimental import pallas as pl
from jax.experimental.pallas import tpu as pltpu
from jax.sharding import PartitionSpec as P

STEP = 4
HALO = 5
REACH = 2
EDGE = 4
LANES = 128
GROUP = 16
VMEM = pl.BlockSpec(memory_space=pltpu.VMEM)
SMEM = pl.BlockSpec(memory_space=pltpu.SMEM)
PARAMS = pltpu.CompilerParams(vmem_limit_bytes=48 * 1024 * 1024)

epsilon = 1e-06
LEVELS = 8.0
LOWEST, HIGHEST = -880.0, 64.0
TOP = 32760.0
LOG_2 = 0.6931471805599453


def iota(shape, dim):
    return lax.broadcasted_iota(jnp.int32, shape, dim)


def row_of(part, line, lines):
    if line < HALO:
        return part * HALO + line
    if line >= lines - HALO:
        return GROUP + part * HALO + line - (lines - HALO)
    middle = part * (lines - 2 * HALO) + line - HALO
    spare = GROUP - 2 * HALO - EDGE
    if middle < spare:
        return 2 * HALO + EDGE + middle
    if middle < 2 * spare:
        return GROUP + 2 * HALO + EDGE + middle - spare
    return 2 * GROUP + middle - 2 * spare


def place_of(date, row, per, date_rows):
    if row < GROUP:
        return date * GROUP + row
    if row < 2 * GROUP:
        return (per + date - 1) * GROUP + row
    return 2 * per * GROUP + date * (date_rows - 2 * GROUP) + row - 2 * GROUP


def rows_of_date(lines):
    return 2 * GROUP + 2 * (lines - 2 * HALO) - 2 * (GROUP - 2 * HALO - EDGE)


def runs(part, lines):
    found = []
    for line in range(lines):
        row = row_of(part, line, lines)
        if line and row == row_of(part, line - 1, lines) + 1 and row % GROUP:
            found[-1][1] += 1
        else:
            found.append([line, 1])
    return found


def partners(blocks):
    return [0] + sorted(range(1, blocks), key=lambda k: (k & 1, -k))


def swap_blocks(pieces):
    blocks = len(pieces)
    found = list(pieces)
    for at, k in enumerate(partners(blocks)):
        if k:
            found[at] = lax.ppermute(pieces[at], "date", [(i, i ^ k) for i in range(blocks)])
    return found


def pack_kernel(blocks, per, lines, chunk, slc, *refs):
    pieces, (send, stage) = refs[:blocks], refs[blocks:]
    me = lax.axis_index("date")
    date_rows = rows_of_date(lines)
    edge_rows = per * GROUP
    turn = 1 - lax.axis_index("strip") % 2
    span = blocks * chunk
    shape = (EDGE * blocks, span)
    place = iota(shape, 0) % EDGE
    wanted = iota(shape, 0) // EDGE * chunk + jnp.where(place < REACH, place - REACH, place - REACH + chunk)
    picks = (iota(shape, 1) == wanted).astype(jnp.bfloat16)
    lane = iota((EDGE * blocks, LANES), 1)
    edges = []
    for date in range(per):
        mine = jnp.zeros((EDGE * blocks, LANES), jnp.float32)
        for part in range(2):
            samples = slc[part, date]
            for first, count in runs(part, lines):
                at = place_of(date, row_of(part, first, lines), per, date_rows)
                stage[at : at + count, :] = samples[first : first + count].astype(jnp.float32)
            found = lax.dot_general(picks, samples, (((1,), (1,)), ((), ())), preferred_element_type=jnp.float32)
            found = jnp.concatenate([found, jnp.zeros((EDGE * blocks, LANES - lines), jnp.float32)], axis=1)
            mine += pltpu.roll(found, part * (LANES // 2), 1) if part else found
        edges.append(mine)
    for block in range(blocks):
        for date in range(per):
            for group in range(2):
                at = place_of(date, group * GROUP + 2 * HALO, per, date_rows)
                value = edges[date][block * EDGE : (block + 1) * EDGE]
                if chunk == LANES:
                    stage[at : at + EDGE, block * LANES : (block + 1) * LANES] = value
        if chunk == LANES:
            piece = stage[:, block * chunk : (block + 1) * chunk]
        else:
            piece = stage[:, block * chunk : (block + 1) * chunk]
            piece = jnp.concatenate([piece, jnp.zeros((per * date_rows, LANES - chunk), jnp.float32)], axis=1)
            row = iota((per * date_rows, LANES), 0)
            for date in range(per):
                for group in range(2):
                    at = place_of(date, group * GROUP + 2 * HALO, per, date_rows)
                    for k in range(EDGE):
                        value = edges[date][block * EDGE + k : block * EDGE + k + 1]
                        piece = jnp.where(row == at + k, value, piece)
        piece = piece.astype(jnp.bfloat16)
        send[block, pl.ds(pl.multiple_of(turn * edge_rows, 16), edge_rows), :] = piece[:edge_rows]
        send[block, pl.ds(pl.multiple_of((1 - turn) * edge_rows, 16), edge_rows), :] = piece[edge_rows : 2 * edge_rows]
        send[block, 2 * edge_rows :, :] = piece[2 * edge_rows :]
    for piece, k in zip(pieces, partners(blocks)):
        piece[...] = send[me ^ k]


def kinds_of_rows(out_rows):
    return list(range(2, out_rows - 2)), [0, 1, out_rows - 2, out_rows - 1]


def weight_kernel(lines, chunk, az, tiled, *weights):
    cols = chunk // STEP
    for rows, target in zip(kinds_of_rows(lines // STEP), weights):
        count = len(rows)
        depth = count * 2 * LANES
        shape = (LANES, count * cols)
        col = iota(shape, 1) % cols
        slot = iota(shape, 1) // cols
        box = jnp.abs(iota(shape, 0) - STEP * col - tiled[:, : count * cols]) <= REACH
        for o in range(count):
            mine = (box & (slot == o)).astype(jnp.bfloat16)
            target[2 * o * LANES : (2 * o + 1) * LANES, :] = mine
            target[(2 * o + 1) * LANES : (2 * o + 2) * LANES, :] = mine
        turn = iota(shape, 0) % (LANES // 2)
        line = jnp.where(turn < lines + HALO, turn + HALO, turn + HALO - LANES // 2)
        lower = jnp.zeros(shape, jnp.int32)
        for place, o in enumerate(rows):
            lower = jnp.where(slot == place, STEP * o + az[o], lower)
        window = (line >= lower) & (line <= lower + 2 * HALO)
        for side, edge_col in ((0, 0), (1, cols - 1)):
            mine = (window & (col == edge_col)).astype(jnp.bfloat16)
            for term in range(2):
                start = depth + (2 * side + term) * LANES
                target[start : start + LANES, :] = mine


def to_sublanes(source, first_row, date_stride, rows, block, dates, per, target):
    for date in range(per):
        at = first_row + date * date_stride
        if not isinstance(at, int):
            at = pl.multiple_of(at, 8)
        value = source[pl.ds(at, rows), :].astype(jnp.float32)
        for row in range(0, rows, 8):
            target[pl.ds(row * dates + block * per + date, 8, stride=dates), :] = value[row : row + 8]


def halo_rows(per):
    return per * 2 * HALO + EDGE


def gather_rows(recv, group, per, lines, target, stage):
    me = lax.axis_index("date")
    tail = 2 * HALO - 8
    for piece, k in zip(recv, partners(len(recv))):
        edges = jnp.zeros((EDGE, LANES), jnp.float32)
        for date in range(per):
            at = (group * per + date) * GROUP
            value = piece[at : at + GROUP].astype(jnp.float32)
            stage[date * 8 : date * 8 + 8, :] = value[:8]
            stage[per * 8 + date * tail : per * 8 + (date + 1) * tail, :] = value[8 : 2 * HALO]
            mine = value[2 * HALO : 2 * HALO + EDGE]
            edges += pltpu.roll(mine, date * lines, 1) if date else mine
        stage[per * 2 * HALO :, :] = edges
        target[me ^ k] = stage[...].astype(jnp.bfloat16)


def gather_kernel(blocks, per, lines, *refs):
    recv, (paired, stage) = refs[:blocks], refs[blocks:]
    gather_rows(recv, 0, per, lines, paired, stage)


def scatter_halo(source, block, lines, dates, per, target):
    value = source.astype(jnp.float32)
    tail = 2 * HALO - 8
    for date in range(per):
        place = block * per + date
        target[pl.ds(place, 8, stride=dates), :] = value[date * 8 : date * 8 + 8]
        rest = value[per * 8 + date * tail : per * 8 + (date + 1) * tail]
        target[pl.ds(8 * dates + place, tail, stride=dates), :] = rest
        mine = value[per * 2 * HALO :]
        mine = pltpu.roll(mine, LANES - date * lines, 1) if date else mine
        target[pl.ds(2 * HALO * dates + place, EDGE, stride=dates), :] = mine


def split(value):
    high = value.astype(jnp.bfloat16)
    return high, (value - high.astype(jnp.float32)).astype(jnp.bfloat16)


def plus(total, value):
    return value if total is None else total + value


def window_sums(product, rows, out_rows, az):
    quads = [None] * (out_rows + 1)
    for k in range(out_rows + 1):
        for line in range(STEP * k + 3, STEP * k + 7):
            if product[line] is not None:
                quads[k] = plus(quads[k], product[line])
    sums = []
    for o in rows:
        total = None
        for quad in (quads[o], quads[o + 1]):
            if quad is not None:
                total = plus(total, quad)
        for k in range(3):
            early, late = product[STEP * o + k], product[STEP * o + 11 + k]
            if early is None and late is None:
                continue
            early = jnp.zeros_like(late) if early is None else early
            late = jnp.zeros_like(early) if late is None else late
            total = plus(total, jnp.where(az[o] <= k, early, late))
        sums.append(total)
    return sums


def products(places, date, first, count, dates):
    real, imag = [], []
    for line in places:
        if line is None:
            real.append(None)
            imag.append(None)
            continue
        (ref, at_re), (_, at_im) = line
        re_i, im_i = (ref[pl.ds(row * dates + date, 1), :] for row in (at_re, at_im))
        re_j, im_j = (ref[row * dates + first : row * dates + first + count, :] for row in (at_re, at_im))
        real.append(re_i * re_j + im_i * im_j)
        imag.append(im_i * re_j - re_i * im_j)
    return real, imag


def store_split(target, rows, start, value):
    upper, rest = split(value)
    target[rows, start : start + LANES] = upper
    target[rows, start + LANES : start + 2 * LANES] = rest


def edge_sums(edges, own, date, first, count, dates, edge_on):
    sums = []
    for side in range(2):
        total = jnp.zeros((count, LANES), jnp.float32)
        for edge in (2 * side, 2 * side + 1):
            others = edges[edge * dates + first : edge * dates + first + count, :]
            total += jnp.where(edge_on[edge], own[pl.ds(edge * dates + date, 1), :] * others, 0.0)
        sums.append(total)
    return sums


def half_of_dates(late_half, dates, group, places, rows, out_rows, az, edges, turned, edge_on, store, finish):
    half = dates // 2
    group = min(group, half)

    def sums_of(date, first, count):
        found = []
        for part, product in enumerate(products(places, date, first, count, dates)):
            sums = window_sums(product, rows, out_rows, az)
            found.append(sums + edge_sums(edges, turned if part else edges, date, first, count, dates, edge_on))
        return found

    def early(first_date, step, carry):
        for tile in range(dates // 16):
            for part, sums in enumerate(sums_of(first_date + step, tile * 16, 16)):
                store(first_date * 2 * dates, step * 2 * dates + part * dates + tile * 16, sums)
        return carry

    def late(first_date, step, carry):
        for tile in range(half // 8):
            real, imag = sums_of(half + first_date + step, half + tile * 8, 8)
            both = [jnp.concatenate([re, im], axis=0) for re, im in zip(real, imag)]
            store(first_date * dates, step * dates + tile * 16, both)
        return carry

    body, width = (late, dates) if late_half else (early, 2 * dates)
    for first_date in range(0, half, group):
        lax.fori_loop(0, group, functools.partial(body, first_date), 0)
        finish(first_date * width, group * width)


def turn_edges(edges, turned, dates):
    lane = iota((dates, LANES), 1)
    for k in range(EDGE):
        value = pltpu.roll(edges[k * dates : (k + 1) * dates, :], LANES // 2, 1)
        turned[k * dates : (k + 1) * dates, :] = jnp.where(lane < LANES // 2, value, -value)


def edges_in_use(rg, cols):
    me = lax.axis_index("date")
    first = rg[me * cols]
    last = rg[me * cols + cols - 1]
    return first <= 0, first <= 1, last >= 2, last >= 3


def own_sums(late_half, blocks, per, lines, chunk, group, az, rg, weights, x, found, partial, turned, left):
    dates = blocks * per
    out_rows = lines // STEP
    inner, outer = kinds_of_rows(out_rows)
    edges = x.at[2 * HALO * dates : (2 * HALO + EDGE) * dates]
    turn_edges(edges, turned, dates)
    places = [None] * HALO
    places += [[(x, row_of(part, line, lines)) for part in range(2)] for line in range(lines)]
    places += [None] * HALO
    rows = inner + outer

    def store(base, start, sums):
        at_rows = pl.ds(pl.multiple_of(start, 16), 16)
        whole = pl.ds(pl.multiple_of(base + start, 16), 16)
        for slot, total in enumerate(sums[: len(inner)] + sums[len(rows) :]):
            store_split(left, at_rows, 2 * slot * LANES, total)
        for slot, total in enumerate(sums[len(inner) : len(rows)]):
            partial[whole, slot * LANES : (slot + 1) * LANES] = total

    def finish(start, count):
        found[start : start + count, :] = jnp.dot(left[:count, :], weights[...], preferred_element_type=jnp.float32)

    edge_on = edges_in_use(rg, chunk // STEP)
    half_of_dates(late_half, dates, group, places, rows, out_rows, az, edges, turned, edge_on, store, finish)


def late_kernel(blocks, per, lines, chunk, group, order, az, rg, weights, *refs):
    recv, (x, other, found, partial, stage, turned, left) = refs[:blocks], refs[blocks:]
    dates = blocks * per
    date_rows = rows_of_date(lines)
    edge_rows = per * GROUP
    me = lax.axis_index("date")
    swap = 1 - lax.axis_index("strip") % 2
    rest = date_rows - 2 * GROUP
    gather_rows(recv, 1, per, lines, other, stage)
    for piece, k in zip(recv, partners(blocks)):
        block = order[me ^ k]
        to_sublanes(piece, swap * edge_rows, GROUP, GROUP, block, dates, per, x)
        to_sublanes(piece, (1 - swap) * edge_rows, GROUP, GROUP, block, dates, per, x.at[GROUP * dates :])
        to_sublanes(piece, 2 * edge_rows, rest, rest, block, dates, per, x.at[2 * GROUP * dates :])
    own_sums(True, blocks, per, lines, chunk, group, az, rg, weights, x, found, partial, turned, left)


def early_kernel(blocks, per, lines, chunk, group, az, rg, weights, x, found, partial, turned, left):
    own_sums(False, blocks, per, lines, chunk, group, az, rg, weights, x, found, partial, turned, left)


def outer_kernel(
    blocks, per, lines, chunk, group, x, paired, other, early, late, early_found, late_found, order, az, rg, weights, *refs
):
    pieces, (send, sums, halo, edges, turned, left, power) = refs[:blocks], refs[blocks:]
    dates = blocks * per
    half = dates // 2
    out_rows = lines // STEP
    cols = chunk // STEP
    wide = out_rows * cols
    me = lax.axis_index("date")
    inner, outer = kinds_of_rows(out_rows)
    split_at = len(inner) * cols

    odd = lax.axis_index("strip") % 2
    for block in range(blocks):
        scatter_halo(paired[block], order[block], lines, dates, per, halo.at[1 - odd])
        scatter_halo(other[block], order[block], lines, dates, per, halo.at[odd])
    below, above = halo.at[0], halo.at[1]
    lane = iota((dates, LANES), 1)
    turn = lane % (LANES // 2)
    for k in range(EDGE):
        at = (2 * HALO + k) * dates
        lower_part = pltpu.roll(below[at : at + dates, :], lines, 1)
        upper_part = pltpu.roll(above[at : at + dates, :], lines, 1)
        value = jnp.where(turn < lines, x[at : at + dates, :], jnp.where(turn < lines + HALO, upper_part, lower_part))
        edges[k * dates : (k + 1) * dates, :] = value
    turn_edges(edges, turned, dates)
    places = [[(below, part * HALO + line) for part in range(2)] for line in range(HALO)]
    places += [None] * lines
    places += [[(above, part * HALO + line) for part in range(2)] for line in range(HALO)]

    edge_on = edges_in_use(rg, cols)
    for late_half, partial, found in ((False, early, early_found), (True, late, late_found)):
        offset = dates * dates * late_half

        def store(base, start, totals):
            at_rows = pl.ds(pl.multiple_of(start, 16), 16)
            whole = pl.ds(pl.multiple_of(base + start, 16), 16)
            for slot, total in enumerate(totals):
                if slot < len(outer):
                    total += partial[whole, slot * LANES : (slot + 1) * LANES]
                store_split(left, at_rows, 2 * slot * LANES, total)

        def finish(start, count):
            rows = slice(offset + start, offset + start + count)
            sums[rows, :split_at] = found[start : start + count, :]
            sums[rows, split_at:] = jnp.dot(left[:count, :], weights[...], preferred_element_type=jnp.float32)

        half_of_dates(late_half, dates, group, places, outer, out_rows, az, edges, turned, edge_on, store, finish)

    def row_at(date, part, later):
        if date < half:
            return (date * 2 + part) * dates + later
        later -= half
        return (dates + date - half) * dates + later // 8 * 16 + part * 8 + later % 8

    for date in range(dates):
        at_row = row_at(date, 0, date)
        power[date : date + 1, :] = sums[at_row : at_row + 1, :]
    scale = lax.rsqrt(power[...] + epsilon)
    power[...] = scale
    position = iota((dates, wide), 0)
    column = iota((dates, wide), 1)
    for date in range(dates):
        factor = scale * power[date : date + 1, :]
        values = []
        for part in range(2):
            if date < half:
                value = sums[row_at(date, part, 0) : row_at(date, part, 0) + dates, :]
            else:
                tiles = [row_at(date, part, half + tile) for tile in range(0, half, 8)]
                value = [jnp.zeros((half, wide), jnp.float32)] + [sums[row : row + 8, :] for row in tiles]
                value = jnp.concatenate(value, axis=0)
            values.append(jnp.where(position > date, value * factor, 0.0))
        largest = jnp.max(jnp.maximum(jnp.abs(values[0]), jnp.abs(values[1])), axis=1, keepdims=True)
        level = jnp.floor(jnp.log(largest) * (LEVELS / LOG_2)) + 1.0
        level = jnp.clip(level, LOWEST, HIGHEST)
        codes = [jnp.floor(value * (jnp.exp(level * (-LOG_2 / LEVELS)) * TOP) + 0.5) for value in values]
        header = jnp.sum(jnp.where(position == column, level, 0.0), axis=0, keepdims=True)
        codes[0] = jnp.where(position == 0, header, codes[0])
        for part, code in enumerate(codes):
            start = ((date // per * 2 + part) * per + date % per) * dates
            send[start : start + dates, :] = code.astype(jnp.int32).astype(jnp.int16)
    count = 2 * per * dates
    for piece, k in zip(pieces, partners(blocks)):
        piece[...] = send[pl.ds(pl.multiple_of(order[me ^ k] * count, 16), count), :]


def join_kernel(blocks, per, out_rows, cols, order, *refs):
    pieces, (out, recv, halves, placed, done) = refs[:blocks], refs[blocks:]
    dates = blocks * per
    own_rows = per * out_rows
    chosen = [[jnp.broadcast_to(order[b : b + 1, :] == r, (own_rows, LANES)) for r in range(blocks)] for b in range(blocks)]
    wide = out_rows * cols
    per_tile = LANES // cols
    me = lax.axis_index("date")
    lane = iota((dates, LANES), 1) // cols
    position = iota((dates, wide), 0)
    column = iota((dates, wide), 1)
    row_order = sum(kinds_of_rows(out_rows), [])
    for piece, k in zip(pieces, partners(blocks)):
        recv[me ^ k] = piece[...]
    factors = [[None] * blocks for _ in range(per)]
    copies = []
    for step in range(2 * per):
        values = []
        for block in range(blocks):
            codes = recv[block, step * dates : (step + 1) * dates, :].astype(jnp.int32).astype(jnp.float32)
            if step < per:
                header = codes[:1]
                level = jnp.sum(jnp.where(position == column, header, 0.0), axis=1, keepdims=True)
                factors[step][block] = jnp.exp(level * (LOG_2 / LEVELS)) * (1.0 / TOP)
            values.append(jnp.where(position == 0, 0.0, codes * factors[step % per][block]))
        for d_tile in range(blocks // per_tile):
            for o_tile in range(out_rows // per_tile):
                tiles = [
                    values[d_tile * per_tile + d][:, o_tile * LANES : (o_tile + 1) * LANES] for d in range(per_tile)
                ]
                width = 1
                while width < per_tile:
                    swap = [None] * per_tile
                    upper = (lane // width) % 2 == 1
                    shift = width * cols
                    for a in range(per_tile):
                        if (a // width) % 2 == 0:
                            b = a + width
                            swap[a] = jnp.where(upper, pltpu.roll(tiles[b], shift, 1), tiles[a])
                            swap[b] = jnp.where(upper, tiles[b], pltpu.roll(tiles[a], LANES - shift, 1))
                    tiles = swap
                    width *= 2
                for o in range(per_tile):
                    for start in range(0, dates, 8):
                        at = start * out_rows + row_order[o_tile * per_tile + o]
                        halves[step, d_tile, pl.ds(at, 8, stride=out_rows), :] = tiles[o][start : start + 8]
            ranked = [halves[step, d_tile, r * own_rows : (r + 1) * own_rows, :] for r in range(blocks)]
            for block in range(blocks):
                found = ranked[0]
                for r in range(1, blocks):
                    found = jnp.where(chosen[block][r], ranked[r], found)
                placed[step, d_tile, block * own_rows : (block + 1) * own_rows, :] = found
            rows = slice(step * dates * out_rows, (step + 1) * dates * out_rows)
            target = out.at[rows, d_tile * LANES : (d_tile + 1) * LANES]
            copies.append(pltpu.make_async_copy(placed.at[step, d_tile], target, done.at[step, d_tile]))
            copies[-1].start()
    for copy in copies:
        copy.wait()


def decode(codes):
    values = codes.astype(jnp.float32)
    dates = codes.shape[3]
    factor = jnp.exp(values[:, 0, :, 0, :dates] * (LOG_2 / LEVELS)) * (1.0 / TOP)
    return (values * factor[:, None, :, :, None]).at[:, :, :, 0].set(0.0)


def on_device(slc, block_order, az_offset, rg_offset):
    blocks = lax.axis_size("date")
    strips = lax.axis_size("strip")
    per, lines, span = slc.shape[1:]
    dates = blocks * per
    chunk = span // blocks
    out_rows = lines // STEP
    cols = chunk // STEP
    wide = out_rows * cols
    date_rows = rows_of_date(lines)
    group = max(per, 256 // dates)
    me = lax.axis_index("date")

    edge_rows = per * GROUP
    piece = jax.ShapeDtypeStruct((per * date_rows, LANES), jnp.bfloat16)
    send = pl.pallas_call(
        functools.partial(pack_kernel, blocks, per, lines, chunk),
        out_shape=[piece] * blocks,
        in_specs=[VMEM],
        out_specs=[VMEM] * blocks,
        scratch_shapes=[
            pltpu.VMEM((blocks, per * date_rows, LANES), jnp.bfloat16),
            pltpu.VMEM((per * date_rows, span), jnp.float32),
        ],
        compiler_params=PARAMS,
        name="pack",
    )(slc)
    recv = swap_blocks(send)
    tiled = jnp.tile(lax.dynamic_slice_in_dim(rg_offset, me * cols, cols), out_rows)[None]
    kinds = kinds_of_rows(out_rows)
    depths = [(len(rows) + 2) * 2 * LANES for rows in kinds]
    weights = pl.pallas_call(
        functools.partial(weight_kernel, lines, chunk),
        out_shape=[
            jax.ShapeDtypeStruct((depth, len(rows) * cols), jnp.bfloat16) for depth, rows in zip(depths, kinds)
        ],
        in_specs=[SMEM, VMEM],
        out_specs=[VMEM] * 2,
        compiler_params=PARAMS,
        cost_estimate=pl.CostEstimate(flops=0, bytes_accessed=4 * 1024 * 1024, transcendentals=0),
        name="weights",
    )(az_offset, tiled)
    recv, weights = lax.optimization_barrier((recv, weights))

    edge = jax.ShapeDtypeStruct((blocks, halo_rows(per), LANES), jnp.bfloat16)
    to_pair = pl.pallas_call(
        functools.partial(gather_kernel, blocks, per, lines),
        out_shape=edge,
        in_specs=[VMEM] * blocks,
        out_specs=VMEM,
        scratch_shapes=[pltpu.VMEM((halo_rows(per), LANES), jnp.float32)],
        compiler_params=PARAMS,
        name="gather",
    )(*recv)

    def swaps(first):
        pairs = [(i, i + 1) for i in range(first, strips - 1, 2)]
        return pairs + [(target, source) for source, target in pairs]

    paired = lax.ppermute(to_pair, "strip", swaps(0))
    half_group = min(group, dates // 2)

    def sums_of(count):
        return [
            jax.ShapeDtypeStruct((count, len(kinds[0]) * cols), jnp.float32),
            jax.ShapeDtypeStruct((count, len(kinds[1]) * LANES), jnp.float32),
        ]

    def scratch(width):
        return [
            pltpu.VMEM((EDGE * dates, LANES), jnp.float32),
            pltpu.VMEM((half_group * width * dates, depths[0]), jnp.bfloat16),
        ]

    x, to_other, late_found, late = pl.pallas_call(
        functools.partial(late_kernel, blocks, per, lines, chunk, group),
        out_shape=[jax.ShapeDtypeStruct((date_rows * dates, LANES), jnp.float32), edge] + sums_of(dates * dates // 2),
        in_specs=[SMEM] * 3 + [VMEM] * (1 + blocks),
        out_specs=[VMEM] * 4,
        scratch_shapes=[pltpu.VMEM((halo_rows(per), LANES), jnp.float32)] + scratch(1),
        compiler_params=PARAMS,
        cost_estimate=pl.CostEstimate(flops=0, bytes_accessed=6 * 1024 * 1024, transcendentals=0),
        name="late",
    )(block_order, az_offset, rg_offset, weights[0], *recv)
    other = lax.ppermute(to_other, "strip", swaps(1))
    early_found, early = pl.pallas_call(
        functools.partial(early_kernel, blocks, per, lines, chunk, group),
        out_shape=sums_of(dates * dates),
        in_specs=[SMEM] * 2 + [VMEM] * 2,
        out_specs=[VMEM] * 2,
        scratch_shapes=scratch(2),
        compiler_params=PARAMS,
        cost_estimate=pl.CostEstimate(flops=0, bytes_accessed=8 * 1024 * 1024, transcendentals=0),
        name="early",
    )(az_offset, rg_offset, weights[0], x)
    count = dates * dates * 3 // 2
    pairs = pl.pallas_call(
        functools.partial(outer_kernel, blocks, per, lines, chunk, group),
        out_shape=[jax.ShapeDtypeStruct((2 * per * dates, wide), jnp.int16)] * blocks,
        in_specs=[VMEM] * 7 + [SMEM] * 3 + [VMEM],
        out_specs=[VMEM] * blocks,
        scratch_shapes=[
            pltpu.VMEM((dates * 2 * dates, wide), jnp.int16),
            pltpu.VMEM((count, wide), jnp.float32),
            pltpu.VMEM((2, GROUP * dates, LANES), jnp.float32),
            pltpu.VMEM((EDGE * dates, LANES), jnp.float32),
            pltpu.VMEM((EDGE * dates, LANES), jnp.float32),
            pltpu.VMEM((half_group * 2 * dates, depths[1]), jnp.bfloat16),
            pltpu.VMEM((dates, wide), jnp.float32),
        ],
        compiler_params=PARAMS,
        name="outer",
    )(x, paired, other, early, late, early_found, late_found, block_order, az_offset, rg_offset, weights[1])
    count = 2 * per * dates
    back = swap_blocks(pairs)
    if LANES % cols == 0 and out_rows * cols % LANES == 0 and blocks * cols % LANES == 0:
        out = pl.pallas_call(
            functools.partial(join_kernel, blocks, per, out_rows, cols),
            out_shape=jax.ShapeDtypeStruct((count * out_rows, blocks * cols), jnp.float32),
            in_specs=[VMEM] * (1 + blocks),
            out_specs=pl.BlockSpec(memory_space=pl.ANY),
            scratch_shapes=[
                pltpu.VMEM((blocks, count, wide), jnp.int16),
                pltpu.VMEM((2 * per, blocks * cols // LANES, dates * out_rows, LANES), jnp.float32),
                pltpu.VMEM((2 * per, blocks * cols // LANES, dates * out_rows, LANES), jnp.float32),
                pltpu.SemaphoreType.DMA((2 * per, blocks * cols // LANES)),
            ],
            compiler_params=PARAMS,
            name="join",
        )(jnp.broadcast_to(block_order[:, None], (blocks, LANES)), *back)
    else:
        place = [partners(blocks).index(k) for k in range(blocks)]
        back = jnp.stack([back[at] for at in place])[me ^ jnp.arange(blocks)]
        values = decode(back.reshape(blocks, 2, per, dates, wide))
        values = values.reshape(blocks, 2, per, blocks, per, wide)[:, :, :, block_order]
        values = values.reshape(blocks, count, out_rows, cols).transpose(1, 2, 0, 3)
        row_order = sum(kinds_of_rows(out_rows), [])
        out = jnp.stack([values[:, row_order.index(o)] for o in range(out_rows)], axis=1)
    return out.reshape(2, per, dates, out_rows, blocks * cols)


def solution(mesh):
    placed = (P(None, "date", "strip", None), P(), P("strip"), P())
    return jax.shard_map(
        on_device,
        mesh=mesh,
        in_specs=placed,
        out_specs=P(None, "date", None, "strip", None),
        check_vma=False,
    )
```

```python
import functools

import jax
import jax.numpy as jnp
from jax import lax
from jax.experimental import pallas as pl
from jax.experimental.pallas import tpu as pltpu
from jax.sharding import PartitionSpec as P

STEP = 4
HALO = 5
REACH = 2
EDGE = 4
LANES = 128
GROUP = 16
VMEM = pl.BlockSpec(memory_space=pltpu.VMEM)
SMEM = pl.BlockSpec(memory_space=pltpu.SMEM)
PARAMS = pltpu.CompilerParams(vmem_limit_bytes=48 * 1024 * 1024)

epsilon = 1e-06
LEVELS = 8.0
LOWEST, HIGHEST = -880.0, 64.0
TOP = 32760.0
LOG_2 = 0.6931471805599453


def iota(shape, dim):
    return lax.broadcasted_iota(jnp.int32, shape, dim)


def row_of(part, line, lines):
    if line < HALO:
        return part * HALO + line
    if line >= lines - HALO:
        return GROUP + part * HALO + line - (lines - HALO)
    middle = part * (lines - 2 * HALO) + line - HALO
    spare = GROUP - 2 * HALO - EDGE
    if middle < spare:
        return 2 * HALO + EDGE + middle
    if middle < 2 * spare:
        return GROUP + 2 * HALO + EDGE + middle - spare
    return 2 * GROUP + middle - 2 * spare


def place_of(date, row, per, date_rows):
    if row < GROUP:
        return date * GROUP + row
    if row < 2 * GROUP:
        return (per + date - 1) * GROUP + row
    return 2 * per * GROUP + date * (date_rows - 2 * GROUP) + row - 2 * GROUP


def rows_of_date(lines):
    return 2 * GROUP + 2 * (lines - 2 * HALO) - 2 * (GROUP - 2 * HALO - EDGE)


def runs(part, lines):
    found = []
    for line in range(lines):
        row = row_of(part, line, lines)
        if line and row == row_of(part, line - 1, lines) + 1 and row % GROUP:
            found[-1][1] += 1
        else:
            found.append([line, 1])
    return found


def partners(blocks):
    even = sorted(range(2, blocks, 2), key=lambda k: (bin(k).count("1"), -k))
    odd = sorted(range(3, blocks, 2), key=lambda k: (-bin(k).count("1"), -k))
    return [0] + even + [1] + odd


def swap_blocks(pieces):
    blocks = len(pieces)
    found = list(pieces)
    for at, k in enumerate(partners(blocks)):
        if k:
            found[at] = lax.ppermute(pieces[at], "date", [(i, i ^ k) for i in range(blocks)])
    return found


def pack_kernel(blocks, per, lines, chunk, slc, *refs):
    pieces, (send, stage) = refs[:blocks], refs[blocks:]
    me = lax.axis_index("date")
    date_rows = rows_of_date(lines)
    edge_rows = per * GROUP
    turn = 1 - lax.axis_index("strip") % 2
    span = blocks * chunk
    shape = (EDGE * blocks, span)
    place = iota(shape, 0) % EDGE
    wanted = iota(shape, 0) // EDGE * chunk + jnp.where(place < REACH, place - REACH, place - REACH + chunk)
    picks = (iota(shape, 1) == wanted).astype(jnp.bfloat16)
    lane = iota((EDGE * blocks, LANES), 1)
    edges = []
    for date in range(per):
        mine = jnp.zeros((EDGE * blocks, LANES), jnp.float32)
        for part in range(2):
            samples = slc[part, date]
            for first, count in runs(part, lines):
                at = place_of(date, row_of(part, first, lines), per, date_rows)
                stage[at : at + count, :] = samples[first : first + count].astype(jnp.float32)
            found = lax.dot_general(picks, samples, (((1,), (1,)), ((), ())), preferred_element_type=jnp.float32)
            found = jnp.concatenate([found, jnp.zeros((EDGE * blocks, LANES - lines), jnp.float32)], axis=1)
            mine += pltpu.roll(found, part * (LANES // 2), 1) if part else found
        edges.append(mine)
    for block in range(blocks):
        for date in range(per):
            for group in range(2):
                at = place_of(date, group * GROUP + 2 * HALO, per, date_rows)
                value = edges[date][block * EDGE : (block + 1) * EDGE]
                if chunk == LANES:
                    stage[at : at + EDGE, block * LANES : (block + 1) * LANES] = value
        if chunk == LANES:
            piece = stage[:, block * chunk : (block + 1) * chunk]
        else:
            piece = stage[:, block * chunk : (block + 1) * chunk]
            piece = jnp.concatenate([piece, jnp.zeros((per * date_rows, LANES - chunk), jnp.float32)], axis=1)
            row = iota((per * date_rows, LANES), 0)
            for date in range(per):
                for group in range(2):
                    at = place_of(date, group * GROUP + 2 * HALO, per, date_rows)
                    for k in range(EDGE):
                        value = edges[date][block * EDGE + k : block * EDGE + k + 1]
                        piece = jnp.where(row == at + k, value, piece)
        piece = piece.astype(jnp.bfloat16)
        send[block, pl.ds(pl.multiple_of(turn * edge_rows, 16), edge_rows), :] = piece[:edge_rows]
        send[block, pl.ds(pl.multiple_of((1 - turn) * edge_rows, 16), edge_rows), :] = piece[edge_rows : 2 * edge_rows]
        send[block, 2 * edge_rows :, :] = piece[2 * edge_rows :]
    for piece, k in zip(pieces, partners(blocks)):
        piece[...] = send[me ^ k]


def kinds_of_rows(out_rows):
    return list(range(2, out_rows - 2)), [0, 1, out_rows - 2, out_rows - 1]


def weight_kernel(lines, chunk, az, tiled, *weights):
    cols = chunk // STEP
    for rows, target in zip(kinds_of_rows(lines // STEP), weights):
        count = len(rows)
        depth = count * 2 * LANES
        shape = (LANES, count * cols)
        col = iota(shape, 1) % cols
        slot = iota(shape, 1) // cols
        box = jnp.abs(iota(shape, 0) - STEP * col - tiled[:, : count * cols]) <= REACH
        for o in range(count):
            mine = (box & (slot == o)).astype(jnp.bfloat16)
            target[2 * o * LANES : (2 * o + 1) * LANES, :] = mine
            target[(2 * o + 1) * LANES : (2 * o + 2) * LANES, :] = mine
        turn = iota(shape, 0) % (LANES // 2)
        line = jnp.where(turn < lines + HALO, turn + HALO, turn + HALO - LANES // 2)
        lower = jnp.zeros(shape, jnp.int32)
        for place, o in enumerate(rows):
            lower = jnp.where(slot == place, STEP * o + az[o], lower)
        window = (line >= lower) & (line <= lower + 2 * HALO)
        for side, edge_col in ((0, 0), (1, cols - 1)):
            mine = (window & (col == edge_col)).astype(jnp.bfloat16)
            for term in range(2):
                start = depth + (2 * side + term) * LANES
                target[start : start + LANES, :] = mine


def to_sublanes(source, first_row, date_stride, rows, block, dates, per, target):
    for date in range(per):
        at = first_row + date * date_stride
        if not isinstance(at, int):
            at = pl.multiple_of(at, 8)
        value = source[pl.ds(at, rows), :].astype(jnp.float32)
        for row in range(0, rows, 8):
            target[pl.ds(row * dates + block * per + date, 8, stride=dates), :] = value[row : row + 8]


def halo_rows(per):
    return per * 2 * HALO + EDGE


def gather_kernel(blocks, per, lines, *refs):
    recv, (paired, other, stage) = refs[:blocks], refs[blocks:]
    me = lax.axis_index("date")
    tail = 2 * HALO - 8
    for piece, k in zip(recv, partners(blocks)):
        for group, target in enumerate((paired, other)):
            edges = jnp.zeros((EDGE, LANES), jnp.float32)
            for date in range(per):
                at = (group * per + date) * GROUP
                value = piece[at : at + GROUP].astype(jnp.float32)
                stage[date * 8 : date * 8 + 8, :] = value[:8]
                stage[per * 8 + date * tail : per * 8 + (date + 1) * tail, :] = value[8 : 2 * HALO]
                mine = value[2 * HALO : 2 * HALO + EDGE]
                edges += pltpu.roll(mine, date * lines, 1) if date else mine
            stage[per * 2 * HALO :, :] = edges
            target[me ^ k] = stage[...].astype(jnp.bfloat16)


def scatter_halo(source, block, lines, dates, per, target):
    value = source.astype(jnp.float32)
    tail = 2 * HALO - 8
    for date in range(per):
        place = block * per + date
        target[pl.ds(place, 8, stride=dates), :] = value[date * 8 : date * 8 + 8]
        rest = value[per * 8 + date * tail : per * 8 + (date + 1) * tail]
        target[pl.ds(8 * dates + place, tail, stride=dates), :] = rest
        mine = value[per * 2 * HALO :]
        mine = pltpu.roll(mine, LANES - date * lines, 1) if date else mine
        target[pl.ds(2 * HALO * dates + place, EDGE, stride=dates), :] = mine


def split(value):
    high = value.astype(jnp.bfloat16)
    return high, (value - high.astype(jnp.float32)).astype(jnp.bfloat16)


def plus(total, value):
    return value if total is None else total + value


def window_sums(product, rows, out_rows, az):
    quads = [None] * (out_rows + 1)
    for k in range(out_rows + 1):
        for line in range(STEP * k + 3, STEP * k + 7):
            if product[line] is not None:
                quads[k] = plus(quads[k], product[line])
    sums = []
    for o in rows:
        total = None
        for quad in (quads[o], quads[o + 1]):
            if quad is not None:
                total = plus(total, quad)
        for k in range(3):
            early, late = product[STEP * o + k], product[STEP * o + 11 + k]
            if early is None and late is None:
                continue
            early = jnp.zeros_like(late) if early is None else early
            late = jnp.zeros_like(early) if late is None else late
            total = plus(total, jnp.where(az[o] <= k, early, late))
        sums.append(total)
    return sums


def products(places, date, first, count, dates):
    real, imag = [], []
    for line in places:
        if line is None:
            real.append(None)
            imag.append(None)
            continue
        (ref, at_re), (_, at_im) = line
        re_i, im_i = (ref[pl.ds(row * dates + date, 1), :] for row in (at_re, at_im))
        re_j, im_j = (ref[row * dates + first : row * dates + first + count, :] for row in (at_re, at_im))
        real.append(re_i * re_j + im_i * im_j)
        imag.append(im_i * re_j - re_i * im_j)
    return real, imag


def store_split(target, rows, start, value):
    upper, rest = split(value)
    target[rows, start : start + LANES] = upper
    target[rows, start + LANES : start + 2 * LANES] = rest


def edge_sums(edges, own, date, first, count, dates, edge_on):
    sums = []
    for side in range(2):
        total = jnp.zeros((count, LANES), jnp.float32)
        for edge in (2 * side, 2 * side + 1):
            others = edges[edge * dates + first : edge * dates + first + count, :]
            total += jnp.where(edge_on[edge], own[pl.ds(edge * dates + date, 1), :] * others, 0.0)
        sums.append(total)
    return sums


def all_dates(dates, group, places, rows, out_rows, az, edges, turned, edge_on, store, finish):
    half = dates // 2
    group = min(group, half)

    def sums_of(date, first, count):
        found = []
        for part, product in enumerate(products(places, date, first, count, dates)):
            sums = window_sums(product, rows, out_rows, az)
            found.append(sums + edge_sums(edges, turned if part else edges, date, first, count, dates, edge_on))
        return found

    def early(first_date, step, carry):
        for tile in range(dates // 16):
            for part, sums in enumerate(sums_of(first_date + step, tile * 16, 16)):
                store(first_date * 2 * dates, step * 2 * dates + part * dates + tile * 16, sums)
        return carry

    def late(first_date, step, carry):
        for tile in range(half // 8):
            real, imag = sums_of(half + first_date + step, half + tile * 8, 8)
            both = [jnp.concatenate([re, im], axis=0) for re, im in zip(real, imag)]
            store((dates + first_date) * dates, step * dates + tile * 16, both)
        return carry

    for body, width in ((early, 2 * dates), (late, dates)):
        for first_date in range(0, half, group):
            lax.fori_loop(0, group, functools.partial(body, first_date), 0)
            start = first_date * width + (half * 2 * dates if body is late else 0)
            finish(start, group * width)


def turn_edges(edges, turned, dates):
    lane = iota((dates, LANES), 1)
    for k in range(EDGE):
        value = pltpu.roll(edges[k * dates : (k + 1) * dates, :], LANES // 2, 1)
        turned[k * dates : (k + 1) * dates, :] = jnp.where(lane < LANES // 2, value, -value)


def edges_in_use(rg, cols):
    me = lax.axis_index("date")
    first = rg[me * cols]
    last = rg[me * cols + cols - 1]
    return first <= 0, first <= 1, last >= 2, last >= 3


def inner_kernel(blocks, per, lines, chunk, group, order, az, rg, weights, *refs):
    recv, (found, partial, own_edges, x, turned, left) = refs[:blocks], refs[blocks:]
    dates = blocks * per
    date_rows = rows_of_date(lines)
    edge_rows = per * GROUP
    me = lax.axis_index("date")
    swap = 1 - lax.axis_index("strip") % 2
    rest = date_rows - 2 * GROUP
    for piece, k in zip(recv, partners(blocks)):
        block = order[me ^ k]
        to_sublanes(piece, swap * edge_rows, GROUP, GROUP, block, dates, per, x)
        to_sublanes(piece, (1 - swap) * edge_rows, GROUP, GROUP, block, dates, per, x.at[GROUP * dates :])
        to_sublanes(piece, 2 * edge_rows, rest, rest, block, dates, per, x.at[2 * GROUP * dates :])
    own_edges[...] = x[2 * HALO * dates : (2 * HALO + EDGE) * dates, :]
    out_rows = lines // STEP
    inner, outer = kinds_of_rows(out_rows)
    edges = x.at[2 * HALO * dates : (2 * HALO + EDGE) * dates]
    turn_edges(edges, turned, dates)
    places = [None] * HALO
    places += [[(x, row_of(part, line, lines)) for part in range(2)] for line in range(lines)]
    places += [None] * HALO
    rows = inner + outer

    def store(base, start, sums):
        at_rows = pl.ds(pl.multiple_of(start, 16), 16)
        whole = pl.ds(pl.multiple_of(base + start, 16), 16)
        for slot, total in enumerate(sums[: len(inner)] + sums[len(rows) :]):
            store_split(left, at_rows, 2 * slot * LANES, total)
        for slot, total in enumerate(sums[len(inner) : len(rows)]):
            partial[whole, slot * LANES : (slot + 1) * LANES] = total

    def finish(start, count):
        found[start : start + count, :] = jnp.dot(left[:count, :], weights[...], preferred_element_type=jnp.float32)

    edge_on = edges_in_use(rg, chunk // STEP)
    all_dates(dates, group, places, rows, out_rows, az, edges, turned, edge_on, store, finish)


def outer_kernel(
    blocks, per, lines, chunk, group, own_edges, paired, other, partial, found, order, az, rg, weights, *refs
):
    pieces, (send, sums, halo, edges, turned, left, power) = refs[:blocks], refs[blocks:]
    dates = blocks * per
    half = dates // 2
    out_rows = lines // STEP
    cols = chunk // STEP
    wide = out_rows * cols
    me = lax.axis_index("date")
    inner, outer = kinds_of_rows(out_rows)
    split_at = len(inner) * cols

    odd = lax.axis_index("strip") % 2
    for block in range(blocks):
        scatter_halo(paired[block], order[block], lines, dates, per, halo.at[1 - odd])
        scatter_halo(other[block], order[block], lines, dates, per, halo.at[odd])
    below, above = halo.at[0], halo.at[1]
    lane = iota((dates, LANES), 1)
    turn = lane % (LANES // 2)
    for k in range(EDGE):
        at = (2 * HALO + k) * dates
        lower_part = pltpu.roll(below[at : at + dates, :], lines, 1)
        upper_part = pltpu.roll(above[at : at + dates, :], lines, 1)
        mine = own_edges[k * dates : (k + 1) * dates, :]
        value = jnp.where(turn < lines, mine, jnp.where(turn < lines + HALO, upper_part, lower_part))
        edges[k * dates : (k + 1) * dates, :] = value
    turn_edges(edges, turned, dates)
    places = [[(below, part * HALO + line) for part in range(2)] for line in range(HALO)]
    places += [None] * lines
    places += [[(above, part * HALO + line) for part in range(2)] for line in range(HALO)]

    def store(base, start, totals):
        at_rows = pl.ds(pl.multiple_of(start, 16), 16)
        whole = pl.ds(pl.multiple_of(base + start, 16), 16)
        for slot, total in enumerate(totals):
            if slot < len(outer):
                total += partial[whole, slot * LANES : (slot + 1) * LANES]
            store_split(left, at_rows, 2 * slot * LANES, total)

    def finish(start, count):
        rows = slice(start, start + count)
        sums[rows, split_at:] = jnp.dot(left[:count, :], weights[...], preferred_element_type=jnp.float32)

    sums[:, :split_at] = found[...]
    edge_on = edges_in_use(rg, cols)
    all_dates(dates, group, places, outer, out_rows, az, edges, turned, edge_on, store, finish)

    def row_at(date, part, later):
        if date < half:
            return (date * 2 + part) * dates + later
        later -= half
        return (dates + date - half) * dates + later // 8 * 16 + part * 8 + later % 8

    for date in range(dates):
        at_row = row_at(date, 0, date)
        power[date : date + 1, :] = sums[at_row : at_row + 1, :]
    scale = lax.rsqrt(power[...] + epsilon)
    power[...] = scale
    position = iota((dates, wide), 0)
    column = iota((dates, wide), 1)
    for date in range(dates):
        factor = scale * power[date : date + 1, :]
        values = []
        for part in range(2):
            if date < half:
                value = sums[row_at(date, part, 0) : row_at(date, part, 0) + dates, :]
            else:
                tiles = [row_at(date, part, half + tile) for tile in range(0, half, 8)]
                value = [jnp.zeros((half, wide), jnp.float32)] + [sums[row : row + 8, :] for row in tiles]
                value = jnp.concatenate(value, axis=0)
            values.append(jnp.where(position > date, value * factor, 0.0))
        largest = jnp.max(jnp.maximum(jnp.abs(values[0]), jnp.abs(values[1])), axis=1, keepdims=True)
        level = jnp.floor(jnp.log(largest) * (LEVELS / LOG_2)) + 1.0
        level = jnp.clip(level, LOWEST, HIGHEST)
        codes = [jnp.floor(value * (jnp.exp(level * (-LOG_2 / LEVELS)) * TOP) + 0.5) for value in values]
        header = jnp.sum(jnp.where(position == column, level, 0.0), axis=0, keepdims=True)
        codes[0] = jnp.where(position == 0, header, codes[0])
        for part, code in enumerate(codes):
            start = ((date // per * 2 + part) * per + date % per) * dates
            send[start : start + dates, :] = code.astype(jnp.int32).astype(jnp.int16)
    count = 2 * per * dates
    for piece, k in zip(pieces, partners(blocks)):
        piece[...] = send[pl.ds(pl.multiple_of(order[me ^ k] * count, 16), count), :]


def join_kernel(blocks, per, out_rows, cols, order, *refs):
    pieces, (out, recv, halves, placed, done) = refs[:blocks], refs[blocks:]
    dates = blocks * per
    own_rows = per * out_rows
    chosen = [[jnp.broadcast_to(order[b : b + 1, :] == r, (own_rows, LANES)) for r in range(blocks)] for b in range(blocks)]
    wide = out_rows * cols
    per_tile = LANES // cols
    me = lax.axis_index("date")
    lane = iota((dates, LANES), 1) // cols
    position = iota((dates, wide), 0)
    column = iota((dates, wide), 1)
    row_order = sum(kinds_of_rows(out_rows), [])
    for piece, k in zip(pieces, partners(blocks)):
        recv[me ^ k] = piece[...]
    factors = [[None] * blocks for _ in range(per)]
    copies = []
    for step in range(2 * per):
        values = []
        for block in range(blocks):
            codes = recv[block, step * dates : (step + 1) * dates, :].astype(jnp.int32).astype(jnp.float32)
            if step < per:
                header = codes[:1]
                level = jnp.sum(jnp.where(position == column, header, 0.0), axis=1, keepdims=True)
                factors[step][block] = jnp.exp(level * (LOG_2 / LEVELS)) * (1.0 / TOP)
            values.append(jnp.where(position == 0, 0.0, codes * factors[step % per][block]))
        for d_tile in range(blocks // per_tile):
            for o_tile in range(out_rows // per_tile):
                tiles = [
                    values[d_tile * per_tile + d][:, o_tile * LANES : (o_tile + 1) * LANES] for d in range(per_tile)
                ]
                width = 1
                while width < per_tile:
                    swap = [None] * per_tile
                    upper = (lane // width) % 2 == 1
                    shift = width * cols
                    for a in range(per_tile):
                        if (a // width) % 2 == 0:
                            b = a + width
                            swap[a] = jnp.where(upper, pltpu.roll(tiles[b], shift, 1), tiles[a])
                            swap[b] = jnp.where(upper, tiles[b], pltpu.roll(tiles[a], LANES - shift, 1))
                    tiles = swap
                    width *= 2
                for o in range(per_tile):
                    for start in range(0, dates, 8):
                        at = start * out_rows + row_order[o_tile * per_tile + o]
                        halves[step, d_tile, pl.ds(at, 8, stride=out_rows), :] = tiles[o][start : start + 8]
            ranked = [halves[step, d_tile, r * own_rows : (r + 1) * own_rows, :] for r in range(blocks)]
            for block in range(blocks):
                found = ranked[0]
                for r in range(1, blocks):
                    found = jnp.where(chosen[block][r], ranked[r], found)
                placed[step, d_tile, block * own_rows : (block + 1) * own_rows, :] = found
            rows = slice(step * dates * out_rows, (step + 1) * dates * out_rows)
            target = out.at[rows, d_tile * LANES : (d_tile + 1) * LANES]
            copies.append(pltpu.make_async_copy(placed.at[step, d_tile], target, done.at[step, d_tile]))
            copies[-1].start()
    for copy in copies:
        copy.wait()


def decode(codes):
    values = codes.astype(jnp.float32)
    dates = codes.shape[3]
    factor = jnp.exp(values[:, 0, :, 0, :dates] * (LOG_2 / LEVELS)) * (1.0 / TOP)
    return (values * factor[:, None, :, :, None]).at[:, :, :, 0].set(0.0)


def on_device(slc, block_order, az_offset, rg_offset):
    blocks = lax.axis_size("date")
    strips = lax.axis_size("strip")
    per, lines, span = slc.shape[1:]
    dates = blocks * per
    chunk = span // blocks
    out_rows = lines // STEP
    cols = chunk // STEP
    wide = out_rows * cols
    date_rows = rows_of_date(lines)
    group = max(per, 256 // dates)
    me = lax.axis_index("date")

    edge_rows = per * GROUP
    piece = jax.ShapeDtypeStruct((per * date_rows, LANES), jnp.bfloat16)
    send = pl.pallas_call(
        functools.partial(pack_kernel, blocks, per, lines, chunk),
        out_shape=[piece] * blocks,
        in_specs=[VMEM],
        out_specs=[VMEM] * blocks,
        scratch_shapes=[
            pltpu.VMEM((blocks, per * date_rows, LANES), jnp.bfloat16),
            pltpu.VMEM((per * date_rows, span), jnp.float32),
        ],
        compiler_params=PARAMS,
        name="pack",
    )(slc)
    recv = swap_blocks(send)
    tiled = jnp.tile(lax.dynamic_slice_in_dim(rg_offset, me * cols, cols), out_rows)[None]
    kinds = kinds_of_rows(out_rows)
    depths = [(len(rows) + 2) * 2 * LANES for rows in kinds]
    weights = pl.pallas_call(
        functools.partial(weight_kernel, lines, chunk),
        out_shape=[
            jax.ShapeDtypeStruct((depth, len(rows) * cols), jnp.bfloat16) for depth, rows in zip(depths, kinds)
        ],
        in_specs=[SMEM, VMEM],
        out_specs=[VMEM] * 2,
        compiler_params=PARAMS,
        cost_estimate=pl.CostEstimate(flops=0, bytes_accessed=4 * 1024 * 1024, transcendentals=0),
        name="weights",
    )(az_offset, tiled)
    recv, weights = lax.optimization_barrier((recv, weights))

    edge = jax.ShapeDtypeStruct((blocks, halo_rows(per), LANES), jnp.bfloat16)
    to_pair, to_other = pl.pallas_call(
        functools.partial(gather_kernel, blocks, per, lines),
        out_shape=[edge] * 2,
        in_specs=[VMEM] * blocks,
        out_specs=[VMEM] * 2,
        scratch_shapes=[pltpu.VMEM((halo_rows(per), LANES), jnp.float32)],
        compiler_params=PARAMS,
        name="gather",
    )(*recv)

    def swaps(first):
        pairs = [(i, i + 1) for i in range(first, strips - 1, 2)]
        return pairs + [(target, source) for source, target in pairs]

    other = lax.ppermute(to_other, "strip", swaps(1))
    paired = lax.ppermute(to_pair, "strip", swaps(0))
    count = dates * dates * 3 // 2
    half_group = min(group, dates // 2)
    found, partial, own_edges = pl.pallas_call(
        functools.partial(inner_kernel, blocks, per, lines, chunk, group),
        out_shape=[
            jax.ShapeDtypeStruct((count, len(kinds[0]) * cols), jnp.float32),
            jax.ShapeDtypeStruct((count, len(kinds[1]) * LANES), jnp.float32),
            jax.ShapeDtypeStruct((EDGE * dates, LANES), jnp.float32),
        ],
        in_specs=[SMEM] * 3 + [VMEM] * (1 + blocks),
        out_specs=[VMEM] * 3,
        scratch_shapes=[
            pltpu.VMEM((date_rows * dates, LANES), jnp.float32),
            pltpu.VMEM((EDGE * dates, LANES), jnp.float32),
            pltpu.VMEM((half_group * 2 * dates, depths[0]), jnp.bfloat16),
        ],
        compiler_params=PARAMS,
        cost_estimate=pl.CostEstimate(flops=0, bytes_accessed=12 * 1024 * 1024, transcendentals=0),
        name="inner",
    )(block_order, az_offset, rg_offset, weights[0], *recv)
    pairs = pl.pallas_call(
        functools.partial(outer_kernel, blocks, per, lines, chunk, group),
        out_shape=[jax.ShapeDtypeStruct((2 * per * dates, wide), jnp.int16)] * blocks,
        in_specs=[VMEM] * 5 + [SMEM] * 3 + [VMEM],
        out_specs=[VMEM] * blocks,
        scratch_shapes=[
            pltpu.VMEM((dates * 2 * dates, wide), jnp.int16),
            pltpu.VMEM((count, wide), jnp.float32),
            pltpu.VMEM((2, GROUP * dates, LANES), jnp.float32),
            pltpu.VMEM((EDGE * dates, LANES), jnp.float32),
            pltpu.VMEM((EDGE * dates, LANES), jnp.float32),
            pltpu.VMEM((half_group * 2 * dates, depths[1]), jnp.bfloat16),
            pltpu.VMEM((dates, wide), jnp.float32),
        ],
        compiler_params=PARAMS,
        name="outer",
    )(own_edges, paired, other, partial, found, block_order, az_offset, rg_offset, weights[1])
    count = 2 * per * dates
    back = swap_blocks(pairs)
    if LANES % cols == 0 and out_rows * cols % LANES == 0 and blocks * cols % LANES == 0:
        out = pl.pallas_call(
            functools.partial(join_kernel, blocks, per, out_rows, cols),
            out_shape=jax.ShapeDtypeStruct((count * out_rows, blocks * cols), jnp.float32),
            in_specs=[VMEM] * (1 + blocks),
            out_specs=pl.BlockSpec(memory_space=pl.ANY),
            scratch_shapes=[
                pltpu.VMEM((blocks, count, wide), jnp.int16),
                pltpu.VMEM((2 * per, blocks * cols // LANES, dates * out_rows, LANES), jnp.float32),
                pltpu.VMEM((2 * per, blocks * cols // LANES, dates * out_rows, LANES), jnp.float32),
                pltpu.SemaphoreType.DMA((2 * per, blocks * cols // LANES)),
            ],
            compiler_params=PARAMS,
            name="join",
        )(jnp.broadcast_to(block_order[:, None], (blocks, LANES)), *back)
    else:
        place = [partners(blocks).index(k) for k in range(blocks)]
        back = jnp.stack([back[at] for at in place])[me ^ jnp.arange(blocks)]
        values = decode(back.reshape(blocks, 2, per, dates, wide))
        values = values.reshape(blocks, 2, per, blocks, per, wide)[:, :, :, block_order]
        values = values.reshape(blocks, count, out_rows, cols).transpose(1, 2, 0, 3)
        row_order = sum(kinds_of_rows(out_rows), [])
        out = jnp.stack([values[:, row_order.index(o)] for o in range(out_rows)], axis=1)
    return out.reshape(2, per, dates, out_rows, blocks * cols)


def solution(mesh):
    placed = (P(None, "date", "strip", None), P(), P("strip"), P())
    return jax.shard_map(
        on_device,
        mesh=mesh,
        in_specs=placed,
        out_specs=P(None, "date", None, "strip", None),
        check_vma=False,
    )
```

```python
import functools

import jax
import jax.numpy as jnp
from jax import lax
from jax.experimental import pallas as pl
from jax.experimental.pallas import tpu as pltpu
from jax.sharding import PartitionSpec as P

STEP = 4
HALO = 5
REACH = 2
EDGE = 4
LANES = 128
GROUP = 16
VMEM = pl.BlockSpec(memory_space=pltpu.VMEM)
SMEM = pl.BlockSpec(memory_space=pltpu.SMEM)
PARAMS = pltpu.CompilerParams(vmem_limit_bytes=48 * 1024 * 1024)

epsilon = 1e-06
LEVELS = 8.0
LOWEST, HIGHEST = -880.0, 64.0
TOP = 32760.0
LOG_2 = 0.6931471805599453


def iota(shape, dim):
    return lax.broadcasted_iota(jnp.int32, shape, dim)


def row_of(part, line, lines):
    if line < HALO:
        return part * HALO + line
    if line >= lines - HALO:
        return GROUP + part * HALO + line - (lines - HALO)
    middle = part * (lines - 2 * HALO) + line - HALO
    spare = GROUP - 2 * HALO - EDGE
    if middle < spare:
        return 2 * HALO + EDGE + middle
    if middle < 2 * spare:
        return GROUP + 2 * HALO + EDGE + middle - spare
    return 2 * GROUP + middle - 2 * spare


def place_of(date, row, per, date_rows):
    if row < GROUP:
        return date * GROUP + row
    if row < 2 * GROUP:
        return (per + date - 1) * GROUP + row
    return 2 * per * GROUP + date * (date_rows - 2 * GROUP) + row - 2 * GROUP


def rows_of_date(lines):
    return 2 * GROUP + 2 * (lines - 2 * HALO) - 2 * (GROUP - 2 * HALO - EDGE)


def runs(part, lines):
    found = []
    for line in range(lines):
        row = row_of(part, line, lines)
        if line and row == row_of(part, line - 1, lines) + 1 and row % GROUP:
            found[-1][1] += 1
        else:
            found.append([line, 1])
    return found


def partners(blocks):
    return [0, 1] + sorted(range(2, blocks), key=lambda k: (k & 1, -k))


def swap_blocks(pieces):
    blocks = len(pieces)
    found = list(pieces)
    for at, k in enumerate(partners(blocks)):
        if k:
            found[at] = lax.ppermute(pieces[at], "date", [(i, i ^ k) for i in range(blocks)])
    return found


def pack_kernel(blocks, per, lines, chunk, slc, *refs):
    pieces, (send, stage) = refs[:blocks], refs[blocks:]
    me = lax.axis_index("date")
    date_rows = rows_of_date(lines)
    edge_rows = per * GROUP
    turn = 1 - lax.axis_index("strip") % 2
    span = blocks * chunk
    shape = (EDGE * blocks, span)
    place = iota(shape, 0) % EDGE
    wanted = iota(shape, 0) // EDGE * chunk + jnp.where(place < REACH, place - REACH, place - REACH + chunk)
    picks = (iota(shape, 1) == wanted).astype(jnp.bfloat16)
    lane = iota((EDGE * blocks, LANES), 1)
    edges = []
    for date in range(per):
        mine = jnp.zeros((EDGE * blocks, LANES), jnp.float32)
        for part in range(2):
            samples = slc[part, date]
            for first, count in runs(part, lines):
                at = place_of(date, row_of(part, first, lines), per, date_rows)
                stage[at : at + count, :] = samples[first : first + count].astype(jnp.float32)
            found = lax.dot_general(picks, samples, (((1,), (1,)), ((), ())), preferred_element_type=jnp.float32)
            found = jnp.concatenate([found, jnp.zeros((EDGE * blocks, LANES - lines), jnp.float32)], axis=1)
            mine += pltpu.roll(found, part * (LANES // 2), 1) if part else found
        edges.append(mine)
    for block in range(blocks):
        for date in range(per):
            for group in range(2):
                at = place_of(date, group * GROUP + 2 * HALO, per, date_rows)
                value = edges[date][block * EDGE : (block + 1) * EDGE]
                if chunk == LANES:
                    stage[at : at + EDGE, block * LANES : (block + 1) * LANES] = value
        if chunk == LANES:
            piece = stage[:, block * chunk : (block + 1) * chunk]
        else:
            piece = stage[:, block * chunk : (block + 1) * chunk]
            piece = jnp.concatenate([piece, jnp.zeros((per * date_rows, LANES - chunk), jnp.float32)], axis=1)
            row = iota((per * date_rows, LANES), 0)
            for date in range(per):
                for group in range(2):
                    at = place_of(date, group * GROUP + 2 * HALO, per, date_rows)
                    for k in range(EDGE):
                        value = edges[date][block * EDGE + k : block * EDGE + k + 1]
                        piece = jnp.where(row == at + k, value, piece)
        piece = piece.astype(jnp.bfloat16)
        send[block, pl.ds(pl.multiple_of(turn * edge_rows, 16), edge_rows), :] = piece[:edge_rows]
        send[block, pl.ds(pl.multiple_of((1 - turn) * edge_rows, 16), edge_rows), :] = piece[edge_rows : 2 * edge_rows]
        send[block, 2 * edge_rows :, :] = piece[2 * edge_rows :]
    for piece, k in zip(pieces, partners(blocks)):
        piece[...] = send[me ^ k]


def kinds_of_rows(out_rows):
    return list(range(2, out_rows - 2)), [0, 1, out_rows - 2, out_rows - 1]


def weight_kernel(lines, chunk, az, tiled, *weights):
    cols = chunk // STEP
    for rows, target in zip(kinds_of_rows(lines // STEP), weights):
        count = len(rows)
        depth = count * 2 * LANES
        shape = (LANES, count * cols)
        col = iota(shape, 1) % cols
        slot = iota(shape, 1) // cols
        box = jnp.abs(iota(shape, 0) - STEP * col - tiled[:, : count * cols]) <= REACH
        for o in range(count):
            mine = (box & (slot == o)).astype(jnp.bfloat16)
            target[2 * o * LANES : (2 * o + 1) * LANES, :] = mine
            target[(2 * o + 1) * LANES : (2 * o + 2) * LANES, :] = mine
        turn = iota(shape, 0) % (LANES // 2)
        line = jnp.where(turn < lines + HALO, turn + HALO, turn + HALO - LANES // 2)
        lower = jnp.zeros(shape, jnp.int32)
        for place, o in enumerate(rows):
            lower = jnp.where(slot == place, STEP * o + az[o], lower)
        window = (line >= lower) & (line <= lower + 2 * HALO)
        for side, edge_col in ((0, 0), (1, cols - 1)):
            mine = (window & (col == edge_col)).astype(jnp.bfloat16)
            for term in range(2):
                start = depth + (2 * side + term) * LANES
                target[start : start + LANES, :] = mine


def to_sublanes(source, first_row, date_stride, rows, block, dates, per, target):
    for date in range(per):
        at = first_row + date * date_stride
        if not isinstance(at, int):
            at = pl.multiple_of(at, 8)
        value = source[pl.ds(at, rows), :].astype(jnp.float32)
        for row in range(0, rows, 8):
            target[pl.ds(row * dates + block * per + date, 8, stride=dates), :] = value[row : row + 8]


def halo_rows(per):
    return per * 2 * HALO + EDGE


def gather_kernel(blocks, per, lines, *refs):
    recv, (paired, other, stage) = refs[:blocks], refs[blocks:]
    me = lax.axis_index("date")
    tail = 2 * HALO - 8
    for piece, k in zip(recv, partners(blocks)):
        for group, target in enumerate((paired, other)):
            edges = jnp.zeros((EDGE, LANES), jnp.float32)
            for date in range(per):
                at = (group * per + date) * GROUP
                value = piece[at : at + GROUP].astype(jnp.float32)
                stage[date * 8 : date * 8 + 8, :] = value[:8]
                stage[per * 8 + date * tail : per * 8 + (date + 1) * tail, :] = value[8 : 2 * HALO]
                mine = value[2 * HALO : 2 * HALO + EDGE]
                edges += pltpu.roll(mine, date * lines, 1) if date else mine
            stage[per * 2 * HALO :, :] = edges
            target[me ^ k] = stage[...].astype(jnp.bfloat16)


def scatter_halo(source, block, lines, dates, per, target):
    value = source.astype(jnp.float32)
    tail = 2 * HALO - 8
    for date in range(per):
        place = block * per + date
        target[pl.ds(place, 8, stride=dates), :] = value[date * 8 : date * 8 + 8]
        rest = value[per * 8 + date * tail : per * 8 + (date + 1) * tail]
        target[pl.ds(8 * dates + place, tail, stride=dates), :] = rest
        mine = value[per * 2 * HALO :]
        mine = pltpu.roll(mine, LANES - date * lines, 1) if date else mine
        target[pl.ds(2 * HALO * dates + place, EDGE, stride=dates), :] = mine


def split(value):
    high = value.astype(jnp.bfloat16)
    return high, (value - high.astype(jnp.float32)).astype(jnp.bfloat16)


def plus(total, value):
    return value if total is None else total + value


def window_sums(product, rows, out_rows, az):
    quads = [None] * (out_rows + 1)
    for k in range(out_rows + 1):
        for line in range(STEP * k + 3, STEP * k + 7):
            if product[line] is not None:
                quads[k] = plus(quads[k], product[line])
    sums = []
    for o in rows:
        total = None
        for quad in (quads[o], quads[o + 1]):
            if quad is not None:
                total = plus(total, quad)
        for k in range(3):
            early, late = product[STEP * o + k], product[STEP * o + 11 + k]
            if early is None and late is None:
                continue
            early = jnp.zeros_like(late) if early is None else early
            late = jnp.zeros_like(early) if late is None else late
            total = plus(total, jnp.where(az[o] <= k, early, late))
        sums.append(total)
    return sums


def products(places, date, first, count, dates):
    real, imag = [], []
    for line in places:
        if line is None:
            real.append(None)
            imag.append(None)
            continue
        (ref, at_re), (_, at_im) = line
        re_i, im_i = (ref[pl.ds(row * dates + date, 1), :] for row in (at_re, at_im))
        re_j, im_j = (ref[row * dates + first : row * dates + first + count, :] for row in (at_re, at_im))
        real.append(re_i * re_j + im_i * im_j)
        imag.append(im_i * re_j - re_i * im_j)
    return real, imag


def store_split(target, rows, start, value):
    upper, rest = split(value)
    target[rows, start : start + LANES] = upper
    target[rows, start + LANES : start + 2 * LANES] = rest


def edge_sums(edges, own, date, first, count, dates, edge_on):
    sums = []
    for side in range(2):
        total = jnp.zeros((count, LANES), jnp.float32)
        for edge in (2 * side, 2 * side + 1):
            others = edges[edge * dates + first : edge * dates + first + count, :]
            total += jnp.where(edge_on[edge], own[pl.ds(edge * dates + date, 1), :] * others, 0.0)
        sums.append(total)
    return sums


def all_dates(dates, group, places, rows, out_rows, az, edges, turned, edge_on, store, finish):
    half = dates // 2
    group = min(group, half)

    def sums_of(date, first, count):
        found = []
        for part, product in enumerate(products(places, date, first, count, dates)):
            sums = window_sums(product, rows, out_rows, az)
            found.append(sums + edge_sums(edges, turned if part else edges, date, first, count, dates, edge_on))
        return found

    def early(first_date, step, carry):
        for tile in range(dates // 16):
            for part, sums in enumerate(sums_of(first_date + step, tile * 16, 16)):
                store(first_date * 2 * dates, step * 2 * dates + part * dates + tile * 16, sums)
        return carry

    def late(first_date, step, carry):
        for tile in range(half // 8):
            real, imag = sums_of(half + first_date + step, half + tile * 8, 8)
            both = [jnp.concatenate([re, im], axis=0) for re, im in zip(real, imag)]
            store((dates + first_date) * dates, step * dates + tile * 16, both)
        return carry

    for body, width in ((early, 2 * dates), (late, dates)):
        for first_date in range(0, half, group):
            lax.fori_loop(0, group, functools.partial(body, first_date), 0)
            start = first_date * width + (half * 2 * dates if body is late else 0)
            finish(start, group * width)


def turn_edges(edges, turned, dates):
    lane = iota((dates, LANES), 1)
    for k in range(EDGE):
        value = pltpu.roll(edges[k * dates : (k + 1) * dates, :], LANES // 2, 1)
        turned[k * dates : (k + 1) * dates, :] = jnp.where(lane < LANES // 2, value, -value)


def edges_in_use(rg, cols):
    me = lax.axis_index("date")
    first = rg[me * cols]
    last = rg[me * cols + cols - 1]
    return first <= 0, first <= 1, last >= 2, last >= 3


def inner_kernel(blocks, per, lines, chunk, group, order, az, rg, weights, *refs):
    recv, (found, partial, own_edges, x, turned, left) = refs[:blocks], refs[blocks:]
    dates = blocks * per
    date_rows = rows_of_date(lines)
    edge_rows = per * GROUP
    me = lax.axis_index("date")
    swap = 1 - lax.axis_index("strip") % 2
    rest = date_rows - 2 * GROUP
    for piece, k in zip(recv, partners(blocks)):
        block = order[me ^ k]
        to_sublanes(piece, swap * edge_rows, GROUP, GROUP, block, dates, per, x)
        to_sublanes(piece, (1 - swap) * edge_rows, GROUP, GROUP, block, dates, per, x.at[GROUP * dates :])
        to_sublanes(piece, 2 * edge_rows, rest, rest, block, dates, per, x.at[2 * GROUP * dates :])
    own_edges[...] = x[2 * HALO * dates : (2 * HALO + EDGE) * dates, :]
    out_rows = lines // STEP
    inner, outer = kinds_of_rows(out_rows)
    edges = x.at[2 * HALO * dates : (2 * HALO + EDGE) * dates]
    turn_edges(edges, turned, dates)
    places = [None] * HALO
    places += [[(x, row_of(part, line, lines)) for part in range(2)] for line in range(lines)]
    places += [None] * HALO
    rows = inner + outer

    def store(base, start, sums):
        at_rows = pl.ds(pl.multiple_of(start, 16), 16)
        whole = pl.ds(pl.multiple_of(base + start, 16), 16)
        for slot, total in enumerate(sums[: len(inner)] + sums[len(rows) :]):
            store_split(left, at_rows, 2 * slot * LANES, total)
        for slot, total in enumerate(sums[len(inner) : len(rows)]):
            partial[whole, slot * LANES : (slot + 1) * LANES] = total

    def finish(start, count):
        found[start : start + count, :] = jnp.dot(left[:count, :], weights[...], preferred_element_type=jnp.float32)

    edge_on = edges_in_use(rg, chunk // STEP)
    all_dates(dates, group, places, rows, out_rows, az, edges, turned, edge_on, store, finish)


def outer_kernel(
    blocks, per, lines, chunk, group, own_edges, paired, other, partial, found, order, az, rg, weights, *refs
):
    pieces, (send, sums, halo, edges, turned, left, power) = refs[:blocks], refs[blocks:]
    dates = blocks * per
    half = dates // 2
    out_rows = lines // STEP
    cols = chunk // STEP
    wide = out_rows * cols
    me = lax.axis_index("date")
    inner, outer = kinds_of_rows(out_rows)
    split_at = len(inner) * cols

    odd = lax.axis_index("strip") % 2
    for block in range(blocks):
        scatter_halo(paired[block], order[block], lines, dates, per, halo.at[1 - odd])
        scatter_halo(other[block], order[block], lines, dates, per, halo.at[odd])
    below, above = halo.at[0], halo.at[1]
    lane = iota((dates, LANES), 1)
    turn = lane % (LANES // 2)
    for k in range(EDGE):
        at = (2 * HALO + k) * dates
        lower_part = pltpu.roll(below[at : at + dates, :], lines, 1)
        upper_part = pltpu.roll(above[at : at + dates, :], lines, 1)
        mine = own_edges[k * dates : (k + 1) * dates, :]
        value = jnp.where(turn < lines, mine, jnp.where(turn < lines + HALO, upper_part, lower_part))
        edges[k * dates : (k + 1) * dates, :] = value
    turn_edges(edges, turned, dates)
    places = [[(below, part * HALO + line) for part in range(2)] for line in range(HALO)]
    places += [None] * lines
    places += [[(above, part * HALO + line) for part in range(2)] for line in range(HALO)]

    def store(base, start, totals):
        at_rows = pl.ds(pl.multiple_of(start, 16), 16)
        whole = pl.ds(pl.multiple_of(base + start, 16), 16)
        for slot, total in enumerate(totals):
            if slot < len(outer):
                total += partial[whole, slot * LANES : (slot + 1) * LANES]
            store_split(left, at_rows, 2 * slot * LANES, total)

    def finish(start, count):
        rows = slice(start, start + count)
        sums[rows, split_at:] = jnp.dot(left[:count, :], weights[...], preferred_element_type=jnp.float32)

    sums[:, :split_at] = found[...]
    edge_on = edges_in_use(rg, cols)
    all_dates(dates, group, places, outer, out_rows, az, edges, turned, edge_on, store, finish)

    def row_at(date, part, later):
        if date < half:
            return (date * 2 + part) * dates + later
        later -= half
        return (dates + date - half) * dates + later // 8 * 16 + part * 8 + later % 8

    for date in range(dates):
        at_row = row_at(date, 0, date)
        power[date : date + 1, :] = sums[at_row : at_row + 1, :]
    scale = lax.rsqrt(power[...] + epsilon)
    power[...] = scale
    position = iota((dates, wide), 0)
    column = iota((dates, wide), 1)
    for date in range(dates):
        factor = scale * power[date : date + 1, :]
        values = []
        for part in range(2):
            if date < half:
                value = sums[row_at(date, part, 0) : row_at(date, part, 0) + dates, :]
            else:
                tiles = [row_at(date, part, half + tile) for tile in range(0, half, 8)]
                value = [jnp.zeros((half, wide), jnp.float32)] + [sums[row : row + 8, :] for row in tiles]
                value = jnp.concatenate(value, axis=0)
            values.append(jnp.where(position > date, value * factor, 0.0))
        largest = jnp.max(jnp.maximum(jnp.abs(values[0]), jnp.abs(values[1])), axis=1, keepdims=True)
        level = jnp.floor(jnp.log(largest) * (LEVELS / LOG_2)) + 1.0
        level = jnp.clip(level, LOWEST, HIGHEST)
        codes = [jnp.floor(value * (jnp.exp(level * (-LOG_2 / LEVELS)) * TOP) + 0.5) for value in values]
        header = jnp.sum(jnp.where(position == column, level, 0.0), axis=0, keepdims=True)
        codes[0] = jnp.where(position == 0, header, codes[0])
        for part, code in enumerate(codes):
            start = ((date // per * 2 + part) * per + date % per) * dates
            send[start : start + dates, :] = code.astype(jnp.int32).astype(jnp.int16)
    count = 2 * per * dates
    for piece, k in zip(pieces, partners(blocks)):
        piece[...] = send[pl.ds(pl.multiple_of(order[me ^ k] * count, 16), count), :]


def join_kernel(blocks, per, out_rows, cols, order, *refs):
    pieces, (out, recv, halves, placed, done) = refs[:blocks], refs[blocks:]
    dates = blocks * per
    own_rows = per * out_rows
    chosen = [[jnp.broadcast_to(order[b : b + 1, :] == r, (own_rows, LANES)) for r in range(blocks)] for b in range(blocks)]
    wide = out_rows * cols
    per_tile = LANES // cols
    me = lax.axis_index("date")
    lane = iota((dates, LANES), 1) // cols
    position = iota((dates, wide), 0)
    column = iota((dates, wide), 1)
    row_order = sum(kinds_of_rows(out_rows), [])
    for piece, k in zip(pieces, partners(blocks)):
        recv[me ^ k] = piece[...]
    factors = [[None] * blocks for _ in range(per)]
    copies = []
    for step in range(2 * per):
        values = []
        for block in range(blocks):
            codes = recv[block, step * dates : (step + 1) * dates, :].astype(jnp.int32).astype(jnp.float32)
            if step < per:
                header = codes[:1]
                level = jnp.sum(jnp.where(position == column, header, 0.0), axis=1, keepdims=True)
                factors[step][block] = jnp.exp(level * (LOG_2 / LEVELS)) * (1.0 / TOP)
            values.append(jnp.where(position == 0, 0.0, codes * factors[step % per][block]))
        for d_tile in range(blocks // per_tile):
            for o_tile in range(out_rows // per_tile):
                tiles = [
                    values[d_tile * per_tile + d][:, o_tile * LANES : (o_tile + 1) * LANES] for d in range(per_tile)
                ]
                width = 1
                while width < per_tile:
                    swap = [None] * per_tile
                    upper = (lane // width) % 2 == 1
                    shift = width * cols
                    for a in range(per_tile):
                        if (a // width) % 2 == 0:
                            b = a + width
                            swap[a] = jnp.where(upper, pltpu.roll(tiles[b], shift, 1), tiles[a])
                            swap[b] = jnp.where(upper, tiles[b], pltpu.roll(tiles[a], LANES - shift, 1))
                    tiles = swap
                    width *= 2
                for o in range(per_tile):
                    for start in range(0, dates, 8):
                        at = start * out_rows + row_order[o_tile * per_tile + o]
                        halves[step, d_tile, pl.ds(at, 8, stride=out_rows), :] = tiles[o][start : start + 8]
            ranked = [halves[step, d_tile, r * own_rows : (r + 1) * own_rows, :] for r in range(blocks)]
            for block in range(blocks):
                found = ranked[0]
                for r in range(1, blocks):
                    found = jnp.where(chosen[block][r], ranked[r], found)
                placed[step, d_tile, block * own_rows : (block + 1) * own_rows, :] = found
            rows = slice(step * dates * out_rows, (step + 1) * dates * out_rows)
            target = out.at[rows, d_tile * LANES : (d_tile + 1) * LANES]
            copies.append(pltpu.make_async_copy(placed.at[step, d_tile], target, done.at[step, d_tile]))
            copies[-1].start()
    for copy in copies:
        copy.wait()


def decode(codes):
    values = codes.astype(jnp.float32)
    dates = codes.shape[3]
    factor = jnp.exp(values[:, 0, :, 0, :dates] * (LOG_2 / LEVELS)) * (1.0 / TOP)
    return (values * factor[:, None, :, :, None]).at[:, :, :, 0].set(0.0)


def on_device(slc, block_order, az_offset, rg_offset):
    blocks = lax.axis_size("date")
    strips = lax.axis_size("strip")
    per, lines, span = slc.shape[1:]
    dates = blocks * per
    chunk = span // blocks
    out_rows = lines // STEP
    cols = chunk // STEP
    wide = out_rows * cols
    date_rows = rows_of_date(lines)
    group = max(per, 256 // dates)
    me = lax.axis_index("date")

    edge_rows = per * GROUP
    piece = jax.ShapeDtypeStruct((per * date_rows, LANES), jnp.bfloat16)
    send = pl.pallas_call(
        functools.partial(pack_kernel, blocks, per, lines, chunk),
        out_shape=[piece] * blocks,
        in_specs=[VMEM],
        out_specs=[VMEM] * blocks,
        scratch_shapes=[
            pltpu.VMEM((blocks, per * date_rows, LANES), jnp.bfloat16),
            pltpu.VMEM((per * date_rows, span), jnp.float32),
        ],
        compiler_params=PARAMS,
        name="pack",
    )(slc)
    recv = swap_blocks(send)
    tiled = jnp.tile(lax.dynamic_slice_in_dim(rg_offset, me * cols, cols), out_rows)[None]
    kinds = kinds_of_rows(out_rows)
    depths = [(len(rows) + 2) * 2 * LANES for rows in kinds]
    weights = pl.pallas_call(
        functools.partial(weight_kernel, lines, chunk),
        out_shape=[
            jax.ShapeDtypeStruct((depth, len(rows) * cols), jnp.bfloat16) for depth, rows in zip(depths, kinds)
        ],
        in_specs=[SMEM, VMEM],
        out_specs=[VMEM] * 2,
        compiler_params=PARAMS,
        cost_estimate=pl.CostEstimate(flops=0, bytes_accessed=4 * 1024 * 1024, transcendentals=0),
        name="weights",
    )(az_offset, tiled)
    recv, weights = lax.optimization_barrier((recv, weights))

    edge = jax.ShapeDtypeStruct((blocks, halo_rows(per), LANES), jnp.bfloat16)
    to_pair, to_other = pl.pallas_call(
        functools.partial(gather_kernel, blocks, per, lines),
        out_shape=[edge] * 2,
        in_specs=[VMEM] * blocks,
        out_specs=[VMEM] * 2,
        scratch_shapes=[pltpu.VMEM((halo_rows(per), LANES), jnp.float32)],
        compiler_params=PARAMS,
        name="gather",
    )(*recv)

    def swaps(first):
        pairs = [(i, i + 1) for i in range(first, strips - 1, 2)]
        return pairs + [(target, source) for source, target in pairs]

    other = lax.ppermute(to_other, "strip", swaps(1))
    paired = lax.ppermute(to_pair, "strip", swaps(0))
    count = dates * dates * 3 // 2
    half_group = min(group, dates // 2)
    found, partial, own_edges = pl.pallas_call(
        functools.partial(inner_kernel, blocks, per, lines, chunk, group),
        out_shape=[
            jax.ShapeDtypeStruct((count, len(kinds[0]) * cols), jnp.float32),
            jax.ShapeDtypeStruct((count, len(kinds[1]) * LANES), jnp.float32),
            jax.ShapeDtypeStruct((EDGE * dates, LANES), jnp.float32),
        ],
        in_specs=[SMEM] * 3 + [VMEM] * (1 + blocks),
        out_specs=[VMEM] * 3,
        scratch_shapes=[
            pltpu.VMEM((date_rows * dates, LANES), jnp.float32),
            pltpu.VMEM((EDGE * dates, LANES), jnp.float32),
            pltpu.VMEM((half_group * 2 * dates, depths[0]), jnp.bfloat16),
        ],
        compiler_params=PARAMS,
        cost_estimate=pl.CostEstimate(flops=0, bytes_accessed=12 * 1024 * 1024, transcendentals=0),
        name="inner",
    )(block_order, az_offset, rg_offset, weights[0], *recv)
    pairs = pl.pallas_call(
        functools.partial(outer_kernel, blocks, per, lines, chunk, group),
        out_shape=[jax.ShapeDtypeStruct((2 * per * dates, wide), jnp.int16)] * blocks,
        in_specs=[VMEM] * 5 + [SMEM] * 3 + [VMEM],
        out_specs=[VMEM] * blocks,
        scratch_shapes=[
            pltpu.VMEM((dates * 2 * dates, wide), jnp.int16),
            pltpu.VMEM((count, wide), jnp.float32),
            pltpu.VMEM((2, GROUP * dates, LANES), jnp.float32),
            pltpu.VMEM((EDGE * dates, LANES), jnp.float32),
            pltpu.VMEM((EDGE * dates, LANES), jnp.float32),
            pltpu.VMEM((half_group * 2 * dates, depths[1]), jnp.bfloat16),
            pltpu.VMEM((dates, wide), jnp.float32),
        ],
        compiler_params=PARAMS,
        name="outer",
    )(own_edges, paired, other, partial, found, block_order, az_offset, rg_offset, weights[1])
    count = 2 * per * dates
    back = swap_blocks(pairs)
    if LANES % cols == 0 and out_rows * cols % LANES == 0 and blocks * cols % LANES == 0:
        out = pl.pallas_call(
            functools.partial(join_kernel, blocks, per, out_rows, cols),
            out_shape=jax.ShapeDtypeStruct((count * out_rows, blocks * cols), jnp.float32),
            in_specs=[VMEM] * (1 + blocks),
            out_specs=pl.BlockSpec(memory_space=pl.ANY),
            scratch_shapes=[
                pltpu.VMEM((blocks, count, wide), jnp.int16),
                pltpu.VMEM((2 * per, blocks * cols // LANES, dates * out_rows, LANES), jnp.float32),
                pltpu.VMEM((2 * per, blocks * cols // LANES, dates * out_rows, LANES), jnp.float32),
                pltpu.SemaphoreType.DMA((2 * per, blocks * cols // LANES)),
            ],
            compiler_params=PARAMS,
            name="join",
        )(jnp.broadcast_to(block_order[:, None], (blocks, LANES)), *back)
    else:
        place = [partners(blocks).index(k) for k in range(blocks)]
        back = jnp.stack([back[at] for at in place])[me ^ jnp.arange(blocks)]
        values = decode(back.reshape(blocks, 2, per, dates, wide))
        values = values.reshape(blocks, 2, per, blocks, per, wide)[:, :, :, block_order]
        values = values.reshape(blocks, count, out_rows, cols).transpose(1, 2, 0, 3)
        row_order = sum(kinds_of_rows(out_rows), [])
        out = jnp.stack([values[:, row_order.index(o)] for o in range(out_rows)], axis=1)
    return out.reshape(2, per, dates, out_rows, blocks * cols)


def solution(mesh):
    placed = (P(None, "date", "strip", None), P(), P("strip"), P())
    return jax.shard_map(
        on_device,
        mesh=mesh,
        in_specs=placed,
        out_specs=P(None, "date", None, "strip", None),
        check_vma=False,
    )
```
